128 devices in a mesh: gx: 16 (over z, x), gy: 8 (over y, core).
Axes of the slice: x: 4, y: 4, z: 4, core: 2. Of those that a mesh axis runs over, the one named last changes fastest.
Arguments:
- right_side: float32 [1024, 512, 128], P('gx', 'gy'), may hold values from -150 to 150
- diagonal: float32 [1024, 512, 128], P('gx', 'gy'), may hold values from 0.25 to 2
- sweep_counts: int32 [128], replicated, may hold values from 2 to 12, as said below
- refine_flags: int32 [128, 128], replicated, may hold values 0 or 1
- coarse_inverse: float32 [128, 128], P(('gx', 'gy')), as said below
Outputs:
- solution_field: float32 [1024, 512, 128], P('gx', 'gy')
- residual: float32 [1024, 512, 128], P('gx', 'gy')
The draws below stay inside these ranges and needn't reach their ends.
Inputs may be any that keep to these rules, and one draw needn't show every extreme that they name: `sweep_counts`: every subdomain makes 2 or more sweeps, and some subdomain makes exactly 12. `coarse_inverse`: symmetric positive definite.
All inputs are finite; a program needn't handle non-finite values.
Results may differ from the reference program's by a relative error of at most 0.019.
Values sent between devices are 32-bit elements; how exact they have to be, the bound alone decides.
A program may use at most 128 MiB of HBM per device.

```python
import jax
import jax.numpy as jnp
from jax import lax

CX = 64
CY = 64
CZ = 128
MOST = 12
ITERS = 4
SUBS = 128
NX = 1024
NY = 512
N_GX = 16
N_GY = 8


def draw_right_side(key, part):
    key = jax.random.fold_in(key, 11)
    place_x = jnp.arange(NX, dtype=jnp.float32) / NX
    place_y = jnp.arange(NY, dtype=jnp.float32) / NY
    ramp = (3.0 ** place_x)[:, None, None] * (3.0 ** place_y)[None, :, None]
    values = jnp.clip(jax.random.normal(key, (NX, NY, CZ), jnp.float32), -5.0, 5.0) * ramp
    return values


def draw_sweep_counts(key, part):
    key = jax.random.fold_in(key, 23)
    first, second, third = jax.random.split(key, 3)
    base = jax.random.randint(first, (SUBS,), 2, 5)
    heavy = jax.random.randint(second, (SUBS,), 0, 8) == 0
    chosen = jax.random.permutation(third, SUBS)[0]
    heavy = heavy | (jnp.arange(SUBS) == chosen)
    return jnp.where(heavy, MOST, base).astype(jnp.int32)


def draw_coarse_inverse(key, part):
    key = jax.random.fold_in(key, 37)
    first, second = jax.random.split(key)
    raw = jax.random.uniform(first, (SUBS, SUBS), jnp.float32, 0.0, 1.0)
    offdiag = (raw + raw.T) / SUBS
    eye = jnp.eye(SUBS, dtype=jnp.float32)
    offdiag = offdiag * (1.0 - eye)
    middle = jax.random.uniform(second, (SUBS,), jnp.float32, 0.5, 1.5)
    matrix = offdiag + eye * (2.0 + middle)[:, None]
    return matrix * (0.1 / jnp.sqrt(CX * CY * CZ * 1.0))


def with_ends(drawn, own_key, low, high):
    longest = drawn.shape.index(max(drawn.shape))
    spots = []
    for shift in (0, 1):
        where = [jax.random.randint(jax.random.fold_in(own_key, axis), (), 0, length) for axis, length in enumerate(drawn.shape)]
        where[longest] = (where[longest] + shift) % drawn.shape[longest]
        spots.append(tuple(where))
    return drawn.at[spots[0]].set(low).at[spots[1]].set(high)


def steps_of(key, extent, cuts, least, top_value):
    gain, own = 1.0, jax.random.fold_in(key, 6)
    for dim, parts in cuts:
        steps = jnp.exp(jax.random.uniform(jax.random.fold_in(own, dim), (parts,), jnp.float32, least / len(cuts), top_value / len(cuts)))
        gain = gain * jnp.repeat(steps, extent[dim] // parts).reshape([-1 if axis == dim else 1 for axis in range(len(extent))])
    return gain


def setup_inputs(seed: int = 0) -> dict:
    arg_keys = jax.random.split(jax.random.key(seed), 6)
    return {
        "right_side": draw_right_side(jax.random.fold_in(arg_keys[5], 71), 0),
        "diagonal": jnp.clip(0.25 + 1.75 * jax.random.uniform(arg_keys[1], (NX, NY, CZ), jnp.float32) ** steps_of(arg_keys[1], (NX, NY, CZ), ((0, 16), (1, 8)), -0.2, 0.2), 0.25, 2.0),
        "sweep_counts": draw_sweep_counts(jax.random.fold_in(arg_keys[5], 71), 0),
        "refine_flags": with_ends((jax.random.randint(arg_keys[3], (SUBS, CZ), 0, 4) < 1).astype(jnp.int32), jax.random.fold_in(arg_keys[3], 1), 0, 1),
        "coarse_inverse": draw_coarse_inverse(jax.random.fold_in(arg_keys[5], 71), 0),
    }


HIGH = lax.Precision.HIGHEST

def sine_table(count):
    index = jnp.arange(count, dtype=jnp.float32)
    angle = jnp.pi * (index[:, None] + 1.0) * (index[None, :] + 1.0) / (count + 1.0)
    return jnp.sqrt(2.0 / (count + 1.0)) * jnp.sin(angle)

def eigen_values(count):
    index = jnp.arange(count, dtype=jnp.float32)
    return 2.0 - 2.0 * jnp.cos(jnp.pi * (index + 1.0) / (count + 1.0))

def sweep(rhs, guess, scale):
    zero = jnp.zeros_like(guess[..., :1])
    below = jnp.concatenate([zero, guess[..., :-1]], -1)
    above = jnp.concatenate([guess[..., 1:], zero], -1)
    return (rhs + below + above) / scale

def operate(field, diagonal):
    padded = jnp.pad(field, 1)
    beside = padded[2:, 1:-1, 1:-1] + padded[:-2, 1:-1, 1:-1]
    beside = beside + padded[1:-1, 2:, 1:-1] + padded[1:-1, :-2, 1:-1]
    beside = beside + padded[1:-1, 1:-1, 2:] + padded[1:-1, 1:-1, :-2]
    return (6.0 + diagonal) * field - beside

def precondition(resid, sweep_counts, refine_flags, coarse_inverse):
    table_x = sine_table(CX)
    table_y = sine_table(CY)
    blocks = resid.reshape(N_GX, CX, N_GY, CY, CZ)
    hat = jnp.einsum('ai,piqjz->paqjz', table_x, blocks, precision=HIGH)
    hat = jnp.einsum('bj,paqjz->paqbz', table_y, hat, precision=HIGH)
    modal = eigen_values(CX)[:, None] + eigen_values(CY)[None, :]
    shifts = (0.5 + 2.5 * refine_flags.astype(jnp.float32)).reshape(N_GX, 1, N_GY, 1, CZ)
    scale = modal[None, :, None, :, None] + 2.0
    scale = scale + shifts
    counts = sweep_counts.reshape(N_GX, 1, N_GY, 1, 1)
    lines = jnp.zeros_like(hat)
    for step in range(MOST):
        fresh = sweep(hat, lines, scale)
        lines = jnp.where(step < counts, fresh, lines)
    back = jnp.einsum('ai,piqjz->paqjz', table_x, lines, precision=HIGH)
    back = jnp.einsum('bj,paqjz->paqbz', table_y, back, precision=HIGH)
    sums = lax.optimization_barrier(jnp.sum(blocks, axis=(1, 3, 4))).reshape(N_GX * N_GY)
    coarse = jnp.dot(coarse_inverse, sums, precision=HIGH)
    result = back + coarse.reshape(N_GX, 1, N_GY, 1, 1)
    return result.reshape(CX * N_GX, CY * N_GY, CZ)

def reference(right_side, diagonal, sweep_counts, refine_flags, coarse_inverse):
    solution_field = jnp.zeros_like(right_side)
    residual = right_side
    precond = precondition(residual, sweep_counts, refine_flags, coarse_inverse)
    direction = precond
    gamma = jnp.sum(residual * precond)
    for step in range(ITERS):
        image = operate(direction, diagonal)
        alpha = gamma / jnp.sum(direction * image)
        solution_field = solution_field + alpha * direction
        residual = residual - alpha * image
        if step + 1 < ITERS:
            precond = precondition(residual, sweep_counts, refine_flags, coarse_inverse)
            fresh = jnp.sum(residual * precond)
            direction = precond + fresh / gamma * direction
            gamma = fresh
    return (solution_field, residual)
```

```python
import functools

import jax
import jax.numpy as jnp
import ml_dtypes
import numpy as np
from jax import lax
from jax.experimental import pallas as pl
from jax.experimental.pallas import tpu as pltpu
from jax.sharding import PartitionSpec as P

ITERS = 4
MOST = 12
LANES = 128
ROWS = 8
GATHERS = ITERS + 1
LINES = 4
PLANES = 8
F32 = jnp.float32
MESH = pl.DeviceIdType.MESH


def sine_table(count):
    index = np.arange(count, dtype=np.float64)
    angle = np.pi * (index[:, None] + 1.0) * (index[None, :] + 1.0) / (count + 1.0)
    return np.sqrt(2.0 / (count + 1.0)) * np.sin(angle)


def eigen_values(count):
    index = np.arange(count, dtype=np.float64)
    return 2.0 - 2.0 * np.cos(np.pi * (index + 1.0) / (count + 1.0))


def split_table(count):
    table = sine_table(count).astype(np.float32)
    high = table.astype(ml_dtypes.bfloat16)
    low = (table - high.astype(np.float32)).astype(ml_dtypes.bfloat16)
    return np.concatenate([np.concatenate([high, high], axis=1), np.concatenate([low, low], axis=1)], axis=0)


def transform(table, field):
    high = field.astype(jnp.bfloat16)
    low = (field - high.astype(F32)).astype(jnp.bfloat16)
    stacked = jnp.concatenate([high, low], axis=0)
    both = jnp.dot(table, stacked, preferred_element_type=F32)
    return both[:field.shape[0]] + both[field.shape[0]:]


def fold(value):
    return jnp.sum(value.reshape(-1, ROWS, LANES), axis=0)


def kernel(
    n_gx, n_gy, size,
    rhs_hbm, diag_hbm, count_hbm, flag_hbm, coarse_hbm, table_hbm, mu_hbm,
    x_ref, r_ref,
    count_ref, flag_ref, coarse_ref, table_ref, mu_ref,
    diag_ref, p_ref, s_ref, image_ref, back_ref, hat_ref, line_ref, step_ref, mode_ref, twice_ref,
    root_ref, near_ref, far_ref, mid_ref,
    edge_ref, ghost_x, ghost_y, fix_ref, small_ref, all_ref, coarse_pad,
    in_sem, halo_send, halo_recv, row_send, row_recv, col_send, col_recv,
):
    gx = lax.axis_index("gx")
    gy = lax.axis_index("gy")
    mine = gx * n_gy + gy
    pitch = size + ROWS
    odd_pitch = size + 1
    row8 = lax.broadcasted_iota(jnp.int32, (ROWS, LANES), 0)
    lane8 = lax.broadcasted_iota(jnp.int32, (ROWS, LANES), 1)

    def plane(index):
        return pl.ds(pl.multiple_of(index * size, ROWS), size)

    def padded(index):
        return pl.ds(pl.multiple_of((index + 1) * pitch, ROWS), size)

    pairs = (
        (flag_hbm, flag_ref), (mu_hbm, mu_ref), (coarse_hbm, coarse_ref), (count_hbm, count_ref),
        (table_hbm, table_ref), (rhs_hbm, r_ref), (diag_hbm, diag_ref),
    )
    loads = [pltpu.make_async_copy(source, target, in_sem.at[n]) for n, (source, target) in enumerate(pairs)]
    for load in loads:
        load.start()
    if n_gx * ROWS < LANES:
        all_ref[...] = jnp.zeros_like(all_ref)

    barrier = pltpu.get_barrier_semaphore()

    def greet_row(step, carry):
        pl.semaphore_signal(barrier, inc=1, device_id=(gx, lax.rem(gy + step, n_gy)), device_id_type=MESH)
        return carry

    def greet_col(step, carry):
        pl.semaphore_signal(barrier, inc=1, device_id=(lax.rem(gx + step, n_gx), gy), device_id_type=MESH)
        return carry

    lax.fori_loop(1, n_gy, greet_row, 0)
    lax.fori_loop(1, n_gx, greet_col, 0)

    loads[0].wait()
    loads[1].wait()
    shift = 2.5 * flag_ref[pl.ds(mine, 1), :].astype(F32) + 2.5
    lane = lax.broadcasted_iota(jnp.int32, (size, LANES), 1)

    def coefficients(b):
        d = mu_ref[...] + mu_ref[pl.ds(b, 1), :] + shift
        root = lax.rsqrt(d)
        root = root * (1.5 - 0.5 * d * root * root)
        near = jnp.where(lane == 0, 0.0, root * pltpu.roll(root, 1, 1))
        square = near * near
        root_ref[plane(b), :] = root
        near_ref[plane(b), :] = near
        far_ref[plane(b), :] = near * pltpu.roll(near, 1, 1)
        mid_ref[plane(b), :] = square + pltpu.roll(square, LANES - 1, 1)

    def coefficient_pair(t, carry):
        coefficients(2 * t)
        coefficients(2 * t + 1)
        return carry

    lax.fori_loop(0, size // 2, coefficient_pair, 0)

    back_ref[pl.ds(0, pitch), :] = jnp.zeros((pitch, LANES), F32)
    back_ref[pl.ds((size + 1) * pitch, pitch), :] = jnp.zeros((pitch, LANES), F32)

    def clear(index, carry):
        start = pl.multiple_of((index + 1) * pitch + size, ROWS)
        back_ref[pl.ds(start, ROWS), :] = jnp.zeros((ROWS, LANES), F32)
        return carry

    lax.fori_loop(0, size, clear, 0)
    coarse_pad[pl.ds(0, ROWS), :] = jnp.zeros((ROWS, LANES), F32)
    coarse_pad[pl.ds(ROWS + LANES, ROWS), :] = jnp.zeros((ROWS, LANES), F32)

    pl.semaphore_wait(barrier, n_gx + n_gy - 2)

    def row_copy(slot, step):
        return pltpu.make_async_remote_copy(
            src_ref=small_ref.at[slot, gy], dst_ref=small_ref.at[slot, gy],
            send_sem=row_send.at[slot, step], recv_sem=row_recv.at[slot, step],
            device_id=(gx, lax.rem(gy + step, n_gy)), device_id_type=MESH,
        )

    def col_copy(slot, step):
        return pltpu.make_async_remote_copy(
            src_ref=all_ref.at[slot, gx], dst_ref=all_ref.at[slot, gx],
            send_sem=col_send.at[slot, step], recv_sem=col_recv.at[slot, step],
            device_id=(lax.rem(gx + step, n_gx), gy), device_id_type=MESH,
        )

    def over(first, last, act):
        def body(step, carry):
            act(step)
            return carry

        lax.fori_loop(first, last, body, 0)

    def gather_start(slot, payload):
        small_ref[slot, gy] = jnp.where(row8 == gy, payload, 0.0)
        over(1, n_gy, lambda step: row_copy(slot, step).start())

    def gather_middle(slot):
        over(1, n_gy, lambda step: row_copy(slot, step).wait())
        total = small_ref[slot, 0]
        for other in range(1, n_gy):
            total = total + small_ref[slot, other]
        all_ref[slot, gx] = total
        over(1, n_gx, lambda step: col_copy(slot, step).start())

    def gather_end(slot):
        over(1, n_gx, lambda step: col_copy(slot, step).wait())
        return all_ref[slot].reshape(LANES, LANES)

    for load in loads[2:5]:
        load.wait()
    gather_start(ITERS, coarse_ref[...])

    count = jnp.full((ROWS, LANES), count_ref[mine], jnp.int32)

    count = jnp.concatenate([count] * (size // ROWS), axis=0)
    odd = count % 2 == 1
    active = [count > 2 * step for step in range(MOST // 2)]

    def rows(base, index):
        return pl.ds(base + index * size, size)

    def transform_all(parts):
        table = table_ref[...]
        done = []
        for n in range(0, len(parts), 2):
            both = transform(table, jnp.concatenate(parts[n:n + 2], axis=1))
            done += [both[:, :LANES], both[:, LANES:]]
        return done

    def forward(first, parts):
        for n, part in enumerate(transform_all(parts)):
            step_ref[pl.ds((first + n) * odd_pitch, size), :] = part

    def group(t):
        return pl.multiple_of(t * (LINES * size), ROWS)

    def lines_in(t, base, shift):
        first = (t + shift) * LINES
        parts = [step_ref[pl.ds(first + m, size, stride=odd_pitch), :] for m in range(LINES)]
        for m, part in enumerate(transform_all(parts)):
            hat_ref[rows(base, m + shift * LINES), :] = part

    def lines_sweep(base, shift):
        here = [rows(base, m + shift * LINES) for m in range(LINES)]
        guess = []
        for m in range(LINES):
            near = near_ref[here[m], :]
            start = hat_ref[here[m], :] * root_ref[here[m], :]
            twice = start + near * pltpu.roll(start, 1, 1) + pltpu.roll(near * start, LANES - 1, 1)
            twice_ref[pl.ds(m * size, size), :] = twice
            guess.append(jnp.where(odd, start, twice))
        for step in range(1, MOST // 2):
            for m in range(LINES):
                far = far_ref[here[m], :]
                fresh = (twice_ref[pl.ds(m * size, size), :] + mid_ref[here[m], :] * guess[m]) + (
                    far * pltpu.roll(guess[m], 2, 1) + pltpu.roll(far * guess[m], LANES - 2, 1)
                )
                guess[m] = jnp.where(active[step], fresh, guess[m])
        for m in range(LINES):
            line_ref[here[m], :] = guess[m] * root_ref[here[m], :]

    def lines_out(base, shift, first):
        parts = [line_ref[rows(base, m + shift * LINES), :] for m in range(LINES)]
        for m, part in enumerate(transform_all(parts)):
            mode_ref[pl.ds((first + m) * odd_pitch, size), :] = part

    def solve_lines():
        groups = size // LINES

        def body(t, carry):
            base = group(t)
            lines_out(base, -2, (t - 2) * LINES)
            lines_sweep(base, -1)
            lines_in(t, base, 0)
            return carry

        lines_in(0, 0, 0)
        lines_sweep(0, 0)
        lines_in(1, group(1), 0)
        lax.fori_loop(2, groups, body, 0)
        last = group(groups)
        lines_out(last, -2, size - 2 * LINES)
        lines_sweep(last, -1)
        lines_out(last, -1, size - LINES)

    def backward(first):
        parts = [mode_ref[pl.ds(first + m, size, stride=odd_pitch), :] for m in range(PLANES)]
        base = pl.multiple_of((first + 1) * pitch, ROWS)
        for m, part in enumerate(transform_all(parts)):
            back_ref[pl.ds(base + m * pitch, size), :] = part
            edge_ref[0, pl.ds(first + m, 1), :] = part[:1]
            edge_ref[1, pl.ds(first + m, 1), :] = part[size - 1:]

    def halo_copy(turn, side):
        if side < 2:
            step = 1 if side == 0 else n_gx - 1
            index = size - 1 if side == 0 else 0
            source = back_ref.at[pl.ds((index + 1) * pitch, size)]
            target = ghost_x.at[turn, side]
            device = (lax.rem(gx + step, n_gx), gy)
        else:
            step = 1 if side == 2 else n_gy - 1
            source = edge_ref.at[1 if side == 2 else 0]
            target = ghost_y.at[turn, side - 2]
            device = (gx, lax.rem(gy + step, n_gy))
        return pltpu.make_async_remote_copy(
            src_ref=source, dst_ref=target,
            send_sem=halo_send.at[turn, side], recv_sem=halo_recv.at[turn, side],
            device_id=device, device_id_type=MESH,
        )

    inside = [gx > 0, gx < n_gx - 1, gy > 0, gy < n_gy - 1]

    def ghosts(turn):
        raw = [ghost_x[turn, 0], ghost_x[turn, 1], ghost_y[turn, 0], ghost_y[turn, 1]]
        return [jnp.where(inside[n], raw[n], 0.0) for n in range(4)]

    def apply(turn, i, sums):
        here = back_ref[padded(i), :]
        start = (i + 1) * pitch
        beside = back_ref[padded(i - 1), :] + back_ref[padded(i + 1), :]
        beside = beside + back_ref[pl.ds(start - 1, size), :] + back_ref[pl.ds(start + 1, size), :]
        below = jnp.where(lane == 0, 0.0, pltpu.roll(here, 1, 1))
        above = jnp.where(lane == LANES - 1, 0.0, pltpu.roll(here, LANES - 1, 1))
        diag = diag_ref[plane(i), :]
        image = (6.0 + diag) * here - (beside + (below + above))
        image_ref[plane(i), :] = image
        resid = r_ref[plane(i), :]
        terms = [resid, resid * here, here * image, image]
        if turn:
            old = s_ref[plane(i), :]
            terms += [here * old, old]
        else:
            terms += [diag]
        return tuple(total + fold(term) for total, term in zip(sums, terms))

    big_row = lax.broadcasted_iota(jnp.int32, (LANES, LANES), 0)
    big_lane = lax.broadcasted_iota(jnp.int32, (LANES, LANES), 1)

    loads[5].wait()
    loads[6].wait()

    def first_forward(t, carry):
        base = pl.multiple_of(t * (PLANES * size), ROWS)
        forward(t * PLANES, [r_ref[rows(base, m), :] for m in range(PLANES)])
        return carry

    lax.fori_loop(0, size // PLANES, first_forward, 0)
    gather_middle(ITERS)

    diag_total = None
    gamma = None
    energy = None
    for turn in range(ITERS):
        solve_lines()

        def ends(t, carry):
            backward(t * (size - PLANES))
            return carry

        def others(t, carry):
            backward(PLANES * t)
            return carry

        lax.fori_loop(0, 2, ends, 0)
        halos = [halo_copy(turn, side) for side in range(4)]
        halos[0].start()
        halos[1].start()
        lax.fori_loop(1, size // PLANES - 1, others, 0)
        halos[2].start()
        halos[3].start()

        zeros = tuple(jnp.zeros((ROWS, LANES), F32) for _ in range(6 if turn else 5))

        def apply_some(t, sums):
            for m in range(4):
                sums = apply(turn, 4 * t + m, sums)
            return sums

        sums = list(lax.fori_loop(0, size // 4, apply_some, zeros))
        for halo in halos:
            halo.wait()
        ghost = ghosts(turn)
        faces = [back_ref[padded(0), :], back_ref[padded(size - 1), :], edge_ref[0], edge_ref[1]]
        for n in range(4):
            sums[2] = sums[2] - fold(faces[n] * ghost[n])
            sums[3] = sums[3] - fold(ghost[n])
        if turn == 0:
            diag_total = sums[4]
            sums = sums[:4] + [jnp.zeros((ROWS, LANES), F32)] * 2
        sums.append(diag_total)
        stacked = jnp.zeros((ROWS, LANES), F32)
        for n, total in enumerate(sums):
            stacked = jnp.where(row8 == n, jnp.sum(total, axis=0, keepdims=True), stacked)
        stacked = jnp.sum(stacked, axis=1, keepdims=True)
        payload = jnp.sum(jnp.where(row8 == lane8, stacked, 0.0), axis=0, keepdims=True)
        gather_start(turn, payload)
        gather_middle(turn)
        if turn == 0:
            gather_end(ITERS)
        every = gather_end(turn)

        matrix = all_ref[ITERS].reshape(LANES, LANES)
        coarse = jnp.dot(matrix, every, precision=lax.Precision.HIGHEST, preferred_element_type=F32)
        coarse = jnp.broadcast_to(coarse[:, :1], (LANES, LANES))
        coarse_pad[pl.ds(ROWS, LANES), :] = coarse
        beside = coarse_pad[pl.ds(0, LANES), :] + coarse_pad[pl.ds(2 * ROWS, LANES), :]
        beside = beside + jnp.where(big_row % ROWS == 0, 0.0, coarse_pad[pl.ds(ROWS - 1, LANES), :])
        beside = beside + jnp.where(big_row % ROWS == n_gy - 1, 0.0, coarse_pad[pl.ds(ROWS + 1, LANES), :])
        ends_total = 2.0 * size * size
        weight = jnp.where((big_lane == 0) | (big_lane == 5), coarse, 1.0)
        weight = jnp.where(big_lane == 3, 2.0 * coarse, weight)
        weight = jnp.where(big_lane == 6, coarse * coarse, weight)
        terms = every * weight
        flux = coarse * (ends_total * coarse + size * LANES * (4.0 * coarse - beside))
        terms = terms + jnp.where(big_lane == 6, flux, 0.0)
        terms = jnp.sum(terms, axis=0, keepdims=True)
        slim = lax.broadcasted_iota(jnp.int32, (1, LANES), 1)

        def pick(*lanes):
            mask = slim == lanes[0]
            for which in lanes[1:]:
                mask = mask | (slim == which)
            total = jnp.sum(jnp.where(mask, terms, 0.0), axis=1, keepdims=True)
            return jnp.broadcast_to(total, (ROWS, LANES))

        fresh = pick(0, 1)
        curve = pick(2, 3, 6)
        if turn:
            beta = fresh / gamma
            energy = curve + beta * (2.0 * pick(4, 5) + beta * energy)
        else:
            beta = None
            energy = curve
        gamma = fresh
        alpha = gamma / energy

        own = coarse_pad[pl.ds(ROWS + mine, 1), :]
        across = [
            coarse_pad[pl.ds(mine, 1), :],
            coarse_pad[pl.ds(2 * ROWS + mine, 1), :],
            jnp.where(inside[2], coarse_pad[pl.ds(ROWS - 1 + mine, 1), :], 0.0),
            jnp.where(inside[3], coarse_pad[pl.ds(ROWS + 1 + mine, 1), :], 0.0),
        ]
        fixes = [(own - across[n]) - ghost[n] for n in range(4)]
        image_ref[plane(0), :] = image_ref[plane(0), :] + fixes[0]
        image_ref[plane(size - 1), :] = image_ref[plane(size - 1), :] + fixes[1]
        fix_ref[0] = fixes[2]
        fix_ref[1] = fixes[3]

        def span(value):
            return jnp.broadcast_to(value[:1], (size, LANES))

        own_wide = jnp.broadcast_to(own, (size, LANES))
        ends_wide = jnp.where((lane == 0) | (lane == LANES - 1), 1.0, 0.0)
        alpha_wide = span(alpha)
        beta_wide = span(beta) if turn else None

        def update(base, first, m):
            here = rows(base, m)
            low = jnp.where(row8 == 0, fix_ref[0, pl.ds(first + m, 1), :], 0.0)
            high = jnp.where(row8 == ROWS - 1, fix_ref[1, pl.ds(first + m, 1), :], 0.0)
            image = image_ref[here, :]
            image = jnp.concatenate(
                [image[:ROWS] + low, image[ROWS:size - ROWS], image[size - ROWS:] + high], axis=0
            )
            image = image + own_wide * (diag_ref[here, :] + ends_wide)
            direction = back_ref[padded(first + m), :] + own_wide
            if turn:
                image = image + beta_wide * s_ref[here, :]
                direction = direction + beta_wide * p_ref[here, :]
                field = x_ref[here, :] + alpha_wide * direction
            else:
                field = alpha_wide * direction
            resid = r_ref[here, :] - alpha_wide * image
            if turn < ITERS - 1:
                s_ref[here, :] = image
                p_ref[here, :] = direction
            x_ref[here, :] = field
            r_ref[here, :] = resid
            return resid

        def update_some(t, carry):
            base = pl.multiple_of(t * (PLANES * size), ROWS)
            parts = [update(base, t * PLANES, m) for m in range(PLANES)]
            if turn < ITERS - 1:
                forward(t * PLANES, parts)
            return carry

        lax.fori_loop(0, size // PLANES, update_some, 0)


def shards(n_gx, n_gy, right_side, diagonal, sweep_counts, refine_flags, coarse_inverse):
    size, _, cells = right_side.shape
    flat = (size * size, cells)
    table = jnp.asarray(split_table(size))
    mu = jnp.asarray(np.repeat(eigen_values(size).astype(np.float32)[:, None], cells, axis=1))
    subs = n_gx * n_gy
    if coarse_inverse.shape[1] < LANES:
        coarse_inverse = jnp.pad(coarse_inverse, ((0, 0), (0, LANES - subs)))
    operands = (
        right_side.reshape(flat), diagonal.reshape(flat), sweep_counts, refine_flags, coarse_inverse, table, mu
    )
    vmem = pl.BlockSpec(memory_space=pltpu.VMEM)
    hbm = pl.BlockSpec(memory_space=pltpu.HBM)
    field = pltpu.VMEM(flat, F32)
    face = (size, LANES)
    outs = pl.pallas_call(
        functools.partial(kernel, n_gx, n_gy, size),
        out_shape=[jax.ShapeDtypeStruct(flat, F32)] * 2,
        in_specs=[hbm] * 7,
        out_specs=[vmem, vmem],
        scratch_shapes=[
            pltpu.SMEM(sweep_counts.shape, jnp.int32),
            pltpu.VMEM(refine_flags.shape, jnp.int32),
            pltpu.VMEM(coarse_inverse.shape, F32),
            pltpu.VMEM(table.shape, table.dtype),
            pltpu.VMEM(mu.shape, F32),
            field, field, field, field,
            pltpu.VMEM(((size + 2) * (size + ROWS), LANES), F32),
            field, field,
            pltpu.VMEM((size * (size + 1), LANES), F32),
            pltpu.VMEM((size * (size + 1), LANES), F32),
            pltpu.VMEM((LINES * size, LANES), F32),
            field, field, field, field,
            pltpu.VMEM((2,) + face, F32),
            pltpu.VMEM((ITERS, 2) + face, F32),
            pltpu.VMEM((ITERS, 2) + face, F32),
            pltpu.VMEM((2,) + face, F32),
            pltpu.VMEM((GATHERS, n_gy, ROWS, LANES), F32),
            pltpu.VMEM((GATHERS, LANES // ROWS, ROWS, LANES), F32),
            pltpu.VMEM((LANES + 2 * ROWS, LANES), F32),
            pltpu.SemaphoreType.DMA((7,)),
            pltpu.SemaphoreType.DMA((ITERS, 4)),
            pltpu.SemaphoreType.DMA((ITERS, 4)),
            pltpu.SemaphoreType.DMA((GATHERS, n_gy)),
            pltpu.SemaphoreType.DMA((GATHERS, n_gy)),
            pltpu.SemaphoreType.DMA((GATHERS, n_gx)),
            pltpu.SemaphoreType.DMA((GATHERS, n_gx)),
        ],
        compiler_params=pltpu.CompilerParams(
            collective_id=0, has_side_effects=True, vmem_limit_bytes=48 * 1024 * 1024
        ),
        cost_estimate=pl.CostEstimate(flops=4 * 10**9, bytes_accessed=8 * 2**20, transcendentals=0),
        name="pressure_solve",
    )(
        *(pltpu.with_memory_space_constraint(operand, pltpu.HBM) for operand in operands)
    )
    return tuple(out.reshape(right_side.shape) for out in outs)


def solution(mesh):
    return jax.shard_map(
        functools.partial(shards, mesh.shape["gx"], mesh.shape["gy"]),
        mesh=mesh,
        in_specs=(P("gx", "gy", None), P("gx", "gy", None), P(), P(), P(("gx", "gy"), None)),
        out_specs=(P("gx", "gy", None), P("gx", "gy", None)),
        check_vma=False,
    )
```

```python
import functools

import jax
import jax.numpy as jnp
import ml_dtypes
import numpy as np
from jax import lax
from jax.experimental import pallas as pl
from jax.experimental.pallas import tpu as pltpu
from jax.sharding import PartitionSpec as P

ITERS = 4
MOST = 12
LANES = 128
ROWS = 8
GATHERS = ITERS + 1
LINES = 4
GROUPS = 2
PLANES = 16
APPLIES = 8
F32 = jnp.float32
MESH = pl.DeviceIdType.MESH


def sine_table(count):
    index = np.arange(count, dtype=np.float64)
    angle = np.pi * (index[:, None] + 1.0) * (index[None, :] + 1.0) / (count + 1.0)
    return np.sqrt(2.0 / (count + 1.0)) * np.sin(angle)


def eigen_values(count):
    index = np.arange(count, dtype=np.float64)
    return 2.0 - 2.0 * np.cos(np.pi * (index + 1.0) / (count + 1.0))


def split_table(count):
    table = sine_table(count).astype(np.float32)
    high = table.astype(ml_dtypes.bfloat16)
    low = (table - high.astype(np.float32)).astype(ml_dtypes.bfloat16)
    return np.concatenate([np.concatenate([high, high], axis=1), np.concatenate([low, low], axis=1)], axis=0)


def transform(table, field):
    high = field.astype(jnp.bfloat16)
    low = (field - high.astype(F32)).astype(jnp.bfloat16)
    stacked = jnp.concatenate([high, low], axis=0)
    both = jnp.dot(table, stacked, preferred_element_type=F32)
    return both[:field.shape[0]] + both[field.shape[0]:]


def fold(value):
    return jnp.sum(value.reshape(-1, ROWS, LANES), axis=0)


def kernel(
    n_gx, n_gy, size,
    rhs_hbm, diag_hbm, count_hbm, flag_hbm, coarse_hbm, table_hbm, mu_hbm,
    x_ref, r_ref,
    count_ref, flag_ref, coarse_ref, table_ref, mu_ref,
    diag_ref, p_ref, s_ref, image_ref, back_ref, hat_ref, line_ref, step_ref, mode_ref, twice_ref,
    root_ref, near_ref, far_ref, mid_ref,
    edge_ref, ghost_x, ghost_y, fix_ref, small_ref, all_ref, coarse_pad,
    in_sem, halo_send, halo_recv, row_send, row_recv, col_send, col_recv,
):
    gx = lax.axis_index("gx")
    gy = lax.axis_index("gy")
    mine = gx * n_gy + gy
    pitch = size + ROWS
    odd_pitch = size + 1
    row8 = lax.broadcasted_iota(jnp.int32, (ROWS, LANES), 0)
    lane8 = lax.broadcasted_iota(jnp.int32, (ROWS, LANES), 1)

    def plane(index):
        return pl.ds(pl.multiple_of(index * size, ROWS), size)

    def padded(index):
        return pl.ds(pl.multiple_of((index + 1) * pitch, ROWS), size)

    pairs = (
        (flag_hbm, flag_ref), (mu_hbm, mu_ref), (coarse_hbm, coarse_ref), (count_hbm, count_ref),
        (table_hbm, table_ref), (rhs_hbm, r_ref), (diag_hbm, diag_ref),
    )
    loads = [pltpu.make_async_copy(source, target, in_sem.at[n]) for n, (source, target) in enumerate(pairs)]
    for load in loads:
        load.start()
    if n_gx * ROWS < LANES:
        all_ref[...] = jnp.zeros_like(all_ref)

    barrier = pltpu.get_barrier_semaphore()

    def greet_row(step, carry):
        pl.semaphore_signal(barrier, inc=1, device_id=(gx, lax.rem(gy + step, n_gy)), device_id_type=MESH)
        return carry

    def greet_col(step, carry):
        pl.semaphore_signal(barrier, inc=1, device_id=(lax.rem(gx + step, n_gx), gy), device_id_type=MESH)
        return carry

    lax.fori_loop(1, n_gy, greet_row, 0)
    lax.fori_loop(1, n_gx, greet_col, 0)

    loads[0].wait()
    loads[1].wait()
    shift = 2.5 * flag_ref[pl.ds(mine, 1), :].astype(F32) + 2.5
    lane = lax.broadcasted_iota(jnp.int32, (size, LANES), 1)

    def coefficients(b):
        d = mu_ref[...] + mu_ref[pl.ds(b, 1), :] + shift
        root = lax.rsqrt(d)
        root = root * (1.5 - 0.5 * d * root * root)
        near = jnp.where(lane == 0, 0.0, root * pltpu.roll(root, 1, 1))
        square = near * near
        root_ref[plane(b), :] = root
        near_ref[plane(b), :] = near
        far_ref[plane(b), :] = near * pltpu.roll(near, 1, 1)
        mid_ref[plane(b), :] = square + pltpu.roll(square, LANES - 1, 1)

    def coefficient_pair(t, carry):
        coefficients(2 * t)
        coefficients(2 * t + 1)
        return carry

    lax.fori_loop(0, size // 2, coefficient_pair, 0)

    back_ref[pl.ds(0, pitch), :] = jnp.zeros((pitch, LANES), F32)
    back_ref[pl.ds((size + 1) * pitch, pitch), :] = jnp.zeros((pitch, LANES), F32)

    def clear(index, carry):
        start = pl.multiple_of((index + 1) * pitch + size, ROWS)
        back_ref[pl.ds(start, ROWS), :] = jnp.zeros((ROWS, LANES), F32)
        return carry

    lax.fori_loop(0, size, clear, 0)
    coarse_pad[pl.ds(0, ROWS), :] = jnp.zeros((ROWS, LANES), F32)
    coarse_pad[pl.ds(ROWS + LANES, ROWS), :] = jnp.zeros((ROWS, LANES), F32)

    def wipe(t, carry):
        here = pl.ds(pl.multiple_of(t * (4 * size), ROWS), 4 * size)
        for field in (p_ref, s_ref, x_ref):
            field[here, :] = jnp.zeros((4 * size, LANES), F32)
        return carry

    lax.fori_loop(0, size // 4, wipe, 0)
    pl.semaphore_wait(barrier, n_gx + n_gy - 2)

    def row_copy(slot, step):
        return pltpu.make_async_remote_copy(
            src_ref=small_ref.at[slot, gy], dst_ref=small_ref.at[slot, gy],
            send_sem=row_send.at[slot, step], recv_sem=row_recv.at[slot, step],
            device_id=(gx, lax.rem(gy + step, n_gy)), device_id_type=MESH,
        )

    def col_copy(slot, step):
        return pltpu.make_async_remote_copy(
            src_ref=all_ref.at[slot, gx], dst_ref=all_ref.at[slot, gx],
            send_sem=col_send.at[slot, step], recv_sem=col_recv.at[slot, step],
            device_id=(lax.rem(gx + step, n_gx), gy), device_id_type=MESH,
        )

    def over(first, last, act):
        def body(step, carry):
            act(step)
            return carry

        lax.fori_loop(first, last, body, 0)

    def gather_start(slot, payload):
        small_ref[slot, gy] = jnp.where(row8 == gy, payload, 0.0)
        over(1, n_gy, lambda step: row_copy(slot, step).start())

    def gather_middle(slot):
        over(1, n_gy, lambda step: row_copy(slot, step).wait_recv())
        total = small_ref[slot, 0]
        for other in range(1, n_gy):
            total = total + small_ref[slot, other]
        all_ref[slot, gx] = total
        over(1, n_gx, lambda step: col_copy(slot, step).start())

    def gather_end(slot):
        over(1, n_gx, lambda step: col_copy(slot, step).wait_recv())
        return all_ref[slot].reshape(LANES, LANES)

    def gather_drain(slot):
        over(1, n_gy, lambda step: row_copy(slot, step).wait_send())
        over(1, n_gx, lambda step: col_copy(slot, step).wait_send())

    for load in loads[2:5]:
        load.wait()
    gather_start(ITERS, coarse_ref[...])

    count = jnp.full((ROWS, LANES), count_ref[mine], jnp.int32)

    count = jnp.concatenate([count] * (size // ROWS), axis=0)
    odd = count % 2 == 1
    active = [count > 2 * step for step in range(MOST // 2)]

    def rows(base, index):
        return pl.ds(base + index * size, size)

    def transform_all(parts):
        table = table_ref[...]
        done = []
        for n in range(0, len(parts), 2):
            both = transform(table, jnp.concatenate(parts[n:n + 2], axis=1))
            done += [both[:, :LANES], both[:, LANES:]]
        return done

    def forward(first, parts):
        for n, part in enumerate(transform_all(parts)):
            step_ref[pl.ds((first + n) * odd_pitch, size), :] = part

    def lines_in(first, base, shift):
        parts = [step_ref[pl.ds(first + m, size, stride=odd_pitch), :] for m in range(GROUPS * LINES)]
        for m, part in enumerate(transform_all(parts)):
            hat_ref[rows(base, m + shift), :] = part

    def lines_sweep(base, shift):
        for part in range(GROUPS):
            here = [rows(base, m + part * LINES + shift) for m in range(LINES)]
            kept = [pl.ds((part * LINES + m) * size, size) for m in range(LINES)]
            guess = []
            for m in range(LINES):
                near = near_ref[here[m], :]
                start = hat_ref[here[m], :] * root_ref[here[m], :]
                twice = start + near * pltpu.roll(start, 1, 1) + pltpu.roll(near * start, LANES - 1, 1)
                twice_ref[kept[m], :] = twice
                guess.append(jnp.where(odd, start, twice))
            for step in range(1, MOST // 2):
                for m in range(LINES):
                    far = far_ref[here[m], :]
                    fresh = (twice_ref[kept[m], :] + mid_ref[here[m], :] * guess[m]) + (
                        far * pltpu.roll(guess[m], 2, 1) + pltpu.roll(far * guess[m], LANES - 2, 1)
                    )
                    guess[m] = jnp.where(active[step], fresh, guess[m])
            for m in range(LINES):
                line_ref[here[m], :] = guess[m] * root_ref[here[m], :]

    def lines_out(first, base, shift):
        parts = [line_ref[rows(base, m + shift), :] for m in range(GROUPS * LINES)]
        for m, part in enumerate(transform_all(parts)):
            mode_ref[pl.ds((first + m) * odd_pitch, size), :] = part

    def solve_lines():
        many = GROUPS * LINES

        def body(t, carry):
            base = pl.multiple_of(t * (many * size), ROWS)
            lines_out((t - 2) * many, base, -2 * many)
            lines_sweep(base, -many)
            lines_in(t * many, base, 0)
            return carry

        lines_in(0, 0, 0)
        lines_sweep(0, 0)
        lines_in(many, many * size, 0)
        lax.fori_loop(2, size // many, body, 0)
        lines_out(size - 2 * many, size * size, -2 * many)
        lines_sweep(size * size, -many)
        lines_out(size - many, size * size, -many)

    def backward(first):
        parts = [mode_ref[pl.ds(first + m, size, stride=odd_pitch), :] for m in range(PLANES)]
        base = pl.multiple_of((first + 1) * pitch, ROWS)
        for m, part in enumerate(transform_all(parts)):
            back_ref[pl.ds(base + m * pitch, size), :] = part
            edge_ref[0, pl.ds(first + m, 1), :] = part[:1]
            edge_ref[1, pl.ds(first + m, 1), :] = part[size - 1:]

    def halo_copy(turn, side):
        if side < 2:
            step = 1 if side == 0 else n_gx - 1
            index = size - 1 if side == 0 else 0
            source = back_ref.at[pl.ds((index + 1) * pitch, size)]
            target = ghost_x.at[turn, side]
            device = (lax.rem(gx + step, n_gx), gy)
        else:
            step = 1 if side == 2 else n_gy - 1
            source = edge_ref.at[1 if side == 2 else 0]
            target = ghost_y.at[turn, side - 2]
            device = (gx, lax.rem(gy + step, n_gy))
        return pltpu.make_async_remote_copy(
            src_ref=source, dst_ref=target,
            send_sem=halo_send.at[turn, side], recv_sem=halo_recv.at[turn, side],
            device_id=device, device_id_type=MESH,
        )

    inside = [gx > 0, gx < n_gx - 1, gy > 0, gy < n_gy - 1]

    def ghosts(turn):
        raw = [ghost_x[turn, 0], ghost_x[turn, 1], ghost_y[turn, 0], ghost_y[turn, 1]]
        return [jnp.where(inside[n], raw[n], 0.0) for n in range(4)]

    def apply(i, sums):
        here = back_ref[padded(i), :]
        start = (i + 1) * pitch
        beside = back_ref[padded(i - 1), :] + back_ref[padded(i + 1), :]
        beside = beside + back_ref[pl.ds(start - 1, size), :] + back_ref[pl.ds(start + 1, size), :]
        below = jnp.where(lane == 0, 0.0, pltpu.roll(here, 1, 1))
        above = jnp.where(lane == LANES - 1, 0.0, pltpu.roll(here, LANES - 1, 1))
        diag = diag_ref[plane(i), :]
        image = (6.0 + diag) * here - (beside + (below + above))
        image_ref[plane(i), :] = image
        resid = r_ref[plane(i), :]
        old = s_ref[plane(i), :]
        terms = [resid, resid * here, here * image, image, here * old, old]
        return tuple(total + fold(term) for total, term in zip(sums, terms))

    big_row = lax.broadcasted_iota(jnp.int32, (LANES, LANES), 0)
    big_lane = lax.broadcasted_iota(jnp.int32, (LANES, LANES), 1)

    loads[5].wait()
    loads[6].wait()

    def first_forward(t, total):
        base = pl.multiple_of(t * (PLANES * size), ROWS)
        forward(t * PLANES, [r_ref[rows(base, m), :] for m in range(PLANES)])
        for m in range(PLANES):
            total = total + fold(diag_ref[rows(base, m), :])
        return total

    diag_total = lax.fori_loop(0, size // PLANES, first_forward, jnp.zeros((ROWS, LANES), F32))
    gather_middle(ITERS)
    slim = lax.broadcasted_iota(jnp.int32, (1, LANES), 1)
    ends_wide = jnp.where((lane == 0) | (lane == LANES - 1), 1.0, 0.0)

    def iterate(turn, scalars):
        gamma, energy = scalars
        solve_lines()

        def ends(t, carry):
            backward(t * (size - PLANES))
            return carry

        def others(t, carry):
            backward(PLANES * t)
            return carry

        lax.fori_loop(0, 2, ends, 0)
        halos = [halo_copy(turn, side) for side in range(4)]
        halos[0].start()
        halos[1].start()
        lax.fori_loop(1, size // PLANES - 1, others, 0)
        halos[2].start()
        halos[3].start()

        def apply_some(t, sums):
            for m in range(APPLIES):
                sums = apply(APPLIES * t + m, sums)
            return sums

        zeros = tuple(jnp.zeros((ROWS, LANES), F32) for _ in range(6))
        sums = list(lax.fori_loop(0, size // APPLIES, apply_some, zeros))
        for halo in halos:
            halo.wait_recv()
        ghost = ghosts(turn)
        faces = [back_ref[padded(0), :], back_ref[padded(size - 1), :], edge_ref[0], edge_ref[1]]
        for n in range(4):
            sums[2] = sums[2] - fold(faces[n] * ghost[n])
            sums[3] = sums[3] - fold(ghost[n])
        sums.append(diag_total)
        stacked = jnp.zeros((ROWS, LANES), F32)
        for n, total in enumerate(sums):
            stacked = jnp.where(row8 == n, jnp.sum(total, axis=0, keepdims=True), stacked)
        stacked = jnp.sum(stacked, axis=1, keepdims=True)
        payload = jnp.sum(jnp.where(row8 == lane8, stacked, 0.0), axis=0, keepdims=True)
        gather_start(turn, payload)
        gather_middle(turn)

        @pl.when(turn == 0)
        def _():
            gather_end(ITERS)
            gather_drain(ITERS)

        for halo in halos:
            halo.wait_send()
        every = gather_end(turn)

        matrix = all_ref[ITERS].reshape(LANES, LANES)
        coarse = jnp.dot(matrix, every, precision=lax.Precision.HIGHEST, preferred_element_type=F32)
        coarse = jnp.broadcast_to(coarse[:, :1], (LANES, LANES))
        coarse_pad[pl.ds(ROWS, LANES), :] = coarse
        beside = coarse_pad[pl.ds(0, LANES), :] + coarse_pad[pl.ds(2 * ROWS, LANES), :]
        beside = beside + jnp.where(big_row % ROWS == 0, 0.0, coarse_pad[pl.ds(ROWS - 1, LANES), :])
        beside = beside + jnp.where(big_row % ROWS == n_gy - 1, 0.0, coarse_pad[pl.ds(ROWS + 1, LANES), :])
        ends_total = 2.0 * size * size
        weight = jnp.where((big_lane == 0) | (big_lane == 5), coarse, 1.0)
        weight = jnp.where(big_lane == 3, 2.0 * coarse, weight)
        weight = jnp.where(big_lane == 6, coarse * coarse, weight)
        terms = every * weight
        flux = coarse * (ends_total * coarse + size * LANES * (4.0 * coarse - beside))
        terms = terms + jnp.where(big_lane == 6, flux, 0.0)
        terms = jnp.sum(terms, axis=0, keepdims=True)

        def pick(*lanes):
            mask = slim == lanes[0]
            for which in lanes[1:]:
                mask = mask | (slim == which)
            total = jnp.sum(jnp.where(mask, terms, 0.0), axis=1, keepdims=True)
            return jnp.broadcast_to(total, (ROWS, LANES))

        fresh = pick(0, 1)
        beta = fresh / gamma
        energy = pick(2, 3, 6) + beta * (2.0 * pick(4, 5) + beta * energy)
        alpha = fresh / energy

        own = coarse_pad[pl.ds(ROWS + mine, 1), :]
        across = [
            coarse_pad[pl.ds(mine, 1), :],
            coarse_pad[pl.ds(2 * ROWS + mine, 1), :],
            jnp.where(inside[2], coarse_pad[pl.ds(ROWS - 1 + mine, 1), :], 0.0),
            jnp.where(inside[3], coarse_pad[pl.ds(ROWS + 1 + mine, 1), :], 0.0),
        ]
        fixes = [(own - across[n]) - ghost[n] for n in range(4)]
        image_ref[plane(0), :] = image_ref[plane(0), :] + fixes[0]
        image_ref[plane(size - 1), :] = image_ref[plane(size - 1), :] + fixes[1]
        fix_ref[0] = fixes[2]
        fix_ref[1] = fixes[3]
        own_wide = jnp.broadcast_to(own, (size, LANES))
        alpha_wide = jnp.broadcast_to(alpha[:1], (size, LANES))
        beta_wide = jnp.broadcast_to(beta[:1], (size, LANES))

        def update(t, keep):
            base = pl.multiple_of(t * (PLANES * size), ROWS)
            for m in range(PLANES):
                here = rows(base, m)
                index = t * PLANES + m
                low = jnp.where(row8 == 0, fix_ref[0, pl.ds(index, 1), :], 0.0)
                high = jnp.where(row8 == ROWS - 1, fix_ref[1, pl.ds(index, 1), :], 0.0)
                image = image_ref[here, :]
                image = jnp.concatenate(
                    [image[:ROWS] + low, image[ROWS:size - ROWS], image[size - ROWS:] + high], axis=0
                )
                image = image + own_wide * (diag_ref[here, :] + ends_wide) + beta_wide * s_ref[here, :]
                direction = back_ref[padded(index), :] + own_wide + beta_wide * p_ref[here, :]
                if keep:
                    s_ref[here, :] = image
                    p_ref[here, :] = direction
                x_ref[here, :] = x_ref[here, :] + alpha_wide * direction
                r_ref[here, :] = r_ref[here, :] - alpha_wide * image

        def forward_some(t, shift):
            base = pl.multiple_of(t * (PLANES * size), ROWS)
            forward((t + shift) * PLANES, [r_ref[rows(base, m + shift * PLANES), :] for m in range(PLANES)])

        @pl.when(turn < ITERS - 1)
        def _():
            def body(t, carry):
                forward_some(t, -1)
                update(t, True)
                return carry

            update(0, True)
            lax.fori_loop(1, size // PLANES, body, 0)
            forward_some(size // PLANES - 1, 0)

        @pl.when(turn == ITERS - 1)
        def _():
            def body(t, carry):
                update(t, False)
                return carry

            lax.fori_loop(0, size // PLANES, body, 0)

        gather_drain(turn)
        return fresh, energy

    one = jnp.ones((ROWS, LANES), F32)
    lax.fori_loop(0, ITERS, iterate, (one, jnp.zeros((ROWS, LANES), F32)))


def shards(n_gx, n_gy, right_side, diagonal, sweep_counts, refine_flags, coarse_inverse):
    size, _, cells = right_side.shape
    flat = (size * size, cells)
    table = jnp.asarray(split_table(size))
    mu = jnp.asarray(np.repeat(eigen_values(size).astype(np.float32)[:, None], cells, axis=1))
    subs = n_gx * n_gy
    if coarse_inverse.shape[1] < LANES:
        coarse_inverse = jnp.pad(coarse_inverse, ((0, 0), (0, LANES - subs)))
    operands = (
        right_side.reshape(flat), diagonal.reshape(flat), sweep_counts, refine_flags, coarse_inverse, table, mu
    )
    vmem = pl.BlockSpec(memory_space=pltpu.VMEM)
    hbm = pl.BlockSpec(memory_space=pltpu.HBM)
    field = pltpu.VMEM(flat, F32)
    face = (size, LANES)
    outs = pl.pallas_call(
        functools.partial(kernel, n_gx, n_gy, size),
        out_shape=[jax.ShapeDtypeStruct(flat, F32)] * 2,
        in_specs=[hbm] * 7,
        out_specs=[vmem, vmem],
        scratch_shapes=[
            pltpu.SMEM(sweep_counts.shape, jnp.int32),
            pltpu.VMEM(refine_flags.shape, jnp.int32),
            pltpu.VMEM(coarse_inverse.shape, F32),
            pltpu.VMEM(table.shape, table.dtype),
            pltpu.VMEM(mu.shape, F32),
            field, field, field, field,
            pltpu.VMEM(((size + 2) * (size + ROWS), LANES), F32),
            field, field,
            pltpu.VMEM((size * (size + 1), LANES), F32),
            pltpu.VMEM((size * (size + 1), LANES), F32),
            pltpu.VMEM((GROUPS * LINES * size, LANES), F32),
            field, field, field, field,
            pltpu.VMEM((2,) + face, F32),
            pltpu.VMEM((ITERS, 2) + face, F32),
            pltpu.VMEM((ITERS, 2) + face, F32),
            pltpu.VMEM((2,) + face, F32),
            pltpu.VMEM((GATHERS, n_gy, ROWS, LANES), F32),
            pltpu.VMEM((GATHERS, LANES // ROWS, ROWS, LANES), F32),
            pltpu.VMEM((LANES + 2 * ROWS, LANES), F32),
            pltpu.SemaphoreType.DMA((7,)),
            pltpu.SemaphoreType.DMA((ITERS, 4)),
            pltpu.SemaphoreType.DMA((ITERS, 4)),
            pltpu.SemaphoreType.DMA((GATHERS, n_gy)),
            pltpu.SemaphoreType.DMA((GATHERS, n_gy)),
            pltpu.SemaphoreType.DMA((GATHERS, n_gx)),
            pltpu.SemaphoreType.DMA((GATHERS, n_gx)),
        ],
        compiler_params=pltpu.CompilerParams(
            collective_id=0, has_side_effects=True, vmem_limit_bytes=48 * 1024 * 1024
        ),
        cost_estimate=pl.CostEstimate(flops=4 * 10**9, bytes_accessed=8 * 2**20, transcendentals=0),
        name="pressure_solve",
    )(
        *(pltpu.with_memory_space_constraint(operand, pltpu.HBM) for operand in operands)
    )
    return tuple(out.reshape(right_side.shape) for out in outs)


def solution(mesh):
    return jax.shard_map(
        functools.partial(shards, mesh.shape["gx"], mesh.shape["gy"]),
        mesh=mesh,
        in_specs=(P("gx", "gy", None), P("gx", "gy", None), P(), P(), P(("gx", "gy"), None)),
        out_specs=(P("gx", "gy", None), P("gx", "gy", None)),
        check_vma=False,
    )
```

```python
import functools

import jax
import jax.numpy as jnp
import ml_dtypes
import numpy as np
from jax import lax
from jax.experimental import pallas as pl
from jax.experimental.pallas import tpu as pltpu
from jax.sharding import PartitionSpec as P

ITERS = 4
MOST = 12
LANES = 128
ROWS = 8
GATHERS = ITERS + 2
SUM_LANE = 3
LINES = 4
COLUMNS = 8
PLANES = 16
APPLIES = 8
UPDATES = 8
F32 = jnp.float32
MESH = pl.DeviceIdType.MESH


def sine_table(count):
    index = np.arange(count, dtype=np.float64)
    angle = np.pi * (index[:, None] + 1.0) * (index[None, :] + 1.0) / (count + 1.0)
    return np.sqrt(2.0 / (count + 1.0)) * np.sin(angle)


def eigen_values(count):
    index = np.arange(count, dtype=np.float64)
    return 2.0 - 2.0 * np.cos(np.pi * (index + 1.0) / (count + 1.0))


def split_table(count):
    table = sine_table(count).astype(np.float32)
    high = table.astype(ml_dtypes.bfloat16)
    low = (table - high.astype(np.float32)).astype(ml_dtypes.bfloat16)
    return np.concatenate([np.concatenate([high, high], axis=1), np.concatenate([low, low], axis=1)], axis=0)


def transform(table, field):
    high = field.astype(jnp.bfloat16)
    low = (field - high.astype(F32)).astype(jnp.bfloat16)
    stacked = jnp.concatenate([high, low], axis=0)
    both = jnp.dot(table, stacked, preferred_element_type=F32)
    return both[:field.shape[0]] + both[field.shape[0]:]


def fold(value):
    return jnp.sum(value.reshape(-1, ROWS, LANES), axis=0)


def kernel(
    n_gx, n_gy, size,
    rhs_hbm, diag_hbm, count_hbm, flag_hbm, coarse_hbm, table_hbm, mu_hbm,
    x_ref, r_ref,
    count_ref, flag_ref, coarse_ref, table_ref, mu_ref,
    diag_ref, p_ref, s_ref, image_ref, back_ref, hat_ref, hat_s_ref, hat_r_ref, line_ref, step_ref, mode_ref,
    twice_ref, root_ref, near_ref, far_ref, mid_ref,
    edge_ref, ghost_x, ghost_y, small_ref, all_ref, known_ref,
    in_sem, halo_send, halo_recv, row_send, row_recv, col_send, col_recv,
):
    gx = lax.axis_index("gx")
    gy = lax.axis_index("gy")
    mine = gx * n_gy + gy
    pitch = size + ROWS
    odd_pitch = size + 1
    plain = size * size
    roomy = (size + 2) * pitch
    row8 = lax.broadcasted_iota(jnp.int32, (ROWS, LANES), 0)
    lane8 = lax.broadcasted_iota(jnp.int32, (ROWS, LANES), 1)
    lane = lax.broadcasted_iota(jnp.int32, (size, LANES), 1)
    slim = lax.broadcasted_iota(jnp.int32, (1, LANES), 1)

    def plane(index):
        return pl.ds(pl.multiple_of(index * size, ROWS), size)

    def rows(base, index):
        return pl.ds(base + index * size, size)

    def image_base(parity, first):
        return pl.multiple_of(parity * plain + first * size, ROWS)

    def back_base(parity, first):
        return pl.multiple_of(parity * roomy + (first + 1) * pitch, ROWS)

    pairs = (
        (rhs_hbm, r_ref), (flag_hbm, flag_ref), (mu_hbm, mu_ref), (coarse_hbm, coarse_ref), (count_hbm, count_ref),
        (table_hbm, table_ref), (diag_hbm, diag_ref),
    )
    loads = [pltpu.make_async_copy(source, target, in_sem.at[n]) for n, (source, target) in enumerate(pairs)]
    for load in loads:
        load.start()
    if n_gx * ROWS < LANES:
        all_ref[...] = jnp.zeros_like(all_ref)

    barrier = pltpu.get_barrier_semaphore()

    def over(first, last, act):
        def body(step, carry):
            act(step)
            return carry

        lax.fori_loop(first, last, body, 0)

    def beside_row(step):
        return gx, lax.rem(gy + step, n_gy)

    def beside_col(step):
        return lax.rem(gx + step, n_gx), gy

    def greet(device):
        pl.semaphore_signal(barrier, inc=1, device_id=device, device_id_type=MESH)

    over(1, n_gy, lambda step: greet(beside_row(step)))
    over(1, n_gx, lambda step: greet(beside_col(step)))

    def row_copy(slot, step):
        return pltpu.make_async_remote_copy(
            src_ref=small_ref.at[slot, gy], dst_ref=small_ref.at[slot, gy],
            send_sem=row_send.at[slot, step], recv_sem=row_recv.at[slot, step],
            device_id=beside_row(step), device_id_type=MESH,
        )

    def col_copy(slot, step):
        return pltpu.make_async_remote_copy(
            src_ref=all_ref.at[slot, gx], dst_ref=all_ref.at[slot, gx],
            send_sem=col_send.at[slot, step], recv_sem=col_recv.at[slot, step],
            device_id=beside_col(step), device_id_type=MESH,
        )

    def gather_start(slot, payload):
        small_ref[slot, gy] = jnp.where(row8 == gy, payload, 0.0)
        over(1, n_gy, lambda step: row_copy(slot, step).start())

    def gather_middle(slot):
        over(1, n_gy, lambda step: row_copy(slot, step).wait_recv())
        total = small_ref[slot, 0]
        for other in range(1, n_gy):
            total = total + small_ref[slot, other]
        all_ref[slot, gx] = total
        over(1, n_gx, lambda step: col_copy(slot, step).start())

    def gather_end(slot):
        over(1, n_gx, lambda step: col_copy(slot, step).wait_recv())
        return all_ref[slot].reshape(LANES, LANES)

    def gather_drain(slot):
        over(1, n_gy, lambda step: row_copy(slot, step).wait_send())
        over(1, n_gx, lambda step: col_copy(slot, step).wait_send())

    def lane_pick(row, which):
        total = jnp.sum(jnp.where(slim == which, row, 0.0), axis=1, keepdims=True)
        return jnp.broadcast_to(total, (ROWS, LANES))

    loads[0].wait()

    def add_up(t, total):
        base = pl.multiple_of(t * (8 * size), ROWS)
        for m in range(8):
            total = total + fold(r_ref[rows(base, m), :])
        return total

    total = lax.fori_loop(0, size // 8, add_up, jnp.zeros((ROWS, LANES), F32))
    total = jnp.sum(jnp.sum(total, axis=0, keepdims=True), axis=1, keepdims=True)
    for load in loads[1:6]:
        load.wait()
    pl.semaphore_wait(barrier, n_gx + n_gy - 2)
    gather_start(ITERS, coarse_ref[...])
    gather_start(ITERS + 1, jnp.where(slim == SUM_LANE, total, 0.0))

    shift = 2.5 * flag_ref[pl.ds(mine, 1), :].astype(F32) + 2.5

    def coefficients(b):
        d = mu_ref[...] + mu_ref[pl.ds(b, 1), :] + shift
        root = lax.rsqrt(d)
        root = root * (1.5 - 0.5 * d * root * root)
        near = jnp.where(lane == 0, 0.0, root * pltpu.roll(root, 1, 1))
        square = near * near
        root_ref[plane(b), :] = root
        near_ref[plane(b), :] = near
        far_ref[plane(b), :] = near * pltpu.roll(near, 1, 1)
        mid_ref[plane(b), :] = square + pltpu.roll(square, LANES - 1, 1)

    def coefficient_some(t, carry):
        for m in range(4):
            coefficients(4 * t + m)
        return carry

    lax.fori_loop(0, size // 4, coefficient_some, 0)

    def wipe(t, carry):
        here = pl.ds(pl.multiple_of(t * (4 * size), ROWS), 4 * size)
        for field in (p_ref, s_ref, x_ref, hat_s_ref, hat_r_ref):
            field[here, :] = jnp.zeros((4 * size, LANES), F32)
        return carry

    lax.fori_loop(0, size // 4, wipe, 0)

    for parity in range(2):
        back_ref[pl.ds(parity * roomy, pitch), :] = jnp.zeros((pitch, LANES), F32)
        back_ref[pl.ds(parity * roomy + (size + 1) * pitch, pitch), :] = jnp.zeros((pitch, LANES), F32)

    def clear(index, carry):
        for parity in range(2):
            start = pl.multiple_of(parity * roomy + (index + 1) * pitch + size, ROWS)
            back_ref[pl.ds(start, ROWS), :] = jnp.zeros((ROWS, LANES), F32)
        return carry

    lax.fori_loop(0, size, clear, 0)
    gather_middle(ITERS)
    gather_middle(ITERS + 1)

    count = jnp.full((ROWS, LANES), count_ref[mine], jnp.int32)
    count = jnp.concatenate([count] * (size // ROWS), axis=0)
    odd = count % 2 == 1
    active = [count > 2 * step for step in range(MOST // 2)]

    def transform_all(parts):
        table = table_ref[...]
        done = []
        for n in range(0, len(parts), 2):
            both = transform(table, jnp.concatenate(parts[n:n + 2], axis=1))
            done += [both[:, :LANES], both[:, LANES:]]
        return done

    def odd_base(first):
        return pl.multiple_of(first * odd_pitch, ROWS)

    def forward_y(source, parity):
        def body(t, carry):
            base = image_base(parity, t * PLANES)
            target = odd_base(t * PLANES)
            parts = [source[rows(base, m), :] for m in range(PLANES)]
            for m, part in enumerate(transform_all(parts)):
                step_ref[pl.ds(target + m * odd_pitch, size), :] = part
            return carry

        lax.fori_loop(0, size // PLANES, body, 0)

    def forward_x():
        def body(t, carry):
            first = t * COLUMNS
            base = pl.multiple_of(first * size, ROWS)
            parts = [step_ref[pl.ds(first + m, size, stride=odd_pitch), :] for m in range(COLUMNS)]
            for m, part in enumerate(transform_all(parts)):
                hat_ref[rows(base, m), :] = part
            return carry

        lax.fori_loop(0, size // COLUMNS, body, 0)

    def lines_sweep(base, shift, alpha, beta, sums):
        sums = list(sums)
        for part in range(0, COLUMNS, LINES):
            here = [rows(base, m + part + shift) for m in range(LINES)]
            kept = [pl.ds((part + m) * size, size) for m in range(LINES)]
            guess = []
            for m in range(LINES):
                hat_s = hat_ref[here[m], :] + beta * hat_s_ref[here[m], :]
                hat_r = hat_r_ref[here[m], :] - alpha * hat_s
                hat_s_ref[here[m], :] = hat_s
                hat_r_ref[here[m], :] = hat_r
                near = near_ref[here[m], :]
                start = hat_r * root_ref[here[m], :]
                twice = start + near * pltpu.roll(start, 1, 1) + pltpu.roll(near * start, LANES - 1, 1)
                twice_ref[kept[m], :] = twice
                guess.append(jnp.where(odd, start, twice))
            for step in range(1, MOST // 2):
                for m in range(LINES):
                    far = far_ref[here[m], :]
                    fresh = (twice_ref[kept[m], :] + mid_ref[here[m], :] * guess[m]) + (
                        far * pltpu.roll(guess[m], 2, 1) + pltpu.roll(far * guess[m], LANES - 2, 1)
                    )
                    guess[m] = jnp.where(active[step], fresh, guess[m])
            for m in range(LINES):
                line = guess[m] * root_ref[here[m], :]
                line_ref[here[m], :] = line
                sums[0] = sums[0] + fold(line * hat_r_ref[here[m], :])
                sums[1] = sums[1] + fold(line * hat_s_ref[here[m], :])
        return tuple(sums)

    def lines_out(base, shift, target):
        parts = [line_ref[rows(base, m + shift), :] for m in range(COLUMNS)]
        for m, part in enumerate(transform_all(parts)):
            mode_ref[pl.ds(target + m * odd_pitch, size), :] = part

    def solve_lines(alpha, beta):
        alpha = jnp.broadcast_to(alpha[:1], (size, LANES))
        beta = jnp.broadcast_to(beta[:1], (size, LANES))

        def body(t, sums):
            base = pl.multiple_of(t * (COLUMNS * size), ROWS)
            lines_out(base, -COLUMNS, odd_base((t - 1) * COLUMNS))
            return lines_sweep(base, 0, alpha, beta, sums)

        zeros = (jnp.zeros((ROWS, LANES), F32),) * 2
        sums = lines_sweep(0, 0, alpha, beta, zeros)
        sums = lax.fori_loop(1, size // COLUMNS, body, sums)
        lines_out(plain, -COLUMNS, (size - COLUMNS) * odd_pitch)
        return sums

    def backward(parity, first, own):
        parts = [mode_ref[pl.ds(first + m, size, stride=odd_pitch), :] for m in range(PLANES)]
        base = back_base(parity, first)
        for m, part in enumerate(transform_all(parts)):
            part = part + own
            back_ref[pl.ds(base + m * pitch, size), :] = part
            edge_ref[0, pl.ds(first + m, 1), :] = part[:1]
            edge_ref[1, pl.ds(first + m, 1), :] = part[size - 1:]

    def halo_copy(turn, side):
        if side < 2:
            device = beside_col(1 if side == 0 else n_gx - 1)
            source = back_ref.at[pl.ds(back_base(turn % 2, size - 1 if side == 0 else 0), size)]
            target = ghost_x.at[turn, side]
        else:
            device = beside_row(1 if side == 2 else n_gy - 1)
            source = edge_ref.at[1 if side == 2 else 0]
            target = ghost_y.at[turn, side - 2]
        return pltpu.make_async_remote_copy(
            src_ref=source, dst_ref=target,
            send_sem=halo_send.at[turn, side], recv_sem=halo_recv.at[turn, side],
            device_id=device, device_id_type=MESH,
        )

    inside = [gx > 0, gx < n_gx - 1, gy > 0, gy < n_gy - 1]

    def ghosts(turn):
        raw = [ghost_x[turn, 0], ghost_x[turn, 1], ghost_y[turn, 0], ghost_y[turn, 1]]
        return [jnp.where(inside[n], raw[n], 0.0) for n in range(4)]

    def apply(parity, i, sums):
        start = back_base(parity, i)
        here = back_ref[pl.ds(start, size), :]
        beside = back_ref[pl.ds(start - pitch, size), :] + back_ref[pl.ds(start + pitch, size), :]
        beside = beside + back_ref[pl.ds(start - 1, size), :] + back_ref[pl.ds(start + 1, size), :]
        below = jnp.where(lane == 0, 0.0, pltpu.roll(here, 1, 1))
        above = jnp.where(lane == LANES - 1, 0.0, pltpu.roll(here, LANES - 1, 1))
        image = (6.0 + diag_ref[plane(i), :]) * here - (beside + (below + above))
        image_ref[pl.ds(image_base(parity, i), size), :] = image
        return sums[0] + fold(here * image), sums[1] + fold(image)

    def update(parity, alpha, beta):
        alpha = jnp.broadcast_to(alpha[:1], (size, LANES))
        beta = jnp.broadcast_to(beta[:1], (size, LANES))

        def body(t, carry):
            base = pl.multiple_of(t * (UPDATES * size), ROWS)
            image = image_base(parity, t * UPDATES)
            back = back_base(parity, t * UPDATES)
            for m in range(UPDATES):
                here = rows(base, m)
                moved = image_ref[rows(image, m), :] + beta * s_ref[here, :]
                direction = back_ref[pl.ds(back + m * pitch, size), :] + beta * p_ref[here, :]
                s_ref[here, :] = moved
                p_ref[here, :] = direction
                x_ref[here, :] = x_ref[here, :] + alpha * direction
                r_ref[here, :] = r_ref[here, :] - alpha * moved
            return carry

        lax.fori_loop(0, size // UPDATES, body, 0)

    forward_y(r_ref, 0)
    forward_x()
    loads[6].wait()
    gather_end(ITERS)
    sums = gather_end(ITERS + 1)

    def spread(matrix):
        return jnp.broadcast_to(matrix[:, SUM_LANE:SUM_LANE + 1], (LANES, LANES))

    def coarse_solve():
        known_ref[2] = jnp.dot(
            all_ref[ITERS].reshape(LANES, LANES), known_ref[0],
            precision=lax.Precision.HIGHEST, preferred_element_type=F32,
        )

    known_ref[0] = spread(sums)
    known_ref[1] = jnp.zeros((LANES, LANES), F32)
    coarse_solve()
    gather_drain(ITERS)
    gather_drain(ITERS + 1)

    def iterate(turn, scalars):
        gamma, energy, alpha, beta = scalars
        parity = turn % 2
        own = known_ref[2, pl.ds(mine, 1), :]
        extra = jnp.where(row8 == 0, own * known_ref[0, pl.ds(mine, 1), :], 0.0)
        extra = jnp.where(row8 == 2, own * known_ref[1, pl.ds(mine, 1), :], extra)
        mode_sums = solve_lines(alpha, beta)

        def ends(t, carry):
            backward(parity, t * (size - PLANES), own)
            return carry

        def others(t, carry):
            backward(parity, t * PLANES, own)
            return carry

        lax.fori_loop(0, 2, ends, 0)
        halos = [halo_copy(turn, side) for side in range(4)]
        halos[0].start()
        halos[1].start()
        lax.fori_loop(1, size // PLANES - 1, others, 0)
        halos[2].start()
        halos[3].start()

        def apply_some(t, sums):
            for m in range(APPLIES):
                sums = apply(parity, APPLIES * t + m, sums)
            return sums

        zeros = (jnp.zeros((ROWS, LANES), F32),) * 2
        curve, flow = lax.fori_loop(0, size // APPLIES, apply_some, zeros)
        for halo in halos:
            halo.wait_recv()
        ghost = ghosts(turn)
        low = pl.ds(back_base(parity, 0), size)
        high = pl.ds(back_base(parity, size - 1), size)
        faces = [back_ref[low, :], back_ref[high, :], edge_ref[0], edge_ref[1]]
        for n in range(4):
            curve = curve - fold(faces[n] * ghost[n])
            flow = flow - fold(ghost[n])
        stacked = jnp.zeros((ROWS, LANES), F32)
        for n, total in enumerate((mode_sums[0], curve, mode_sums[1], flow)):
            stacked = jnp.where(row8 == n, jnp.sum(total, axis=0, keepdims=True), stacked)
        stacked = jnp.sum(stacked, axis=1, keepdims=True) + extra
        payload = jnp.sum(jnp.where(row8 == lane8, stacked, 0.0), axis=0, keepdims=True)
        gather_start(turn, payload)

        base = image_base(parity, 0)
        spots = [
            pl.ds(base, size), pl.ds(base + (size - 1) * size, size),
            pl.ds(base, size, stride=size), pl.ds(base + size - 1, size, stride=size),
        ]
        for n in range(4):
            image_ref[spots[n], :] = image_ref[spots[n], :] - ghost[n]

        @pl.when(turn < ITERS - 1)
        def _():
            forward_y(image_ref, parity)

        gather_middle(turn)

        @pl.when(turn < ITERS - 1)
        def _():
            forward_x()

        @pl.when(turn > 0)
        def _():
            update(1 - parity, alpha, beta)

        for halo in halos:
            halo.wait_send()
        every = gather_end(turn)
        totals = jnp.sum(every, axis=0, keepdims=True)
        fresh = lane_pick(totals, 0)
        beta = jnp.where(turn == 0, 0.0, fresh / gamma)
        energy = lane_pick(totals, 1) + beta * (2.0 * lane_pick(totals, 2) + beta * energy)
        alpha = fresh / energy
        known_ref[1] = spread(every) + beta[:1] * known_ref[1]
        known_ref[0] = known_ref[0] - alpha[:1] * known_ref[1]
        coarse_solve()
        gather_drain(turn)
        return fresh, energy, alpha, beta

    one = jnp.ones((ROWS, LANES), F32)
    zero = jnp.zeros((ROWS, LANES), F32)
    gamma, energy, alpha, beta = lax.fori_loop(0, ITERS, iterate, (one, zero, -one, zero))
    update((ITERS - 1) % 2, alpha, beta)


def shards(n_gx, n_gy, right_side, diagonal, sweep_counts, refine_flags, coarse_inverse):
    size, _, cells = right_side.shape
    flat = (size * size, cells)
    table = jnp.asarray(split_table(size))
    mu = jnp.asarray(np.repeat(eigen_values(size).astype(np.float32)[:, None], cells, axis=1))
    subs = n_gx * n_gy
    if coarse_inverse.shape[1] < LANES:
        coarse_inverse = jnp.pad(coarse_inverse, ((0, 0), (0, LANES - subs)))
    operands = (
        right_side.reshape(flat), diagonal.reshape(flat), sweep_counts, refine_flags, coarse_inverse, table, mu
    )
    vmem = pl.BlockSpec(memory_space=pltpu.VMEM)
    hbm = pl.BlockSpec(memory_space=pltpu.HBM)
    field = pltpu.VMEM(flat, F32)
    face = (size, LANES)
    outs = pl.pallas_call(
        functools.partial(kernel, n_gx, n_gy, size),
        out_shape=[jax.ShapeDtypeStruct(flat, F32)] * 2,
        in_specs=[hbm] * 7,
        out_specs=[vmem, vmem],
        scratch_shapes=[
            pltpu.SMEM(sweep_counts.shape, jnp.int32),
            pltpu.VMEM(refine_flags.shape, jnp.int32),
            pltpu.VMEM(coarse_inverse.shape, F32),
            pltpu.VMEM(table.shape, table.dtype),
            pltpu.VMEM(mu.shape, F32),
            field, field, field,
            pltpu.VMEM((2 * size * size, LANES), F32),
            pltpu.VMEM((2 * (size + 2) * (size + ROWS), LANES), F32),
            field, field, field, field,
            pltpu.VMEM((size * (size + 1), LANES), F32),
            pltpu.VMEM((size * (size + 1), LANES), F32),
            pltpu.VMEM((COLUMNS * size, LANES), F32),
            field, field, field, field,
            pltpu.VMEM((2,) + face, F32),
            pltpu.VMEM((ITERS, 2) + face, F32),
            pltpu.VMEM((ITERS, 2) + face, F32),
            pltpu.VMEM((GATHERS, n_gy, ROWS, LANES), F32),
            pltpu.VMEM((GATHERS, LANES // ROWS, ROWS, LANES), F32),
            pltpu.VMEM((3, LANES, LANES), F32),
            pltpu.SemaphoreType.DMA((7,)),
            pltpu.SemaphoreType.DMA((ITERS, 4)),
            pltpu.SemaphoreType.DMA((ITERS, 4)),
            pltpu.SemaphoreType.DMA((GATHERS, n_gy)),
            pltpu.SemaphoreType.DMA((GATHERS, n_gy)),
            pltpu.SemaphoreType.DMA((GATHERS, n_gx)),
            pltpu.SemaphoreType.DMA((GATHERS, n_gx)),
        ],
        compiler_params=pltpu.CompilerParams(
            collective_id=0, has_side_effects=True, vmem_limit_bytes=48 * 1024 * 1024
        ),
        cost_estimate=pl.CostEstimate(flops=4 * 10**9, bytes_accessed=8 * 2**20, transcendentals=0),
        name="pressure_solve",
    )(
        *(pltpu.with_memory_space_constraint(operand, pltpu.HBM) for operand in operands)
    )
    return tuple(out.reshape(right_side.shape) for out in outs)


def solution(mesh):
    return jax.shard_map(
        functools.partial(shards, mesh.shape["gx"], mesh.shape["gy"]),
        mesh=mesh,
        in_specs=(P("gx", "gy", None), P("gx", "gy", None), P(), P(), P(("gx", "gy"), None)),
        out_specs=(P("gx", "gy", None), P("gx", "gy", None)),
        check_vma=False,
    )
```

```python
import functools

import jax
import jax.numpy as jnp
import ml_dtypes
import numpy as np
from jax import lax
from jax.experimental import pallas as pl
from jax.experimental.pallas import tpu as pltpu
from jax.sharding import PartitionSpec as P

ITERS = 4
MOST = 12
LANES = 128
ROWS = 8
GATHERS = ITERS + 2
SUM_LANE = 3
LINES = 4
COLUMNS = 8
PLANES = 16
APPLIES = 8
UPDATES = 8
F32 = jnp.float32
MESH = pl.DeviceIdType.MESH


def sine_table(count):
    index = np.arange(count, dtype=np.float64)
    angle = np.pi * (index[:, None] + 1.0) * (index[None, :] + 1.0) / (count + 1.0)
    return np.sqrt(2.0 / (count + 1.0)) * np.sin(angle)


def eigen_values(count):
    index = np.arange(count, dtype=np.float64)
    return 2.0 - 2.0 * np.cos(np.pi * (index + 1.0) / (count + 1.0))


def split_table(count):
    table = sine_table(count).astype(np.float32)
    high = table.astype(ml_dtypes.bfloat16)
    low = (table - high.astype(np.float32)).astype(ml_dtypes.bfloat16)
    return np.concatenate([high, high, low, low], axis=1)


def transform(table, field):
    high = field.astype(jnp.bfloat16)
    low = (field - high.astype(F32)).astype(jnp.bfloat16)
    stacked = jnp.concatenate([high, low, high, low], axis=0)
    return jnp.dot(table, stacked, preferred_element_type=F32)


def fold(value):
    return jnp.sum(value.reshape(-1, ROWS, LANES), axis=0)


def kernel(
    n_gx, n_gy, size,
    rhs_hbm, diag_hbm, count_hbm, flag_hbm, coarse_hbm, table_hbm, mu_hbm,
    x_ref, r_ref,
    count_ref, flag_ref, coarse_ref, table_ref, mu_ref,
    diag_ref, p_ref, s_ref, image_ref, back_ref, hat_ref, hat_s_ref, hat_r_ref, line_ref, step_ref, mode_ref,
    twice_ref, root_ref, near_ref, far_ref, mid_ref,
    edge_ref, ghost_x, ghost_y, small_ref, all_ref, known_ref,
    in_sem, halo_send, halo_recv, row_send, row_recv, col_send, col_recv,
):
    gx = lax.axis_index("gx")
    gy = lax.axis_index("gy")
    mine = gx * n_gy + gy
    pitch = size + ROWS
    odd_pitch = size + 1
    plain = size * size
    roomy = (size + 2) * pitch
    row8 = lax.broadcasted_iota(jnp.int32, (ROWS, LANES), 0)
    lane8 = lax.broadcasted_iota(jnp.int32, (ROWS, LANES), 1)
    lane = lax.broadcasted_iota(jnp.int32, (size, LANES), 1)
    slim = lax.broadcasted_iota(jnp.int32, (1, LANES), 1)

    def plane(index):
        return pl.ds(pl.multiple_of(index * size, ROWS), size)

    def rows(base, index):
        return pl.ds(base + index * size, size)

    def image_base(parity, first):
        return pl.multiple_of(parity * plain + first * size, ROWS)

    def back_base(parity, first):
        return pl.multiple_of(parity * roomy + (first + 1) * pitch, ROWS)

    pairs = (
        (rhs_hbm, r_ref), (flag_hbm, flag_ref), (mu_hbm, mu_ref), (coarse_hbm, coarse_ref), (count_hbm, count_ref),
        (table_hbm, table_ref), (diag_hbm, diag_ref),
    )
    loads = [pltpu.make_async_copy(source, target, in_sem.at[n]) for n, (source, target) in enumerate(pairs)]
    for load in loads:
        load.start()
    if n_gx * ROWS < LANES:
        all_ref[...] = jnp.zeros_like(all_ref)

    barrier = pltpu.get_barrier_semaphore()

    def over(first, last, act):
        def body(step, carry):
            act(step)
            return carry

        lax.fori_loop(first, last, body, 0)

    def beside_row(step):
        return gx, lax.rem(gy + step, n_gy)

    def beside_col(step):
        return lax.rem(gx + step, n_gx), gy

    def greet(device):
        pl.semaphore_signal(barrier, inc=1, device_id=device, device_id_type=MESH)

    over(1, n_gy, lambda step: greet(beside_row(step)))
    over(1, n_gx, lambda step: greet(beside_col(step)))

    def row_copy(slot, step):
        return pltpu.make_async_remote_copy(
            src_ref=small_ref.at[slot, gy], dst_ref=small_ref.at[slot, gy],
            send_sem=row_send.at[slot, step], recv_sem=row_recv.at[slot, step],
            device_id=beside_row(step), device_id_type=MESH,
        )

    def col_copy(slot, step):
        return pltpu.make_async_remote_copy(
            src_ref=all_ref.at[slot, gx], dst_ref=all_ref.at[slot, gx],
            send_sem=col_send.at[slot, step], recv_sem=col_recv.at[slot, step],
            device_id=beside_col(step), device_id_type=MESH,
        )

    def gather_start(slot, payload):
        small_ref[slot, gy] = jnp.where(row8 == gy, payload, 0.0)
        over(1, n_gy, lambda step: row_copy(slot, step).start())

    def gather_middle(slot):
        over(1, n_gy, lambda step: row_copy(slot, step).wait_recv())
        total = small_ref[slot, 0]
        for other in range(1, n_gy):
            total = total + small_ref[slot, other]
        all_ref[slot, gx] = total
        over(1, n_gx, lambda step: col_copy(slot, step).start())

    def gather_end(slot):
        over(1, n_gx, lambda step: col_copy(slot, step).wait_recv())
        return all_ref[slot].reshape(LANES, LANES)

    def gather_drain(slot):
        over(1, n_gy, lambda step: row_copy(slot, step).wait_send())
        over(1, n_gx, lambda step: col_copy(slot, step).wait_send())

    def lane_pick(row, which):
        total = jnp.sum(jnp.where(slim == which, row, 0.0), axis=1, keepdims=True)
        return jnp.broadcast_to(total, (ROWS, LANES))

    loads[0].wait()

    def add_up(t, total):
        base = pl.multiple_of(t * (8 * size), ROWS)
        for m in range(8):
            total = total + fold(r_ref[rows(base, m), :])
        return total

    total = lax.fori_loop(0, size // 8, add_up, jnp.zeros((ROWS, LANES), F32))
    total = jnp.sum(jnp.sum(total, axis=0, keepdims=True), axis=1, keepdims=True)
    for load in loads[1:6]:
        load.wait()
    pl.semaphore_wait(barrier, n_gx + n_gy - 2)
    gather_start(ITERS, coarse_ref[...])
    gather_start(ITERS + 1, jnp.where(slim == SUM_LANE, total, 0.0))

    shift = 2.5 * flag_ref[pl.ds(mine, 1), :].astype(F32) + 2.5

    def coefficients(b):
        d = mu_ref[...] + mu_ref[pl.ds(b, 1), :] + shift
        root = lax.rsqrt(d)
        root = root * (1.5 - 0.5 * d * root * root)
        near = jnp.where(lane == 0, 0.0, root * pltpu.roll(root, 1, 1))
        square = near * near
        root_ref[plane(b), :] = root
        near_ref[plane(b), :] = near
        far_ref[plane(b), :] = near * pltpu.roll(near, 1, 1)
        mid_ref[plane(b), :] = square + pltpu.roll(square, LANES - 1, 1)

    def wipe(t, carry):
        here = pl.ds(pl.multiple_of(t * (4 * size), ROWS), 4 * size)
        for field in (p_ref, s_ref, x_ref, hat_s_ref, hat_r_ref):
            field[here, :] = jnp.zeros((4 * size, LANES), F32)
        return carry

    lax.fori_loop(0, size // 4, wipe, 0)

    for parity in range(2):
        back_ref[pl.ds(parity * roomy, pitch), :] = jnp.zeros((pitch, LANES), F32)
        back_ref[pl.ds(parity * roomy + (size + 1) * pitch, pitch), :] = jnp.zeros((pitch, LANES), F32)

    def clear(index, carry):
        for parity in range(2):
            start = pl.multiple_of(parity * roomy + (index + 1) * pitch + size, ROWS)
            back_ref[pl.ds(start, ROWS), :] = jnp.zeros((ROWS, LANES), F32)
        return carry

    lax.fori_loop(0, size, clear, 0)

    count = jnp.full((ROWS, LANES), count_ref[mine], jnp.int32)
    count = jnp.concatenate([count] * (size // ROWS), axis=0)
    odd = count % 2 == 1
    active = [count > 2 * step for step in range(MOST // 2)]

    def transform_all(parts):
        table = table_ref[...]
        done = []
        for n in range(0, len(parts), 2):
            both = transform(table, jnp.concatenate(parts[n:n + 2], axis=1))
            done += [both[:, :LANES], both[:, LANES:]]
        return done

    def odd_base(first):
        return pl.multiple_of(first * odd_pitch, ROWS)

    def forward_y(source, parity, also=None):
        def body(t):
            base = image_base(parity, t * PLANES)
            target = odd_base(t * PLANES)
            parts = [source[rows(base, m), :] for m in range(PLANES)]
            for m, part in enumerate(transform_all(parts)):
                step_ref[pl.ds(target + m * odd_pitch, size), :] = part
            if also is not None:
                for m in range(PLANES):
                    also(t * PLANES + m)

        over(0, size // PLANES, body)

    def forward_x(t):
        first = t * COLUMNS
        base = pl.multiple_of(first * size, ROWS)
        parts = [step_ref[pl.ds(first + m, size, stride=odd_pitch), :] for m in range(COLUMNS)]
        for m, part in enumerate(transform_all(parts)):
            hat_ref[rows(base, m), :] = part

    def lines_sweep(base, shift, alpha, beta, sums):
        sums = list(sums)
        for part in range(0, COLUMNS, LINES):
            here = [rows(base, m + part + shift) for m in range(LINES)]
            kept = [pl.ds((part + m) * size, size) for m in range(LINES)]
            guess = []
            for m in range(LINES):
                hat_s = hat_ref[here[m], :] + beta * hat_s_ref[here[m], :]
                hat_r = hat_r_ref[here[m], :] - alpha * hat_s
                hat_s_ref[here[m], :] = hat_s
                hat_r_ref[here[m], :] = hat_r
                near = near_ref[here[m], :]
                start = hat_r * root_ref[here[m], :]
                twice = start + near * pltpu.roll(start, 1, 1) + pltpu.roll(near * start, LANES - 1, 1)
                twice_ref[kept[m], :] = twice
                guess.append(jnp.where(odd, start, twice))
            for step in range(1, MOST // 2):
                for m in range(LINES):
                    far = far_ref[here[m], :]
                    fresh = (twice_ref[kept[m], :] + mid_ref[here[m], :] * guess[m]) + (
                        far * pltpu.roll(guess[m], 2, 1) + pltpu.roll(far * guess[m], LANES - 2, 1)
                    )
                    guess[m] = jnp.where(active[step], fresh, guess[m])
            for m in range(LINES):
                line = guess[m] * root_ref[here[m], :]
                line_ref[here[m], :] = line
                sums[0] = sums[0] + fold(line * hat_r_ref[here[m], :])
                sums[1] = sums[1] + fold(line * hat_s_ref[here[m], :])
        return tuple(sums)

    def lines_out(base, shift, target):
        parts = [line_ref[rows(base, m + shift), :] for m in range(COLUMNS)]
        for m, part in enumerate(transform_all(parts)):
            mode_ref[pl.ds(target + m * odd_pitch, size), :] = part

    def solve_lines(alpha, beta):
        alpha = jnp.broadcast_to(alpha[:1], (size, LANES))
        beta = jnp.broadcast_to(beta[:1], (size, LANES))

        def body(t, sums):
            base = pl.multiple_of(t * (COLUMNS * size), ROWS)
            lines_out(base, -COLUMNS, odd_base((t - 1) * COLUMNS))
            return lines_sweep(base, 0, alpha, beta, sums)

        zeros = (jnp.zeros((ROWS, LANES), F32),) * 2
        sums = lines_sweep(0, 0, alpha, beta, zeros)
        sums = lax.fori_loop(1, size // COLUMNS, body, sums)
        lines_out(plain, -COLUMNS, (size - COLUMNS) * odd_pitch)
        return sums

    def backward(parity, first, own):
        parts = [mode_ref[pl.ds(first + m, size, stride=odd_pitch), :] for m in range(PLANES)]
        base = back_base(parity, first)
        for m, part in enumerate(transform_all(parts)):
            part = part + own
            back_ref[pl.ds(base + m * pitch, size), :] = part
            edge_ref[0, pl.ds(first + m, 1), :] = part[:1]
            edge_ref[1, pl.ds(first + m, 1), :] = part[size - 1:]

    def halo_copy(turn, side):
        if side < 2:
            device = beside_col(1 if side == 0 else n_gx - 1)
            source = back_ref.at[pl.ds(back_base(turn % 2, size - 1 if side == 0 else 0), size)]
            target = ghost_x.at[turn, side]
        else:
            device = beside_row(1 if side == 2 else n_gy - 1)
            source = edge_ref.at[1 if side == 2 else 0]
            target = ghost_y.at[turn, side - 2]
        return pltpu.make_async_remote_copy(
            src_ref=source, dst_ref=target,
            send_sem=halo_send.at[turn, side], recv_sem=halo_recv.at[turn, side],
            device_id=device, device_id_type=MESH,
        )

    inside = [gx > 0, gx < n_gx - 1, gy > 0, gy < n_gy - 1]

    def ghosts(turn):
        raw = [ghost_x[turn, 0], ghost_x[turn, 1], ghost_y[turn, 0], ghost_y[turn, 1]]
        return [jnp.where(inside[n], raw[n], 0.0) for n in range(4)]

    def apply(parity, i, sums):
        start = back_base(parity, i)
        here = back_ref[pl.ds(start, size), :]
        beside = back_ref[pl.ds(start - pitch, size), :] + back_ref[pl.ds(start + pitch, size), :]
        beside = beside + back_ref[pl.ds(start - 1, size), :] + back_ref[pl.ds(start + 1, size), :]
        below = jnp.where(lane == 0, 0.0, pltpu.roll(here, 1, 1))
        above = jnp.where(lane == LANES - 1, 0.0, pltpu.roll(here, LANES - 1, 1))
        image = (6.0 + diag_ref[plane(i), :]) * here - (beside + (below + above))
        image_ref[pl.ds(image_base(parity, i), size), :] = image
        return sums[0] + fold(here * image), sums[1] + fold(image)

    def update(parity, alpha, beta):
        alpha = jnp.broadcast_to(alpha[:1], (size, LANES))
        beta = jnp.broadcast_to(beta[:1], (size, LANES))

        def body(t):
            base = pl.multiple_of(t * (UPDATES * size), ROWS)
            image = image_base(parity, t * UPDATES)
            back = back_base(parity, t * UPDATES)
            for m in range(UPDATES):
                here = rows(base, m)
                moved = image_ref[rows(image, m), :] + beta * s_ref[here, :]
                direction = back_ref[pl.ds(back + m * pitch, size), :] + beta * p_ref[here, :]
                s_ref[here, :] = moved
                p_ref[here, :] = direction
                x_ref[here, :] = x_ref[here, :] + alpha * direction
                r_ref[here, :] = r_ref[here, :] - alpha * moved

        return body

    forward_y(r_ref, 0, coefficients)
    gather_middle(ITERS)
    gather_middle(ITERS + 1)
    over(0, size // COLUMNS, forward_x)
    loads[6].wait()
    gather_end(ITERS)
    sums = gather_end(ITERS + 1)

    def spread(matrix):
        return jnp.broadcast_to(matrix[:, SUM_LANE:SUM_LANE + 1], (LANES, LANES))

    def coarse_solve():
        known_ref[2] = jnp.dot(
            all_ref[ITERS].reshape(LANES, LANES), known_ref[0],
            precision=lax.Precision.HIGHEST, preferred_element_type=F32,
        )

    known_ref[0] = spread(sums)
    known_ref[1] = jnp.zeros((LANES, LANES), F32)
    coarse_solve()
    gather_drain(ITERS)
    gather_drain(ITERS + 1)

    def iterate(turn, scalars):
        gamma, energy, alpha, beta = scalars
        parity = turn % 2
        own = known_ref[2, pl.ds(mine, 1), :]
        extra = jnp.where(row8 == 0, own * known_ref[0, pl.ds(mine, 1), :], 0.0)
        extra = jnp.where(row8 == 2, own * known_ref[1, pl.ds(mine, 1), :], extra)
        mode_sums = solve_lines(alpha, beta)

        def ends(t, carry):
            backward(parity, t * (size - PLANES), own)
            return carry

        def others(t, carry):
            backward(parity, t * PLANES, own)
            return carry

        lax.fori_loop(0, 2, ends, 0)
        halos = [halo_copy(turn, side) for side in range(4)]
        halos[0].start()
        halos[1].start()
        lax.fori_loop(1, size // PLANES - 1, others, 0)
        halos[2].start()
        halos[3].start()

        def apply_some(t, sums):
            for m in range(APPLIES):
                sums = apply(parity, APPLIES * t + m, sums)
            return sums

        zeros = (jnp.zeros((ROWS, LANES), F32),) * 2
        curve, flow = lax.fori_loop(0, size // APPLIES, apply_some, zeros)
        for halo in halos:
            halo.wait_recv()
        ghost = ghosts(turn)
        low = pl.ds(back_base(parity, 0), size)
        high = pl.ds(back_base(parity, size - 1), size)
        faces = [back_ref[low, :], back_ref[high, :], edge_ref[0], edge_ref[1]]
        for n in range(4):
            curve = curve - fold(faces[n] * ghost[n])
            flow = flow - fold(ghost[n])
        stacked = jnp.zeros((ROWS, LANES), F32)
        for n, total in enumerate((mode_sums[0], curve, mode_sums[1], flow)):
            stacked = jnp.where(row8 == n, jnp.sum(total, axis=0, keepdims=True), stacked)
        stacked = jnp.sum(stacked, axis=1, keepdims=True) + extra
        payload = jnp.sum(jnp.where(row8 == lane8, stacked, 0.0), axis=0, keepdims=True)
        gather_start(turn, payload)

        base = image_base(parity, 0)
        spots = [
            pl.ds(base, size), pl.ds(base + (size - 1) * size, size),
            pl.ds(base, size, stride=size), pl.ds(base + size - 1, size, stride=size),
        ]
        for n in range(4):
            image_ref[spots[n], :] = image_ref[spots[n], :] - ghost[n]

        @pl.when(turn < ITERS - 1)
        def _():
            forward_y(image_ref, parity)

        gather_middle(turn)

        updated = update(1 - parity, alpha, beta)

        def both(t):
            forward_x(t)
            updated(t)

        @pl.when(turn == 0)
        def _():
            over(0, size // COLUMNS, forward_x)

        @pl.when((turn > 0) & (turn < ITERS - 1))
        def _():
            over(0, size // COLUMNS, both)

        @pl.when(turn == ITERS - 1)
        def _():
            over(0, size // UPDATES, updated)

        for halo in halos:
            halo.wait_send()
        every = gather_end(turn)
        totals = jnp.sum(every, axis=0, keepdims=True)
        fresh = lane_pick(totals, 0)
        beta = jnp.where(turn == 0, 0.0, fresh / gamma)
        energy = lane_pick(totals, 1) + beta * (2.0 * lane_pick(totals, 2) + beta * energy)
        alpha = fresh / energy
        known_ref[1] = spread(every) + beta[:1] * known_ref[1]
        known_ref[0] = known_ref[0] - alpha[:1] * known_ref[1]
        coarse_solve()
        gather_drain(turn)
        return fresh, energy, alpha, beta

    one = jnp.ones((ROWS, LANES), F32)
    zero = jnp.zeros((ROWS, LANES), F32)
    gamma, energy, alpha, beta = lax.fori_loop(0, ITERS, iterate, (one, zero, -one, zero))
    over(0, size // UPDATES, update((ITERS - 1) % 2, alpha, beta))


def shards(n_gx, n_gy, right_side, diagonal, sweep_counts, refine_flags, coarse_inverse):
    size, _, cells = right_side.shape
    flat = (size * size, cells)
    table = jnp.asarray(split_table(size))
    mu = jnp.asarray(np.repeat(eigen_values(size).astype(np.float32)[:, None], cells, axis=1))
    subs = n_gx * n_gy
    if coarse_inverse.shape[1] < LANES:
        coarse_inverse = jnp.pad(coarse_inverse, ((0, 0), (0, LANES - subs)))
    operands = (
        right_side.reshape(flat), diagonal.reshape(flat), sweep_counts, refine_flags, coarse_inverse, table, mu
    )
    vmem = pl.BlockSpec(memory_space=pltpu.VMEM)
    hbm = pl.BlockSpec(memory_space=pltpu.HBM)
    field = pltpu.VMEM(flat, F32)
    face = (size, LANES)
    outs = pl.pallas_call(
        functools.partial(kernel, n_gx, n_gy, size),
        out_shape=[jax.ShapeDtypeStruct(flat, F32)] * 2,
        in_specs=[hbm] * 7,
        out_specs=[vmem, vmem],
        scratch_shapes=[
            pltpu.SMEM(sweep_counts.shape, jnp.int32),
            pltpu.VMEM(refine_flags.shape, jnp.int32),
            pltpu.VMEM(coarse_inverse.shape, F32),
            pltpu.VMEM(table.shape, table.dtype),
            pltpu.VMEM(mu.shape, F32),
            field, field, field,
            pltpu.VMEM((2 * size * size, LANES), F32),
            pltpu.VMEM((2 * (size + 2) * (size + ROWS), LANES), F32),
            field, field, field, field,
            pltpu.VMEM((size * (size + 1), LANES), F32),
            pltpu.VMEM((size * (size + 1), LANES), F32),
            pltpu.VMEM((COLUMNS * size, LANES), F32),
            field, field, field, field,
            pltpu.VMEM((2,) + face, F32),
            pltpu.VMEM((ITERS, 2) + face, F32),
            pltpu.VMEM((ITERS, 2) + face, F32),
            pltpu.VMEM((GATHERS, n_gy, ROWS, LANES), F32),
            pltpu.VMEM((GATHERS, LANES // ROWS, ROWS, LANES), F32),
            pltpu.VMEM((3, LANES, LANES), F32),
            pltpu.SemaphoreType.DMA((7,)),
            pltpu.SemaphoreType.DMA((ITERS, 4)),
            pltpu.SemaphoreType.DMA((ITERS, 4)),
            pltpu.SemaphoreType.DMA((GATHERS, n_gy)),
            pltpu.SemaphoreType.DMA((GATHERS, n_gy)),
            pltpu.SemaphoreType.DMA((GATHERS, n_gx)),
            pltpu.SemaphoreType.DMA((GATHERS, n_gx)),
        ],
        compiler_params=pltpu.CompilerParams(
            collective_id=0, has_side_effects=True, vmem_limit_bytes=48 * 1024 * 1024
        ),
        cost_estimate=pl.CostEstimate(flops=4 * 10**9, bytes_accessed=8 * 2**20, transcendentals=0),
        name="pressure_solve",
    )(
        *(pltpu.with_memory_space_constraint(operand, pltpu.HBM) for operand in operands)
    )
    return tuple(out.reshape(right_side.shape) for out in outs)


def solution(mesh):
    return jax.shard_map(
        functools.partial(shards, mesh.shape["gx"], mesh.shape["gy"]),
        mesh=mesh,
        in_specs=(P("gx", "gy", None), P("gx", "gy", None), P(), P(), P(("gx", "gy"), None)),
        out_specs=(P("gx", "gy", None), P("gx", "gy", None)),
        check_vma=False,
    )
```

```python
import functools

import jax
import jax.numpy as jnp
import ml_dtypes
import numpy as np
from jax import lax
from jax.experimental import pallas as pl
from jax.experimental.pallas import tpu as pltpu
from jax.sharding import PartitionSpec as P

ITERS = 4
MOST = 12
LANES = 128
ROWS = 8
GATHERS = ITERS + 2
SUM_LANE = 3
LINES = 4
COLUMNS = 8
PLANES = 16
APPLIES = 8
UPDATES = 8
F32 = jnp.float32
MESH = pl.DeviceIdType.MESH


def sine_table(count):
    index = np.arange(count, dtype=np.float64)
    angle = np.pi * (index[:, None] + 1.0) * (index[None, :] + 1.0) / (count + 1.0)
    return np.sqrt(2.0 / (count + 1.0)) * np.sin(angle)


def eigen_values(count):
    index = np.arange(count, dtype=np.float64)
    return 2.0 - 2.0 * np.cos(np.pi * (index + 1.0) / (count + 1.0))


def split_table(count):
    table = sine_table(count).astype(np.float32)
    high = table.astype(ml_dtypes.bfloat16)
    low = (table - high.astype(np.float32)).astype(ml_dtypes.bfloat16)
    return np.concatenate([high, high, low, low], axis=1)


def transform(table, field):
    high = field.astype(jnp.bfloat16)
    low = (field - high.astype(F32)).astype(jnp.bfloat16)
    stacked = jnp.concatenate([high, low, high, low], axis=0)
    return jnp.dot(table, stacked, preferred_element_type=F32)


def fold(value):
    return jnp.sum(value.reshape(-1, ROWS, LANES), axis=0)


def kernel(
    n_gx, n_gy, inner, size,
    rhs_hbm, diag_hbm, count_hbm, flag_hbm, coarse_hbm, table_hbm, mu_hbm,
    x_ref, r_ref,
    count_ref, flag_ref, coarse_ref, table_ref, mu_ref,
    diag_ref, p_ref, s_ref, image_ref, back_ref, hat_ref, hat_s_ref, hat_r_ref, line_ref, step_ref, mode_ref,
    twice_ref, root_ref, near_ref, far_ref, mid_ref,
    edge_ref, ghost_x, ghost_y, small_ref, all_ref, known_ref,
    in_sem, halo_send, halo_recv, row_send, row_recv, col_send, col_recv, far_send, far_recv,
):
    gx = lax.axis_index("gx")
    gy = lax.axis_index("gy")
    mine = gx * n_gy + gy
    pitch = size + ROWS
    odd_pitch = size + 1
    plain = size * size
    roomy = (size + 2) * pitch
    row8 = lax.broadcasted_iota(jnp.int32, (ROWS, LANES), 0)
    lane8 = lax.broadcasted_iota(jnp.int32, (ROWS, LANES), 1)
    lane = lax.broadcasted_iota(jnp.int32, (size, LANES), 1)
    slim = lax.broadcasted_iota(jnp.int32, (1, LANES), 1)

    def plane(index):
        return pl.ds(pl.multiple_of(index * size, ROWS), size)

    def rows(base, index):
        return pl.ds(base + index * size, size)

    def image_base(parity, first):
        return pl.multiple_of(parity * plain + first * size, ROWS)

    def back_base(parity, first):
        return pl.multiple_of(parity * roomy + (first + 1) * pitch, ROWS)

    pairs = (
        (rhs_hbm, r_ref), (flag_hbm, flag_ref), (mu_hbm, mu_ref), (coarse_hbm, coarse_ref), (count_hbm, count_ref),
        (table_hbm, table_ref), (diag_hbm, diag_ref),
    )
    loads = [pltpu.make_async_copy(source, target, in_sem.at[n]) for n, (source, target) in enumerate(pairs)]
    for load in loads:
        load.start()
    if n_gx * ROWS < LANES:
        all_ref[...] = jnp.zeros_like(all_ref)

    barrier = pltpu.get_barrier_semaphore()

    def over(first, last, act):
        def body(step, carry):
            act(step)
            return carry

        lax.fori_loop(first, last, body, 0)

    def beside_row(step):
        return gx, lax.rem(gy + step, n_gy)

    def beside_col(step):
        return lax.rem(gx + step, n_gx), gy

    def greet(device):
        pl.semaphore_signal(barrier, inc=1, device_id=device, device_id_type=MESH)

    over(1, n_gy, lambda step: greet(beside_row(step)))
    over(1, n_gx, lambda step: greet(beside_col(step)))

    near_gx = lax.rem(gx, inner)
    first_gx = gx - near_gx

    def row_copy(slot, step):
        return pltpu.make_async_remote_copy(
            src_ref=small_ref.at[slot, gy], dst_ref=small_ref.at[slot, gy],
            send_sem=row_send.at[slot, step], recv_sem=row_recv.at[slot, step],
            device_id=beside_row(step), device_id_type=MESH,
        )

    def col_copy(slot, step):
        return pltpu.make_async_remote_copy(
            src_ref=all_ref.at[slot, gx], dst_ref=all_ref.at[slot, gx],
            send_sem=col_send.at[slot, step], recv_sem=col_recv.at[slot, step],
            device_id=(first_gx + lax.rem(near_gx + step, inner), gy), device_id_type=MESH,
        )

    def far_copy(slot, step):
        block = all_ref.at[slot, pl.ds(first_gx, inner)]
        return pltpu.make_async_remote_copy(
            src_ref=block, dst_ref=block,
            send_sem=far_send.at[slot, step], recv_sem=far_recv.at[slot, step],
            device_id=beside_col(step * inner), device_id_type=MESH,
        )

    row_steps = range(1, n_gy)
    col_steps = range(1, inner)
    far_steps = range(1, n_gx // inner)

    def gather_start(slot, payload):
        small_ref[slot, gy] = jnp.where(row8 == gy, payload, 0.0)
        for step in row_steps:
            row_copy(slot, step).start()

    def gather_middle(slot):
        for step in row_steps:
            row_copy(slot, step).wait_recv()
        total = small_ref[slot, 0]
        for other in range(1, n_gy):
            total = total + small_ref[slot, other]
        all_ref[slot, gx] = total
        for step in col_steps:
            col_copy(slot, step).start()

    def gather_far(slot):
        for step in col_steps:
            col_copy(slot, step).wait_recv()
        for step in far_steps:
            far_copy(slot, step).start()

    def gather_end(slot):
        for step in far_steps:
            far_copy(slot, step).wait_recv()
        return all_ref[slot].reshape(LANES, LANES)

    def gather_drain(slot):
        for step in row_steps:
            row_copy(slot, step).wait_send()
        for step in col_steps:
            col_copy(slot, step).wait_send()
        for step in far_steps:
            far_copy(slot, step).wait_send()

    def lane_pick(row, which):
        total = jnp.sum(jnp.where(slim == which, row, 0.0), axis=1, keepdims=True)
        return jnp.broadcast_to(total, (ROWS, LANES))

    loads[0].wait()

    def add_up(t, total):
        base = pl.multiple_of(t * (8 * size), ROWS)
        for m in range(8):
            total = total + fold(r_ref[rows(base, m), :])
        return total

    total = lax.fori_loop(0, size // 8, add_up, jnp.zeros((ROWS, LANES), F32))
    total = jnp.sum(jnp.sum(total, axis=0, keepdims=True), axis=1, keepdims=True)
    for load in loads[1:6]:
        load.wait()
    pl.semaphore_wait(barrier, n_gx + n_gy - 2)
    gather_start(ITERS, coarse_ref[...])
    gather_start(ITERS + 1, jnp.where(slim == SUM_LANE, total, 0.0))

    shift = 2.5 * flag_ref[pl.ds(mine, 1), :].astype(F32) + 2.5

    def coefficients(b):
        d = mu_ref[...] + mu_ref[pl.ds(b, 1), :] + shift
        root = lax.rsqrt(d)
        root = root * (1.5 - 0.5 * d * root * root)
        near = jnp.where(lane == 0, 0.0, root * pltpu.roll(root, 1, 1))
        square = near * near
        root_ref[plane(b), :] = root
        near_ref[plane(b), :] = near
        far_ref[plane(b), :] = near * pltpu.roll(near, 1, 1)
        mid_ref[plane(b), :] = square + pltpu.roll(square, LANES - 1, 1)

    def wipe(t, carry):
        here = pl.ds(pl.multiple_of(t * (4 * size), ROWS), 4 * size)
        for field in (p_ref, s_ref, x_ref, hat_s_ref, hat_r_ref):
            field[here, :] = jnp.zeros((4 * size, LANES), F32)
        return carry

    lax.fori_loop(0, size // 4, wipe, 0)

    for parity in range(2):
        back_ref[pl.ds(parity * roomy, pitch), :] = jnp.zeros((pitch, LANES), F32)
        back_ref[pl.ds(parity * roomy + (size + 1) * pitch, pitch), :] = jnp.zeros((pitch, LANES), F32)

    def clear(index, carry):
        for parity in range(2):
            start = pl.multiple_of(parity * roomy + (index + 1) * pitch + size, ROWS)
            back_ref[pl.ds(start, ROWS), :] = jnp.zeros((ROWS, LANES), F32)
        return carry

    lax.fori_loop(0, size, clear, 0)

    count = jnp.full((ROWS, LANES), count_ref[mine], jnp.int32)
    count = jnp.concatenate([count] * (size // ROWS), axis=0)
    odd = count % 2 == 1
    active = [count > 2 * step for step in range(MOST // 2)]

    def transform_all(parts):
        table = table_ref[...]
        done = []
        for n in range(0, len(parts), 2):
            both = transform(table, jnp.concatenate(parts[n:n + 2], axis=1))
            done += [both[:, :LANES], both[:, LANES:]]
        return done

    def odd_base(first):
        return pl.multiple_of(first * odd_pitch, ROWS)

    def forward_y(source, parity, also=None):
        def body(t):
            base = image_base(parity, t * PLANES)
            target = odd_base(t * PLANES)
            parts = [source[rows(base, m), :] for m in range(PLANES)]
            for m, part in enumerate(transform_all(parts)):
                step_ref[pl.ds(target + m * odd_pitch, size), :] = part
            if also is not None:
                for m in range(PLANES):
                    also(t * PLANES + m)

        over(0, size // PLANES, body)

    def forward_x(t):
        first = t * COLUMNS
        base = pl.multiple_of(first * size, ROWS)
        parts = [step_ref[pl.ds(first + m, size, stride=odd_pitch), :] for m in range(COLUMNS)]
        for m, part in enumerate(transform_all(parts)):
            hat_ref[rows(base, m), :] = part

    def lines_sweep(base, shift, alpha, beta, sums):
        sums = list(sums)
        for part in range(0, COLUMNS, LINES):
            here = [rows(base, m + part + shift) for m in range(LINES)]
            kept = [pl.ds((part + m) * size, size) for m in range(LINES)]
            guess = []
            for m in range(LINES):
                hat_s = hat_ref[here[m], :] + beta * hat_s_ref[here[m], :]
                hat_r = hat_r_ref[here[m], :] - alpha * hat_s
                hat_s_ref[here[m], :] = hat_s
                hat_r_ref[here[m], :] = hat_r
                near = near_ref[here[m], :]
                start = hat_r * root_ref[here[m], :]
                twice = start + near * pltpu.roll(start, 1, 1) + pltpu.roll(near * start, LANES - 1, 1)
                twice_ref[kept[m], :] = twice
                guess.append(jnp.where(odd, start, twice))
            for step in range(1, MOST // 2):
                for m in range(LINES):
                    far = far_ref[here[m], :]
                    fresh = (twice_ref[kept[m], :] + mid_ref[here[m], :] * guess[m]) + (
                        far * pltpu.roll(guess[m], 2, 1) + pltpu.roll(far * guess[m], LANES - 2, 1)
                    )
                    guess[m] = jnp.where(active[step], fresh, guess[m])
            for m in range(LINES):
                line = guess[m] * root_ref[here[m], :]
                line_ref[here[m], :] = line
                sums[0] = sums[0] + fold(line * hat_r_ref[here[m], :])
                sums[1] = sums[1] + fold(line * hat_s_ref[here[m], :])
        return tuple(sums)

    def lines_out(base, shift, target):
        parts = [line_ref[rows(base, m + shift), :] for m in range(COLUMNS)]
        for m, part in enumerate(transform_all(parts)):
            mode_ref[pl.ds(target + m * odd_pitch, size), :] = part

    def solve_lines(alpha, beta):
        alpha = jnp.broadcast_to(alpha[:1], (size, LANES))
        beta = jnp.broadcast_to(beta[:1], (size, LANES))

        def body(t, sums):
            base = pl.multiple_of(t * (COLUMNS * size), ROWS)
            lines_out(base, -COLUMNS, odd_base((t - 1) * COLUMNS))
            return lines_sweep(base, 0, alpha, beta, sums)

        zeros = (jnp.zeros((ROWS, LANES), F32),) * 2
        sums = lines_sweep(0, 0, alpha, beta, zeros)
        sums = lax.fori_loop(1, size // COLUMNS, body, sums)
        lines_out(plain, -COLUMNS, (size - COLUMNS) * odd_pitch)
        return sums

    def backward(parity, first, own):
        parts = [mode_ref[pl.ds(first + m, size, stride=odd_pitch), :] for m in range(PLANES)]
        base = back_base(parity, first)
        for m, part in enumerate(transform_all(parts)):
            part = part + own
            back_ref[pl.ds(base + m * pitch, size), :] = part
            edge_ref[0, pl.ds(first + m, 1), :] = part[:1]
            edge_ref[1, pl.ds(first + m, 1), :] = part[size - 1:]

    def halo_copy(turn, side):
        if side < 2:
            device = beside_col(1 if side == 0 else n_gx - 1)
            source = back_ref.at[pl.ds(back_base(turn % 2, size - 1 if side == 0 else 0), size)]
            target = ghost_x.at[turn, side]
        else:
            device = beside_row(1 if side == 2 else n_gy - 1)
            source = edge_ref.at[1 if side == 2 else 0]
            target = ghost_y.at[turn, side - 2]
        return pltpu.make_async_remote_copy(
            src_ref=source, dst_ref=target,
            send_sem=halo_send.at[turn, side], recv_sem=halo_recv.at[turn, side],
            device_id=device, device_id_type=MESH,
        )

    inside = [gx > 0, gx < n_gx - 1, gy > 0, gy < n_gy - 1]

    def ghosts(turn):
        raw = [ghost_x[turn, 0], ghost_x[turn, 1], ghost_y[turn, 0], ghost_y[turn, 1]]
        return [jnp.where(inside[n], raw[n], 0.0) for n in range(4)]

    def apply(parity, i, sums):
        start = back_base(parity, i)
        here = back_ref[pl.ds(start, size), :]
        beside = back_ref[pl.ds(start - pitch, size), :] + back_ref[pl.ds(start + pitch, size), :]
        beside = beside + back_ref[pl.ds(start - 1, size), :] + back_ref[pl.ds(start + 1, size), :]
        below = jnp.where(lane == 0, 0.0, pltpu.roll(here, 1, 1))
        above = jnp.where(lane == LANES - 1, 0.0, pltpu.roll(here, LANES - 1, 1))
        image = (6.0 + diag_ref[plane(i), :]) * here - (beside + (below + above))
        image_ref[pl.ds(image_base(parity, i), size), :] = image
        return sums[0] + fold(here * image), sums[1] + fold(image)

    def update(parity, alpha, beta):
        alpha = jnp.broadcast_to(alpha[:1], (size, LANES))
        beta = jnp.broadcast_to(beta[:1], (size, LANES))

        def body(t):
            base = pl.multiple_of(t * (UPDATES * size), ROWS)
            image = image_base(parity, t * UPDATES)
            back = back_base(parity, t * UPDATES)
            for m in range(UPDATES):
                here = rows(base, m)
                moved = image_ref[rows(image, m), :] + beta * s_ref[here, :]
                direction = back_ref[pl.ds(back + m * pitch, size), :] + beta * p_ref[here, :]
                s_ref[here, :] = moved
                p_ref[here, :] = direction
                x_ref[here, :] = x_ref[here, :] + alpha * direction
                r_ref[here, :] = r_ref[here, :] - alpha * moved

        return body

    gather_middle(ITERS)
    gather_middle(ITERS + 1)
    forward_y(r_ref, 0, coefficients)
    gather_far(ITERS)
    gather_far(ITERS + 1)
    over(0, size // COLUMNS, forward_x)
    loads[6].wait()
    gather_end(ITERS)
    sums = gather_end(ITERS + 1)

    def spread(matrix):
        return jnp.broadcast_to(matrix[:, SUM_LANE:SUM_LANE + 1], (LANES, LANES))

    def coarse_solve():
        known_ref[2] = jnp.dot(
            all_ref[ITERS].reshape(LANES, LANES), known_ref[0],
            precision=lax.Precision.HIGHEST, preferred_element_type=F32,
        )

    known_ref[0] = spread(sums)
    known_ref[1] = jnp.zeros((LANES, LANES), F32)
    coarse_solve()
    gather_drain(ITERS)
    gather_drain(ITERS + 1)

    def iterate(turn, scalars):
        gamma, energy, alpha, beta = scalars
        parity = turn % 2
        own = known_ref[2, pl.ds(mine, 1), :]
        extra = jnp.where(row8 == 0, own * known_ref[0, pl.ds(mine, 1), :], 0.0)
        extra = jnp.where(row8 == 2, own * known_ref[1, pl.ds(mine, 1), :], extra)
        mode_sums = solve_lines(alpha, beta)

        def ends(t, carry):
            backward(parity, t * (size - PLANES), own)
            return carry

        def others(t, carry):
            backward(parity, t * PLANES, own)
            return carry

        lax.fori_loop(0, 2, ends, 0)
        halos = [halo_copy(turn, side) for side in range(4)]
        halos[0].start()
        halos[1].start()
        lax.fori_loop(1, size // PLANES - 1, others, 0)
        halos[2].start()
        halos[3].start()

        def apply_some(t, sums):
            for m in range(APPLIES):
                sums = apply(parity, APPLIES * t + m, sums)
            return sums

        zeros = (jnp.zeros((ROWS, LANES), F32),) * 2
        curve, flow = lax.fori_loop(0, size // APPLIES, apply_some, zeros)
        for halo in halos:
            halo.wait_recv()
        ghost = ghosts(turn)
        low = pl.ds(back_base(parity, 0), size)
        high = pl.ds(back_base(parity, size - 1), size)
        faces = [back_ref[low, :], back_ref[high, :], edge_ref[0], edge_ref[1]]
        for n in range(4):
            curve = curve - fold(faces[n] * ghost[n])
            flow = flow - fold(ghost[n])
        stacked = jnp.zeros((ROWS, LANES), F32)
        for n, total in enumerate((mode_sums[0], curve, mode_sums[1], flow)):
            stacked = jnp.where(row8 == n, jnp.sum(total, axis=0, keepdims=True), stacked)
        stacked = jnp.sum(stacked, axis=1, keepdims=True) + extra
        payload = jnp.sum(jnp.where(row8 == lane8, stacked, 0.0), axis=0, keepdims=True)
        gather_start(turn, payload)

        base = image_base(parity, 0)
        spots = [
            pl.ds(base, size), pl.ds(base + (size - 1) * size, size),
            pl.ds(base, size, stride=size), pl.ds(base + size - 1, size, stride=size),
        ]
        for n in range(4):
            image_ref[spots[n], :] = image_ref[spots[n], :] - ghost[n]

        @pl.when(turn < ITERS - 1)
        def _():
            forward_y(image_ref, parity)

        gather_middle(turn)

        @pl.when(turn < ITERS - 1)
        def _():
            over(0, size // COLUMNS, forward_x)

        gather_far(turn)

        @pl.when(turn > 0)
        def _():
            over(0, size // UPDATES, update(1 - parity, alpha, beta))

        for halo in halos:
            halo.wait_send()
        every = gather_end(turn)
        totals = jnp.sum(every, axis=0, keepdims=True)
        fresh = lane_pick(totals, 0)
        beta = jnp.where(turn == 0, 0.0, fresh / gamma)
        energy = lane_pick(totals, 1) + beta * (2.0 * lane_pick(totals, 2) + beta * energy)
        alpha = fresh / energy
        known_ref[1] = spread(every) + beta[:1] * known_ref[1]
        known_ref[0] = known_ref[0] - alpha[:1] * known_ref[1]
        coarse_solve()
        gather_drain(turn)
        return fresh, energy, alpha, beta

    one = jnp.ones((ROWS, LANES), F32)
    zero = jnp.zeros((ROWS, LANES), F32)
    gamma, energy, alpha, beta = lax.fori_loop(0, ITERS, iterate, (one, zero, -one, zero))
    over(0, size // UPDATES, update((ITERS - 1) % 2, alpha, beta))


def shards(n_gx, n_gy, right_side, diagonal, sweep_counts, refine_flags, coarse_inverse):
    size, _, cells = right_side.shape
    flat = (size * size, cells)
    table = jnp.asarray(split_table(size))
    mu = jnp.asarray(np.repeat(eigen_values(size).astype(np.float32)[:, None], cells, axis=1))
    subs = n_gx * n_gy
    inner = 4 if n_gx % 4 == 0 and n_gx > 4 else 2
    if coarse_inverse.shape[1] < LANES:
        coarse_inverse = jnp.pad(coarse_inverse, ((0, 0), (0, LANES - subs)))
    operands = (
        right_side.reshape(flat), diagonal.reshape(flat), sweep_counts, refine_flags, coarse_inverse, table, mu
    )
    vmem = pl.BlockSpec(memory_space=pltpu.VMEM)
    hbm = pl.BlockSpec(memory_space=pltpu.HBM)
    field = pltpu.VMEM(flat, F32)
    face = (size, LANES)
    outs = pl.pallas_call(
        functools.partial(kernel, n_gx, n_gy, inner, size),
        out_shape=[jax.ShapeDtypeStruct(flat, F32)] * 2,
        in_specs=[hbm] * 7,
        out_specs=[vmem, vmem],
        scratch_shapes=[
            pltpu.SMEM(sweep_counts.shape, jnp.int32),
            pltpu.VMEM(refine_flags.shape, jnp.int32),
            pltpu.VMEM(coarse_inverse.shape, F32),
            pltpu.VMEM(table.shape, table.dtype),
            pltpu.VMEM(mu.shape, F32),
            field, field, field,
            pltpu.VMEM((2 * size * size, LANES), F32),
            pltpu.VMEM((2 * (size + 2) * (size + ROWS), LANES), F32),
            field, field, field, field,
            pltpu.VMEM((size * (size + 1), LANES), F32),
            pltpu.VMEM((size * (size + 1), LANES), F32),
            pltpu.VMEM((COLUMNS * size, LANES), F32),
            field, field, field, field,
            pltpu.VMEM((2,) + face, F32),
            pltpu.VMEM((ITERS, 2) + face, F32),
            pltpu.VMEM((ITERS, 2) + face, F32),
            pltpu.VMEM((GATHERS, n_gy, ROWS, LANES), F32),
            pltpu.VMEM((GATHERS, LANES // ROWS, ROWS, LANES), F32),
            pltpu.VMEM((3, LANES, LANES), F32),
            pltpu.SemaphoreType.DMA((7,)),
            pltpu.SemaphoreType.DMA((ITERS, 4)),
            pltpu.SemaphoreType.DMA((ITERS, 4)),
            pltpu.SemaphoreType.DMA((GATHERS, n_gy)),
            pltpu.SemaphoreType.DMA((GATHERS, n_gy)),
            pltpu.SemaphoreType.DMA((GATHERS, inner)),
            pltpu.SemaphoreType.DMA((GATHERS, inner)),
            pltpu.SemaphoreType.DMA((GATHERS, n_gx // inner)),
            pltpu.SemaphoreType.DMA((GATHERS, n_gx // inner)),
        ],
        compiler_params=pltpu.CompilerParams(
            collective_id=0, has_side_effects=True, vmem_limit_bytes=48 * 1024 * 1024
        ),
        cost_estimate=pl.CostEstimate(flops=4 * 10**9, bytes_accessed=8 * 2**20, transcendentals=0),
        name="pressure_solve",
    )(
        *(pltpu.with_memory_space_constraint(operand, pltpu.HBM) for operand in operands)
    )
    return tuple(out.reshape(right_side.shape) for out in outs)


def solution(mesh):
    return jax.shard_map(
        functools.partial(shards, mesh.shape["gx"], mesh.shape["gy"]),
        mesh=mesh,
        in_specs=(P("gx", "gy", None), P("gx", "gy", None), P(), P(), P(("gx", "gy"), None)),
        out_specs=(P("gx", "gy", None), P("gx", "gy", None)),
        check_vma=False,
    )
```

```python
import functools

import jax
import jax.numpy as jnp
import ml_dtypes
import numpy as np
from jax import lax
from jax.experimental import pallas as pl
from jax.experimental.pallas import tpu as pltpu
from jax.sharding import PartitionSpec as P

ITERS = 4
MOST = 12
LANES = 128
ROWS = 8
GATHERS = ITERS + 2
SUM_LANE = 3
PAIRS = 2
COLUMNS = 8
PLANES = 16
APPLIES = 8
UPDATES = 8
F32 = jnp.float32
MESH = pl.DeviceIdType.MESH


def sine_table(count):
    index = np.arange(count, dtype=np.float64)
    angle = np.pi * (index[:, None] + 1.0) * (index[None, :] + 1.0) / (count + 1.0)
    return np.sqrt(2.0 / (count + 1.0)) * np.sin(angle)


def eigen_values(count):
    index = np.arange(count, dtype=np.float64)
    return 2.0 - 2.0 * np.cos(np.pi * (index + 1.0) / (count + 1.0))


def split_table(count):
    table = sine_table(count).astype(np.float32)
    high = table.astype(ml_dtypes.bfloat16)
    low = (table - high.astype(np.float32)).astype(ml_dtypes.bfloat16)
    return np.concatenate([np.concatenate([high, high], axis=1), np.concatenate([low, low], axis=1)], axis=0)


def transform(table, field):
    high = field.astype(jnp.bfloat16)
    low = (field - high.astype(F32)).astype(jnp.bfloat16)
    stacked = jnp.concatenate([high, low], axis=0)
    both = jnp.dot(table, stacked, preferred_element_type=F32)
    return both[:field.shape[0]] + both[field.shape[0]:]


def fold(value):
    return jnp.sum(value.reshape(-1, ROWS, LANES), axis=0)


def kernel(
    n_gx, n_gy, size,
    rhs_hbm, diag_hbm, count_hbm, flag_hbm, coarse_hbm, table_hbm, mu_hbm,
    x_ref, r_ref,
    count_ref, flag_ref, coarse_ref, table_ref, mu_ref,
    diag_ref, p_ref, s_ref, image_ref, back_ref, hat_ref, hat_s_ref, hat_r_ref, line_ref, step_ref, mode_ref,
    twice_ref, guess_ref, root_ref, near_ref, far_ref, mid_ref,
    edge_ref, ghost_x, ghost_y, small_ref, all_ref, known_ref,
    in_sem, halo_send, halo_recv, row_send, row_recv, col_send, col_recv,
):
    gx = lax.axis_index("gx")
    gy = lax.axis_index("gy")
    mine = gx * n_gy + gy
    pitch = size + ROWS
    odd_pitch = size + 1
    plain = size * size
    roomy = (size + 2) * pitch
    row8 = lax.broadcasted_iota(jnp.int32, (ROWS, LANES), 0)
    lane8 = lax.broadcasted_iota(jnp.int32, (ROWS, LANES), 1)
    lane = lax.broadcasted_iota(jnp.int32, (size, LANES), 1)
    slim = lax.broadcasted_iota(jnp.int32, (1, LANES), 1)

    def plane(index):
        return pl.ds(pl.multiple_of(index * size, ROWS), size)

    def rows(base, index):
        return pl.ds(base + index * size, size)

    def image_base(parity, first):
        return pl.multiple_of(parity * plain + first * size, ROWS)

    def back_base(parity, first):
        return pl.multiple_of(parity * roomy + (first + 1) * pitch, ROWS)

    pairs = (
        (rhs_hbm, r_ref), (flag_hbm, flag_ref), (mu_hbm, mu_ref), (coarse_hbm, coarse_ref), (count_hbm, count_ref),
        (table_hbm, table_ref), (diag_hbm, diag_ref),
    )
    loads = [pltpu.make_async_copy(source, target, in_sem.at[n]) for n, (source, target) in enumerate(pairs)]
    for load in loads:
        load.start()
    if n_gx * ROWS < LANES:
        all_ref[...] = jnp.zeros_like(all_ref)

    barrier = pltpu.get_barrier_semaphore()

    def over(first, last, act):
        def body(step, carry):
            act(step)
            return carry

        lax.fori_loop(first, last, body, 0)

    def beside_row(step):
        return gx, lax.rem(gy + step, n_gy)

    def beside_col(step):
        return lax.rem(gx + step, n_gx), gy

    def greet(device):
        pl.semaphore_signal(barrier, inc=1, device_id=device, device_id_type=MESH)

    over(1, n_gy, lambda step: greet(beside_row(step)))
    over(1, n_gx, lambda step: greet(beside_col(step)))

    def row_copy(slot, step):
        return pltpu.make_async_remote_copy(
            src_ref=small_ref.at[slot, gy], dst_ref=small_ref.at[slot, gy],
            send_sem=row_send.at[slot, step], recv_sem=row_recv.at[slot, step],
            device_id=beside_row(step), device_id_type=MESH,
        )

    def col_copy(slot, step):
        return pltpu.make_async_remote_copy(
            src_ref=all_ref.at[slot, gx], dst_ref=all_ref.at[slot, gx],
            send_sem=col_send.at[slot, step], recv_sem=col_recv.at[slot, step],
            device_id=beside_col(step), device_id_type=MESH,
        )

    def gather_start(slot, payload):
        small_ref[slot, gy] = jnp.where(row8 == gy, payload, 0.0)
        over(1, n_gy, lambda step: row_copy(slot, step).start())

    def gather_middle(slot):
        over(1, n_gy, lambda step: row_copy(slot, step).wait_recv())
        total = small_ref[slot, 0]
        for other in range(1, n_gy):
            total = total + small_ref[slot, other]
        all_ref[slot, gx] = total
        over(1, n_gx, lambda step: col_copy(slot, step).start())

    def gather_end(slot):
        over(1, n_gx, lambda step: col_copy(slot, step).wait_recv())
        return all_ref[slot].reshape(LANES, LANES)

    def gather_drain(slot):
        over(1, n_gy, lambda step: row_copy(slot, step).wait_send())
        over(1, n_gx, lambda step: col_copy(slot, step).wait_send())

    def lane_pick(row, which):
        total = jnp.sum(jnp.where(slim == which, row, 0.0), axis=1, keepdims=True)
        return jnp.broadcast_to(total, (ROWS, LANES))

    loads[0].wait()

    def add_up(t, total):
        base = pl.multiple_of(t * (8 * size), ROWS)
        for m in range(8):
            total = total + fold(r_ref[rows(base, m), :])
        return total

    total = lax.fori_loop(0, size // 8, add_up, jnp.zeros((ROWS, LANES), F32))
    total = jnp.sum(jnp.sum(total, axis=0, keepdims=True), axis=1, keepdims=True)
    for load in loads[1:6]:
        load.wait()
    pl.semaphore_wait(barrier, n_gx + n_gy - 2)
    gather_start(ITERS, coarse_ref[...])
    gather_start(ITERS + 1, jnp.where(slim == SUM_LANE, total, 0.0))

    shift = 2.5 * flag_ref[pl.ds(mine, 1), :].astype(F32) + 2.5

    height = jnp.transpose(jnp.broadcast_to(shift, (LANES, LANES)))
    two = 2 * size
    wide_lane = lax.broadcasted_iota(jnp.int32, (LANES, LANES), 1)
    wide_row = lax.broadcasted_iota(jnp.int32, (LANES, LANES), 0)

    def turned(pair, offset=0):
        return pl.ds(pl.multiple_of(pair * LANES, LANES) + offset, LANES)

    def coefficients(pair):
        columns = jnp.where(wide_lane < size, mu_ref[pl.ds(2 * pair, 1), :], mu_ref[pl.ds(2 * pair + 1, 1), :])
        d = columns + mu_ref[pl.ds(size, 1), :] + height
        root = lax.rsqrt(d)
        root = root * (1.5 - 0.5 * d * root * root)
        near = jnp.where(wide_row == 0, 0.0, root * pltpu.roll(root, 1, 0))
        square = near * near
        root_ref[turned(pair), :] = root
        near_ref[turned(pair), :] = near
        far_ref[turned(pair), :] = near * pltpu.roll(near, 1, 0)
        mid_ref[turned(pair), :] = square + pltpu.roll(square, LANES - 1, 0)

    def coefficient_some(t, carry):
        coefficients(2 * t)
        coefficients(2 * t + 1)
        return carry

    lax.fori_loop(0, size // 4, coefficient_some, 0)
    near_ref[pl.ds(plain, ROWS), :] = jnp.zeros((ROWS, LANES), F32)
    far_ref[pl.ds(plain, ROWS), :] = jnp.zeros((ROWS, LANES), F32)
    guess_ref[...] = jnp.zeros_like(guess_ref)

    def wipe(t, carry):
        here = pl.ds(pl.multiple_of(t * (4 * size), ROWS), 4 * size)
        for field in (p_ref, s_ref, x_ref, hat_s_ref, hat_r_ref):
            field[here, :] = jnp.zeros((4 * size, LANES), F32)
        return carry

    lax.fori_loop(0, size // 4, wipe, 0)

    for parity in range(2):
        back_ref[pl.ds(parity * roomy, pitch), :] = jnp.zeros((pitch, LANES), F32)
        back_ref[pl.ds(parity * roomy + (size + 1) * pitch, pitch), :] = jnp.zeros((pitch, LANES), F32)

    def clear(index, carry):
        for parity in range(2):
            start = pl.multiple_of(parity * roomy + (index + 1) * pitch + size, ROWS)
            back_ref[pl.ds(start, ROWS), :] = jnp.zeros((ROWS, LANES), F32)
        return carry

    lax.fori_loop(0, size, clear, 0)
    gather_middle(ITERS)
    gather_middle(ITERS + 1)

    count = jnp.full((ROWS, LANES), count_ref[mine], jnp.int32)
    count = jnp.concatenate([count] * (LANES // ROWS), axis=0)
    odd = count % 2 == 1
    active = [count > 2 * step for step in range(MOST // 2)]

    def transform_all(parts):
        table = table_ref[...]
        done = []
        for n in range(0, len(parts), 2):
            both = transform(table, jnp.concatenate(parts[n:n + 2], axis=1))
            done += [both[:, :LANES], both[:, LANES:]]
        return done

    def odd_base(first):
        return pl.multiple_of(first * odd_pitch, ROWS)

    def forward_y(source, parity):
        def body(t, carry):
            base = image_base(parity, t * PLANES)
            target = odd_base(t * PLANES)
            parts = [source[rows(base, m), :] for m in range(PLANES)]
            for m, part in enumerate(transform_all(parts)):
                step_ref[pl.ds(target + m * odd_pitch, size), :] = part
            return carry

        lax.fori_loop(0, size // PLANES, body, 0)

    def forward_x():
        def body(t, carry):
            first = t * COLUMNS
            base = pl.multiple_of(first * size, ROWS)
            parts = [step_ref[pl.ds(first + m, size, stride=odd_pitch), :] for m in range(COLUMNS)]
            for m, part in enumerate(transform_all(parts)):
                hat_ref[rows(base, m), :] = part
            return carry

        lax.fori_loop(0, size // COLUMNS, body, 0)

    turn_over = jnp.transpose

    def lines_sweep(base, shift, alpha, beta, sums):
        first = base
        sums = list(sums)
        for part in range(0, COLUMNS // 2, PAIRS):
            pairs = range(part, part + PAIRS)
            here = [pl.ds(base + n * two + shift * size, two) for n in pairs]
            after = [[pl.ds(first + n * LANES + far, LANES) for far in range(3)] for n in pairs]
            held = [n * (LANES + 2 * ROWS) + ROWS for n in pairs]
            kept = [pl.ds(n * LANES, LANES) for n in pairs]
            guess = []
            for n in range(PAIRS):
                hat_s = hat_ref[here[n], :] + beta * hat_s_ref[here[n], :]
                hat_r = hat_r_ref[here[n], :] - alpha * hat_s
                hat_s_ref[here[n], :] = hat_s
                hat_r_ref[here[n], :] = hat_r
                start = turn_over(hat_r) * root_ref[after[n][0], :]
                guess_ref[pl.ds(held[n], LANES), :] = start
                low = guess_ref[pl.ds(held[n] - 1, LANES), :]
                high = guess_ref[pl.ds(held[n] + 1, LANES), :]
                twice = start + near_ref[after[n][0], :] * low + near_ref[after[n][1], :] * high
                twice_ref[kept[n], :] = twice
                guess.append(jnp.where(odd, start, twice))
            for step in range(1, MOST // 2):
                for n in range(PAIRS):
                    guess_ref[pl.ds(held[n], LANES), :] = guess[n]
                    low = guess_ref[pl.ds(held[n] - 2, LANES), :]
                    high = guess_ref[pl.ds(held[n] + 2, LANES), :]
                    fresh = (twice_ref[kept[n], :] + mid_ref[after[n][0], :] * guess[n]) + (
                        far_ref[after[n][0], :] * low + far_ref[after[n][2], :] * high
                    )
                    guess[n] = jnp.where(active[step], fresh, guess[n])
            for n in range(PAIRS):
                line = turn_over(guess[n] * root_ref[after[n][0], :])
                line_ref[here[n], :] = line
                sums[0] = sums[0] + fold(line * hat_r_ref[here[n], :])
                sums[1] = sums[1] + fold(line * hat_s_ref[here[n], :])
        return tuple(sums)

    def lines_out(base, shift, target):
        parts = [line_ref[rows(base, m + shift), :] for m in range(COLUMNS)]
        for m, part in enumerate(transform_all(parts)):
            mode_ref[pl.ds(target + m * odd_pitch, size), :] = part

    def solve_lines(alpha, beta):
        alpha = jnp.broadcast_to(alpha[:1], (two, LANES))
        beta = jnp.broadcast_to(beta[:1], (two, LANES))

        def body(t, sums):
            base = pl.multiple_of(t * (COLUMNS * size), ROWS)
            lines_out(base, -COLUMNS, odd_base((t - 1) * COLUMNS))
            return lines_sweep(base, 0, alpha, beta, sums)

        zeros = (jnp.zeros((ROWS, LANES), F32),) * 2
        sums = lines_sweep(0, 0, alpha, beta, zeros)
        sums = lax.fori_loop(1, size // COLUMNS, body, sums)
        lines_out(plain, -COLUMNS, (size - COLUMNS) * odd_pitch)
        return sums

    def backward(parity, first, own):
        parts = [mode_ref[pl.ds(first + m, size, stride=odd_pitch), :] for m in range(PLANES)]
        base = back_base(parity, first)
        for m, part in enumerate(transform_all(parts)):
            part = part + own
            back_ref[pl.ds(base + m * pitch, size), :] = part
            edge_ref[0, pl.ds(first + m, 1), :] = part[:1]
            edge_ref[1, pl.ds(first + m, 1), :] = part[size - 1:]

    def halo_copy(turn, side):
        if side < 2:
            device = beside_col(1 if side == 0 else n_gx - 1)
            source = back_ref.at[pl.ds(back_base(turn % 2, size - 1 if side == 0 else 0), size)]
            target = ghost_x.at[turn, side]
        else:
            device = beside_row(1 if side == 2 else n_gy - 1)
            source = edge_ref.at[1 if side == 2 else 0]
            target = ghost_y.at[turn, side - 2]
        return pltpu.make_async_remote_copy(
            src_ref=source, dst_ref=target,
            send_sem=halo_send.at[turn, side], recv_sem=halo_recv.at[turn, side],
            device_id=device, device_id_type=MESH,
        )

    inside = [gx > 0, gx < n_gx - 1, gy > 0, gy < n_gy - 1]

    def ghosts(turn):
        raw = [ghost_x[turn, 0], ghost_x[turn, 1], ghost_y[turn, 0], ghost_y[turn, 1]]
        return [jnp.where(inside[n], raw[n], 0.0) for n in range(4)]

    def apply(parity, i, sums):
        start = back_base(parity, i)
        here = back_ref[pl.ds(start, size), :]
        beside = back_ref[pl.ds(start - pitch, size), :] + back_ref[pl.ds(start + pitch, size), :]
        beside = beside + back_ref[pl.ds(start - 1, size), :] + back_ref[pl.ds(start + 1, size), :]
        below = jnp.where(lane == 0, 0.0, pltpu.roll(here, 1, 1))
        above = jnp.where(lane == LANES - 1, 0.0, pltpu.roll(here, LANES - 1, 1))
        image = (6.0 + diag_ref[plane(i), :]) * here - (beside + (below + above))
        image_ref[pl.ds(image_base(parity, i), size), :] = image
        return sums[0] + fold(here * image), sums[1] + fold(image)

    def update(parity, alpha, beta):
        alpha = jnp.broadcast_to(alpha[:1], (size, LANES))
        beta = jnp.broadcast_to(beta[:1], (size, LANES))

        def body(t, carry):
            base = pl.multiple_of(t * (UPDATES * size), ROWS)
            image = image_base(parity, t * UPDATES)
            back = back_base(parity, t * UPDATES)
            for m in range(UPDATES):
                here = rows(base, m)
                moved = image_ref[rows(image, m), :] + beta * s_ref[here, :]
                direction = back_ref[pl.ds(back + m * pitch, size), :] + beta * p_ref[here, :]
                s_ref[here, :] = moved
                p_ref[here, :] = direction
                x_ref[here, :] = x_ref[here, :] + alpha * direction
                r_ref[here, :] = r_ref[here, :] - alpha * moved
            return carry

        lax.fori_loop(0, size // UPDATES, body, 0)

    forward_y(r_ref, 0)
    forward_x()
    loads[6].wait()
    gather_end(ITERS)
    sums = gather_end(ITERS + 1)

    def spread(matrix):
        return jnp.broadcast_to(matrix[:, SUM_LANE:SUM_LANE + 1], (LANES, LANES))

    def coarse_solve():
        known_ref[2] = jnp.dot(
            all_ref[ITERS].reshape(LANES, LANES), known_ref[0],
            precision=lax.Precision.HIGHEST, preferred_element_type=F32,
        )

    known_ref[0] = spread(sums)
    known_ref[1] = jnp.zeros((LANES, LANES), F32)
    coarse_solve()
    gather_drain(ITERS)
    gather_drain(ITERS + 1)

    def iterate(turn, scalars):
        gamma, energy, alpha, beta = scalars
        parity = turn % 2
        own = known_ref[2, pl.ds(mine, 1), :]
        extra = jnp.where(row8 == 0, own * known_ref[0, pl.ds(mine, 1), :], 0.0)
        extra = jnp.where(row8 == 2, own * known_ref[1, pl.ds(mine, 1), :], extra)
        mode_sums = solve_lines(alpha, beta)

        def ends(t, carry):
            backward(parity, t * (size - PLANES), own)
            return carry

        def others(t, carry):
            backward(parity, t * PLANES, own)
            return carry

        lax.fori_loop(0, 2, ends, 0)
        halos = [halo_copy(turn, side) for side in range(4)]
        halos[0].start()
        halos[1].start()
        lax.fori_loop(1, size // PLANES - 1, others, 0)
        halos[2].start()
        halos[3].start()

        def apply_some(t, sums):
            for m in range(APPLIES):
                sums = apply(parity, APPLIES * t + m, sums)
            return sums

        zeros = (jnp.zeros((ROWS, LANES), F32),) * 2
        curve, flow = lax.fori_loop(0, size // APPLIES, apply_some, zeros)
        for halo in halos:
            halo.wait_recv()
        ghost = ghosts(turn)
        low = pl.ds(back_base(parity, 0), size)
        high = pl.ds(back_base(parity, size - 1), size)
        faces = [back_ref[low, :], back_ref[high, :], edge_ref[0], edge_ref[1]]
        for n in range(4):
            curve = curve - fold(faces[n] * ghost[n])
            flow = flow - fold(ghost[n])
        stacked = jnp.zeros((ROWS, LANES), F32)
        for n, total in enumerate((mode_sums[0], curve, mode_sums[1], flow)):
            stacked = jnp.where(row8 == n, jnp.sum(total, axis=0, keepdims=True), stacked)
        stacked = jnp.sum(stacked, axis=1, keepdims=True) + extra
        payload = jnp.sum(jnp.where(row8 == lane8, stacked, 0.0), axis=0, keepdims=True)
        gather_start(turn, payload)

        base = image_base(parity, 0)
        spots = [
            pl.ds(base, size), pl.ds(base + (size - 1) * size, size),
            pl.ds(base, size, stride=size), pl.ds(base + size - 1, size, stride=size),
        ]
        for n in range(4):
            image_ref[spots[n], :] = image_ref[spots[n], :] - ghost[n]

        @pl.when(turn < ITERS - 1)
        def _():
            forward_y(image_ref, parity)

        gather_middle(turn)

        @pl.when(turn < ITERS - 1)
        def _():
            forward_x()

        @pl.when(turn > 0)
        def _():
            update(1 - parity, alpha, beta)

        for halo in halos:
            halo.wait_send()
        every = gather_end(turn)
        totals = jnp.sum(every, axis=0, keepdims=True)
        fresh = lane_pick(totals, 0)
        beta = jnp.where(turn == 0, 0.0, fresh / gamma)
        energy = lane_pick(totals, 1) + beta * (2.0 * lane_pick(totals, 2) + beta * energy)
        alpha = fresh / energy
        known_ref[1] = spread(every) + beta[:1] * known_ref[1]
        known_ref[0] = known_ref[0] - alpha[:1] * known_ref[1]
        coarse_solve()
        gather_drain(turn)
        return fresh, energy, alpha, beta

    one = jnp.ones((ROWS, LANES), F32)
    zero = jnp.zeros((ROWS, LANES), F32)
    gamma, energy, alpha, beta = lax.fori_loop(0, ITERS, iterate, (one, zero, -one, zero))
    update((ITERS - 1) % 2, alpha, beta)


def shards(n_gx, n_gy, right_side, diagonal, sweep_counts, refine_flags, coarse_inverse):
    size, _, cells = right_side.shape
    flat = (size * size, cells)
    table = jnp.asarray(split_table(size))
    mu = eigen_values(size).astype(np.float32)
    mu = np.concatenate([np.repeat(mu[:, None], cells, axis=1), np.tile(mu, (ROWS, cells // size))], axis=0)
    mu = jnp.asarray(mu)
    subs = n_gx * n_gy
    if coarse_inverse.shape[1] < LANES:
        coarse_inverse = jnp.pad(coarse_inverse, ((0, 0), (0, LANES - subs)))
    operands = (
        right_side.reshape(flat), diagonal.reshape(flat), sweep_counts, refine_flags, coarse_inverse, table, mu
    )
    vmem = pl.BlockSpec(memory_space=pltpu.VMEM)
    hbm = pl.BlockSpec(memory_space=pltpu.HBM)
    field = pltpu.VMEM(flat, F32)
    face = (size, LANES)
    outs = pl.pallas_call(
        functools.partial(kernel, n_gx, n_gy, size),
        out_shape=[jax.ShapeDtypeStruct(flat, F32)] * 2,
        in_specs=[hbm] * 7,
        out_specs=[vmem, vmem],
        scratch_shapes=[
            pltpu.SMEM(sweep_counts.shape, jnp.int32),
            pltpu.VMEM(refine_flags.shape, jnp.int32),
            pltpu.VMEM(coarse_inverse.shape, F32),
            pltpu.VMEM(table.shape, table.dtype),
            pltpu.VMEM(mu.shape, F32),
            field, field, field,
            pltpu.VMEM((2 * size * size, LANES), F32),
            pltpu.VMEM((2 * (size + 2) * (size + ROWS), LANES), F32),
            field, field, field, field,
            pltpu.VMEM((size * (size + 1), LANES), F32),
            pltpu.VMEM((size * (size + 1), LANES), F32),
            pltpu.VMEM((COLUMNS * size, LANES), F32),
            pltpu.VMEM((COLUMNS // 2 * (LANES + 2 * ROWS), LANES), F32),
            field,
            pltpu.VMEM((size * size + ROWS, LANES), F32),
            pltpu.VMEM((size * size + ROWS, LANES), F32),
            field,
            pltpu.VMEM((2,) + face, F32),
            pltpu.VMEM((ITERS, 2) + face, F32),
            pltpu.VMEM((ITERS, 2) + face, F32),
            pltpu.VMEM((GATHERS, n_gy, ROWS, LANES), F32),
            pltpu.VMEM((GATHERS, LANES // ROWS, ROWS, LANES), F32),
            pltpu.VMEM((3, LANES, LANES), F32),
            pltpu.SemaphoreType.DMA((7,)),
            pltpu.SemaphoreType.DMA((ITERS, 4)),
            pltpu.SemaphoreType.DMA((ITERS, 4)),
            pltpu.SemaphoreType.DMA((GATHERS, n_gy)),
            pltpu.SemaphoreType.DMA((GATHERS, n_gy)),
            pltpu.SemaphoreType.DMA((GATHERS, n_gx)),
            pltpu.SemaphoreType.DMA((GATHERS, n_gx)),
        ],
        compiler_params=pltpu.CompilerParams(
            collective_id=0, has_side_effects=True, vmem_limit_bytes=48 * 1024 * 1024
        ),
        cost_estimate=pl.CostEstimate(flops=4 * 10**9, bytes_accessed=8 * 2**20, transcendentals=0),
        name="pressure_solve",
    )(
        *(pltpu.with_memory_space_constraint(operand, pltpu.HBM) for operand in operands)
    )
    return tuple(out.reshape(right_side.shape) for out in outs)


def solution(mesh):
    return jax.shard_map(
        functools.partial(shards, mesh.shape["gx"], mesh.shape["gy"]),
        mesh=mesh,
        in_specs=(P("gx", "gy", None), P("gx", "gy", None), P(), P(), P(("gx", "gy"), None)),
        out_specs=(P("gx", "gy", None), P("gx", "gy", None)),
        check_vma=False,
    )
```

```python
import functools

import jax
import jax.numpy as jnp
import ml_dtypes
import numpy as np
from jax import lax
from jax.experimental import pallas as pl
from jax.experimental.pallas import tpu as pltpu
from jax.sharding import PartitionSpec as P

ITERS = 4
MOST = 12
LANES = 128
ROWS = 8
GATHERS = ITERS + 2
SUM_LANE = 3
PAIRS = 2
COLUMNS = 16
PLANES = 16
APPLIES = 16
UPDATES = 8
F32 = jnp.float32
MESH = pl.DeviceIdType.MESH


def sine_table(count):
    index = np.arange(count, dtype=np.float64)
    angle = np.pi * (index[:, None] + 1.0) * (index[None, :] + 1.0) / (count + 1.0)
    return np.sqrt(2.0 / (count + 1.0)) * np.sin(angle)


def eigen_values(count):
    index = np.arange(count, dtype=np.float64)
    return 2.0 - 2.0 * np.cos(np.pi * (index + 1.0) / (count + 1.0))


def split_table(count):
    table = sine_table(count).astype(np.float32)
    high = table.astype(ml_dtypes.bfloat16)
    low = (table - high.astype(np.float32)).astype(ml_dtypes.bfloat16)
    return np.concatenate([np.concatenate([high, high], axis=1), np.concatenate([low, low], axis=1)], axis=0)


def transform(table, field):
    high = field.astype(jnp.bfloat16)
    low = (field - high.astype(F32)).astype(jnp.bfloat16)
    stacked = jnp.concatenate([high, low], axis=0)
    both = jnp.dot(table, stacked, preferred_element_type=F32)
    return both[:field.shape[0]] + both[field.shape[0]:]


def fold(value):
    return jnp.sum(value.reshape(-1, ROWS, LANES), axis=0)


def kernel(
    n_gx, n_gy, size,
    rhs_hbm, diag_hbm, count_hbm, flag_hbm, coarse_hbm, table_hbm, mu_hbm,
    x_ref, r_ref,
    count_ref, flag_ref, coarse_ref, table_ref, mu_ref,
    diag_ref, p_ref, s_ref, image_ref, back_ref, hat_ref, hat_s_ref, hat_r_ref, line_ref, step_ref, mode_ref,
    twice_ref, guess_ref, root_ref, near_ref, far_ref, mid_ref,
    edge_ref, ghost_x, ghost_y, small_ref, all_ref, known_ref,
    in_sem, halo_send, halo_recv, row_send, row_recv, col_send, col_recv,
):
    gx = lax.axis_index("gx")
    gy = lax.axis_index("gy")
    mine = gx * n_gy + gy
    pitch = size + ROWS
    odd_pitch = size + 1
    plain = size * size
    roomy = (size + 2) * pitch
    row8 = lax.broadcasted_iota(jnp.int32, (ROWS, LANES), 0)
    lane8 = lax.broadcasted_iota(jnp.int32, (ROWS, LANES), 1)
    lane = lax.broadcasted_iota(jnp.int32, (size, LANES), 1)
    slim = lax.broadcasted_iota(jnp.int32, (1, LANES), 1)

    def plane(index):
        return pl.ds(pl.multiple_of(index * size, ROWS), size)

    def rows(base, index):
        return pl.ds(base + index * size, size)

    def image_base(parity, first):
        return pl.multiple_of(parity * plain + first * size, ROWS)

    def back_base(parity, first):
        return pl.multiple_of(parity * roomy + (first + 1) * pitch, ROWS)

    pairs = (
        (rhs_hbm, r_ref), (flag_hbm, flag_ref), (mu_hbm, mu_ref), (coarse_hbm, coarse_ref), (count_hbm, count_ref),
        (table_hbm, table_ref), (diag_hbm, diag_ref),
    )
    loads = [pltpu.make_async_copy(source, target, in_sem.at[n]) for n, (source, target) in enumerate(pairs)]
    for load in loads:
        load.start()
    if n_gx * ROWS < LANES:
        all_ref[...] = jnp.zeros_like(all_ref)

    barrier = pltpu.get_barrier_semaphore()

    def over(first, last, act):
        def body(step, carry):
            act(step)
            return carry

        lax.fori_loop(first, last, body, 0)

    def beside_row(step):
        return gx, lax.rem(gy + step, n_gy)

    def beside_col(step):
        return lax.rem(gx + step, n_gx), gy

    def greet(device):
        pl.semaphore_signal(barrier, inc=1, device_id=device, device_id_type=MESH)

    over(1, n_gy, lambda step: greet(beside_row(step)))
    over(1, n_gx, lambda step: greet(beside_col(step)))

    def row_copy(slot, step):
        return pltpu.make_async_remote_copy(
            src_ref=small_ref.at[slot, gy], dst_ref=small_ref.at[slot, gy],
            send_sem=row_send.at[slot, step], recv_sem=row_recv.at[slot, step],
            device_id=beside_row(step), device_id_type=MESH,
        )

    def col_copy(slot, step):
        return pltpu.make_async_remote_copy(
            src_ref=all_ref.at[slot, gx], dst_ref=all_ref.at[slot, gx],
            send_sem=col_send.at[slot, step], recv_sem=col_recv.at[slot, step],
            device_id=beside_col(step), device_id_type=MESH,
        )

    def gather_start(slot, payload):
        small_ref[slot, gy] = jnp.where(row8 == gy, payload, 0.0)
        over(1, n_gy, lambda step: row_copy(slot, step).start())

    def gather_middle(slot):
        over(1, n_gy, lambda step: row_copy(slot, step).wait_recv())
        total = small_ref[slot, 0]
        for other in range(1, n_gy):
            total = total + small_ref[slot, other]
        all_ref[slot, gx] = total
        over(1, n_gx, lambda step: col_copy(slot, step).start())

    def gather_end(slot):
        over(1, n_gx, lambda step: col_copy(slot, step).wait_recv())
        return all_ref[slot].reshape(LANES, LANES)

    def gather_drain(slot):
        over(1, n_gy, lambda step: row_copy(slot, step).wait_send())
        over(1, n_gx, lambda step: col_copy(slot, step).wait_send())

    def lane_pick(row, which):
        total = jnp.sum(jnp.where(slim == which, row, 0.0), axis=1, keepdims=True)
        return jnp.broadcast_to(total, (ROWS, LANES))

    loads[0].wait()

    def add_up(t, total):
        base = pl.multiple_of(t * (8 * size), ROWS)
        for m in range(8):
            total = total + fold(r_ref[rows(base, m), :])
        return total

    total = lax.fori_loop(0, size // 8, add_up, jnp.zeros((ROWS, LANES), F32))
    total = jnp.sum(jnp.sum(total, axis=0, keepdims=True), axis=1, keepdims=True)
    for load in loads[1:6]:
        load.wait()
    pl.semaphore_wait(barrier, n_gx + n_gy - 2)
    gather_start(ITERS, coarse_ref[...])
    gather_start(ITERS + 1, jnp.where(slim == SUM_LANE, total, 0.0))

    shift = 2.5 * flag_ref[pl.ds(mine, 1), :].astype(F32) + 2.5

    height = jnp.transpose(jnp.broadcast_to(shift, (LANES, LANES)))
    two = 2 * size
    wide_lane = lax.broadcasted_iota(jnp.int32, (LANES, LANES), 1)
    wide_row = lax.broadcasted_iota(jnp.int32, (LANES, LANES), 0)

    def turned(pair, offset=0):
        return pl.ds(pl.multiple_of(pair * LANES, LANES) + offset, LANES)

    def coefficients(pair):
        columns = jnp.where(wide_lane < size, mu_ref[pl.ds(2 * pair, 1), :], mu_ref[pl.ds(2 * pair + 1, 1), :])
        d = columns + mu_ref[pl.ds(size, 1), :] + height
        root = lax.rsqrt(d)
        root = root * (1.5 - 0.5 * d * root * root)
        near = jnp.where(wide_row == 0, 0.0, root * pltpu.roll(root, 1, 0))
        square = near * near
        root_ref[turned(pair), :] = root
        near_ref[turned(pair), :] = near
        far_ref[turned(pair), :] = near * pltpu.roll(near, 1, 0)
        mid_ref[turned(pair), :] = square + pltpu.roll(square, LANES - 1, 0)

    def coefficient_some(t, carry):
        coefficients(2 * t)
        coefficients(2 * t + 1)
        return carry

    lax.fori_loop(0, size // 4, coefficient_some, 0)
    near_ref[pl.ds(plain, ROWS), :] = jnp.zeros((ROWS, LANES), F32)
    far_ref[pl.ds(plain, ROWS), :] = jnp.zeros((ROWS, LANES), F32)
    guess_ref[...] = jnp.zeros_like(guess_ref)

    def wipe(t, carry):
        here = pl.ds(pl.multiple_of(t * (4 * size), ROWS), 4 * size)
        for field in (p_ref, s_ref, x_ref, hat_s_ref, hat_r_ref):
            field[here, :] = jnp.zeros((4 * size, LANES), F32)
        return carry

    lax.fori_loop(0, size // 4, wipe, 0)

    for parity in range(2):
        back_ref[pl.ds(parity * roomy, pitch), :] = jnp.zeros((pitch, LANES), F32)
        back_ref[pl.ds(parity * roomy + (size + 1) * pitch, pitch), :] = jnp.zeros((pitch, LANES), F32)

    def clear(index, carry):
        for parity in range(2):
            start = pl.multiple_of(parity * roomy + (index + 1) * pitch + size, ROWS)
            back_ref[pl.ds(start, ROWS), :] = jnp.zeros((ROWS, LANES), F32)
        return carry

    lax.fori_loop(0, size, clear, 0)
    gather_middle(ITERS)
    gather_middle(ITERS + 1)

    count = jnp.full((ROWS, LANES), count_ref[mine], jnp.int32)
    count = jnp.concatenate([count] * (LANES // ROWS), axis=0)
    odd = count % 2 == 1
    active = [count > 2 * step for step in range(MOST // 2)]

    def transform_all(parts):
        table = table_ref[...]
        done = []
        for n in range(0, len(parts), 2):
            both = transform(table, jnp.concatenate(parts[n:n + 2], axis=1))
            done += [both[:, :LANES], both[:, LANES:]]
        return done

    def odd_base(first):
        return pl.multiple_of(first * odd_pitch, ROWS)

    def forward_y(source, parity):
        def body(t, carry):
            base = image_base(parity, t * PLANES)
            target = odd_base(t * PLANES)
            parts = [source[rows(base, m), :] for m in range(PLANES)]
            for m, part in enumerate(transform_all(parts)):
                step_ref[pl.ds(target + m * odd_pitch, size), :] = part
            return carry

        lax.fori_loop(0, size // PLANES, body, 0)

    def forward_x():
        def body(t, carry):
            first = t * COLUMNS
            base = pl.multiple_of(first * size, ROWS)
            parts = [step_ref[pl.ds(first + m, size, stride=odd_pitch), :] for m in range(COLUMNS)]
            for m, part in enumerate(transform_all(parts)):
                hat_ref[rows(base, m), :] = part
            return carry

        lax.fori_loop(0, size // COLUMNS, body, 0)

    turn_over = jnp.transpose

    def lines_sweep(base, shift, alpha, beta, sums):
        first = base
        sums = list(sums)
        for part in range(0, COLUMNS // 2, PAIRS):
            pairs = range(part, part + PAIRS)
            here = [pl.ds(base + n * two + shift * size, two) for n in pairs]
            after = [[pl.ds(first + n * LANES + far, LANES) for far in range(3)] for n in pairs]
            held = [n * (LANES + 2 * ROWS) + ROWS for n in pairs]
            kept = [pl.ds(n * LANES, LANES) for n in pairs]
            guess = []
            for n in range(PAIRS):
                hat_s = hat_ref[here[n], :] + beta * hat_s_ref[here[n], :]
                hat_r = hat_r_ref[here[n], :] - alpha * hat_s
                hat_s_ref[here[n], :] = hat_s
                hat_r_ref[here[n], :] = hat_r
                start = turn_over(hat_r) * root_ref[after[n][0], :]
                guess_ref[pl.ds(held[n], LANES), :] = start
                low = guess_ref[pl.ds(held[n] - 1, LANES), :]
                high = guess_ref[pl.ds(held[n] + 1, LANES), :]
                twice = start + near_ref[after[n][0], :] * low + near_ref[after[n][1], :] * high
                twice_ref[kept[n], :] = twice
                guess.append(jnp.where(odd, start, twice))
            for step in range(1, MOST // 2):
                for n in range(PAIRS):
                    guess_ref[pl.ds(held[n], LANES), :] = guess[n]
                    low = guess_ref[pl.ds(held[n] - 2, LANES), :]
                    high = guess_ref[pl.ds(held[n] + 2, LANES), :]
                    fresh = (twice_ref[kept[n], :] + mid_ref[after[n][0], :] * guess[n]) + (
                        far_ref[after[n][0], :] * low + far_ref[after[n][2], :] * high
                    )
                    guess[n] = jnp.where(active[step], fresh, guess[n])
            for n in range(PAIRS):
                line = turn_over(guess[n] * root_ref[after[n][0], :])
                line_ref[here[n], :] = line
                sums[0] = sums[0] + fold(line * hat_r_ref[here[n], :])
                sums[1] = sums[1] + fold(line * hat_s_ref[here[n], :])
        return tuple(sums)

    def lines_out(base, shift, target):
        parts = [line_ref[rows(base, m + shift), :] for m in range(COLUMNS)]
        for m, part in enumerate(transform_all(parts)):
            mode_ref[pl.ds(target + m * odd_pitch, size), :] = part

    def solve_lines(alpha, beta):
        alpha = jnp.broadcast_to(alpha[:1], (two, LANES))
        beta = jnp.broadcast_to(beta[:1], (two, LANES))

        def body(t, sums):
            base = pl.multiple_of(t * (COLUMNS * size), ROWS)
            lines_out(base, -COLUMNS, odd_base((t - 1) * COLUMNS))
            return lines_sweep(base, 0, alpha, beta, sums)

        zeros = (jnp.zeros((ROWS, LANES), F32),) * 2
        sums = lines_sweep(0, 0, alpha, beta, zeros)
        sums = lax.fori_loop(1, size // COLUMNS, body, sums)
        lines_out(plain, -COLUMNS, (size - COLUMNS) * odd_pitch)
        return sums

    def backward(parity, first, own):
        parts = [mode_ref[pl.ds(first + m, size, stride=odd_pitch), :] for m in range(PLANES)]
        base = back_base(parity, first)
        for m, part in enumerate(transform_all(parts)):
            part = part + own
            back_ref[pl.ds(base + m * pitch, size), :] = part
            edge_ref[0, pl.ds(first + m, 1), :] = part[:1]
            edge_ref[1, pl.ds(first + m, 1), :] = part[size - 1:]

    def halo_copy(turn, side):
        if side < 2:
            device = beside_col(1 if side == 0 else n_gx - 1)
            source = back_ref.at[pl.ds(back_base(turn % 2, size - 1 if side == 0 else 0), size)]
            target = ghost_x.at[turn, side]
        else:
            device = beside_row(1 if side == 2 else n_gy - 1)
            source = edge_ref.at[1 if side == 2 else 0]
            target = ghost_y.at[turn, side - 2]
        return pltpu.make_async_remote_copy(
            src_ref=source, dst_ref=target,
            send_sem=halo_send.at[turn, side], recv_sem=halo_recv.at[turn, side],
            device_id=device, device_id_type=MESH,
        )

    inside = [gx > 0, gx < n_gx - 1, gy > 0, gy < n_gy - 1]

    def ghosts(turn):
        raw = [ghost_x[turn, 0], ghost_x[turn, 1], ghost_y[turn, 0], ghost_y[turn, 1]]
        return [jnp.where(inside[n], raw[n], 0.0) for n in range(4)]

    def apply(parity, i, sums):
        start = back_base(parity, i)
        here = back_ref[pl.ds(start, size), :]
        beside = back_ref[pl.ds(start - pitch, size), :] + back_ref[pl.ds(start + pitch, size), :]
        beside = beside + back_ref[pl.ds(start - 1, size), :] + back_ref[pl.ds(start + 1, size), :]
        below = jnp.where(lane == 0, 0.0, pltpu.roll(here, 1, 1))
        above = jnp.where(lane == LANES - 1, 0.0, pltpu.roll(here, LANES - 1, 1))
        image = (6.0 + diag_ref[plane(i), :]) * here - (beside + (below + above))
        image_ref[pl.ds(image_base(parity, i), size), :] = image
        return sums[0] + fold(here * image), sums[1] + fold(image)

    def update(parity, alpha, beta):
        alpha = jnp.broadcast_to(alpha[:1], (size, LANES))
        beta = jnp.broadcast_to(beta[:1], (size, LANES))

        def body(t, carry):
            base = pl.multiple_of(t * (UPDATES * size), ROWS)
            image = image_base(parity, t * UPDATES)
            back = back_base(parity, t * UPDATES)
            for m in range(UPDATES):
                here = rows(base, m)
                moved = image_ref[rows(image, m), :] + beta * s_ref[here, :]
                direction = back_ref[pl.ds(back + m * pitch, size), :] + beta * p_ref[here, :]
                s_ref[here, :] = moved
                p_ref[here, :] = direction
                x_ref[here, :] = x_ref[here, :] + alpha * direction
                r_ref[here, :] = r_ref[here, :] - alpha * moved
            return carry

        lax.fori_loop(0, size // UPDATES, body, 0)

    forward_y(r_ref, 0)
    forward_x()
    loads[6].wait()
    gather_end(ITERS)
    sums = gather_end(ITERS + 1)

    def spread(matrix):
        return jnp.broadcast_to(matrix[:, SUM_LANE:SUM_LANE + 1], (LANES, LANES))

    def coarse_solve():
        known_ref[2] = jnp.dot(
            all_ref[ITERS].reshape(LANES, LANES), known_ref[0],
            precision=lax.Precision.HIGHEST, preferred_element_type=F32,
        )

    known_ref[0] = spread(sums)
    known_ref[1] = jnp.zeros((LANES, LANES), F32)
    coarse_solve()
    gather_drain(ITERS)
    gather_drain(ITERS + 1)

    def iterate(turn, scalars):
        gamma, energy, alpha, beta = scalars
        parity = turn % 2
        own = known_ref[2, pl.ds(mine, 1), :]
        extra = jnp.where(row8 == 0, own * known_ref[0, pl.ds(mine, 1), :], 0.0)
        extra = jnp.where(row8 == 2, own * known_ref[1, pl.ds(mine, 1), :], extra)
        mode_sums = solve_lines(alpha, beta)

        def ends(t, carry):
            backward(parity, t * (size - PLANES), own)
            return carry

        def others(t, carry):
            backward(parity, t * PLANES, own)
            return carry

        lax.fori_loop(0, 2, ends, 0)
        halos = [halo_copy(turn, side) for side in range(4)]
        halos[0].start()
        halos[1].start()
        lax.fori_loop(1, size // PLANES - 1, others, 0)
        halos[2].start()
        halos[3].start()

        def apply_some(t, sums):
            for m in range(APPLIES):
                sums = apply(parity, APPLIES * t + m, sums)
            return sums

        zeros = (jnp.zeros((ROWS, LANES), F32),) * 2
        curve, flow = lax.fori_loop(0, size // APPLIES, apply_some, zeros)
        for halo in halos:
            halo.wait_recv()
        ghost = ghosts(turn)
        low = pl.ds(back_base(parity, 0), size)
        high = pl.ds(back_base(parity, size - 1), size)
        faces = [back_ref[low, :], back_ref[high, :], edge_ref[0], edge_ref[1]]
        for n in range(4):
            curve = curve - fold(faces[n] * ghost[n])
            flow = flow - fold(ghost[n])
        stacked = jnp.zeros((ROWS, LANES), F32)
        for n, total in enumerate((mode_sums[0], curve, mode_sums[1], flow)):
            stacked = jnp.where(row8 == n, jnp.sum(total, axis=0, keepdims=True), stacked)
        stacked = jnp.sum(stacked, axis=1, keepdims=True) + extra
        payload = jnp.sum(jnp.where(row8 == lane8, stacked, 0.0), axis=0, keepdims=True)
        gather_start(turn, payload)

        base = image_base(parity, 0)
        spots = [
            pl.ds(base, size), pl.ds(base + (size - 1) * size, size),
            pl.ds(base, size, stride=size), pl.ds(base + size - 1, size, stride=size),
        ]
        for n in range(4):
            image_ref[spots[n], :] = image_ref[spots[n], :] - ghost[n]

        @pl.when(turn < ITERS - 1)
        def _():
            forward_y(image_ref, parity)

        gather_middle(turn)

        @pl.when(turn < ITERS - 1)
        def _():
            forward_x()

        @pl.when(turn > 0)
        def _():
            update(1 - parity, alpha, beta)

        for halo in halos:
            halo.wait_send()
        every = gather_end(turn)
        totals = jnp.sum(every, axis=0, keepdims=True)
        fresh = lane_pick(totals, 0)
        beta = jnp.where(turn == 0, 0.0, fresh / gamma)
        energy = lane_pick(totals, 1) + beta * (2.0 * lane_pick(totals, 2) + beta * energy)
        alpha = fresh / energy
        known_ref[1] = spread(every) + beta[:1] * known_ref[1]
        known_ref[0] = known_ref[0] - alpha[:1] * known_ref[1]
        coarse_solve()
        gather_drain(turn)
        return fresh, energy, alpha, beta

    one = jnp.ones((ROWS, LANES), F32)
    zero = jnp.zeros((ROWS, LANES), F32)
    gamma, energy, alpha, beta = lax.fori_loop(0, ITERS, iterate, (one, zero, -one, zero))
    update((ITERS - 1) % 2, alpha, beta)


def shards(n_gx, n_gy, right_side, diagonal, sweep_counts, refine_flags, coarse_inverse):
    size, _, cells = right_side.shape
    flat = (size * size, cells)
    table = jnp.asarray(split_table(size))
    mu = eigen_values(size).astype(np.float32)
    mu = np.concatenate([np.repeat(mu[:, None], cells, axis=1), np.tile(mu, (ROWS, cells // size))], axis=0)
    mu = jnp.asarray(mu)
    subs = n_gx * n_gy
    if coarse_inverse.shape[1] < LANES:
        coarse_inverse = jnp.pad(coarse_inverse, ((0, 0), (0, LANES - subs)))
    operands = (
        right_side.reshape(flat), diagonal.reshape(flat), sweep_counts, refine_flags, coarse_inverse, table, mu
    )
    vmem = pl.BlockSpec(memory_space=pltpu.VMEM)
    hbm = pl.BlockSpec(memory_space=pltpu.HBM)
    field = pltpu.VMEM(flat, F32)
    face = (size, LANES)
    outs = pl.pallas_call(
        functools.partial(kernel, n_gx, n_gy, size),
        out_shape=[jax.ShapeDtypeStruct(flat, F32)] * 2,
        in_specs=[hbm] * 7,
        out_specs=[vmem, vmem],
        scratch_shapes=[
            pltpu.SMEM(sweep_counts.shape, jnp.int32),
            pltpu.VMEM(refine_flags.shape, jnp.int32),
            pltpu.VMEM(coarse_inverse.shape, F32),
            pltpu.VMEM(table.shape, table.dtype),
            pltpu.VMEM(mu.shape, F32),
            field, field, field,
            pltpu.VMEM((2 * size * size, LANES), F32),
            pltpu.VMEM((2 * (size + 2) * (size + ROWS), LANES), F32),
            field, field, field, field,
            pltpu.VMEM((size * (size + 1), LANES), F32),
            pltpu.VMEM((size * (size + 1), LANES), F32),
            pltpu.VMEM((COLUMNS * size, LANES), F32),
            pltpu.VMEM((COLUMNS // 2 * (LANES + 2 * ROWS), LANES), F32),
            field,
            pltpu.VMEM((size * size + ROWS, LANES), F32),
            pltpu.VMEM((size * size + ROWS, LANES), F32),
            field,
            pltpu.VMEM((2,) + face, F32),
            pltpu.VMEM((ITERS, 2) + face, F32),
            pltpu.VMEM((ITERS, 2) + face, F32),
            pltpu.VMEM((GATHERS, n_gy, ROWS, LANES), F32),
            pltpu.VMEM((GATHERS, LANES // ROWS, ROWS, LANES), F32),
            pltpu.VMEM((3, LANES, LANES), F32),
            pltpu.SemaphoreType.DMA((7,)),
            pltpu.SemaphoreType.DMA((ITERS, 4)),
            pltpu.SemaphoreType.DMA((ITERS, 4)),
            pltpu.SemaphoreType.DMA((GATHERS, n_gy)),
            pltpu.SemaphoreType.DMA((GATHERS, n_gy)),
            pltpu.SemaphoreType.DMA((GATHERS, n_gx)),
            pltpu.SemaphoreType.DMA((GATHERS, n_gx)),
        ],
        compiler_params=pltpu.CompilerParams(
            collective_id=0, has_side_effects=True, vmem_limit_bytes=48 * 1024 * 1024
        ),
        cost_estimate=pl.CostEstimate(flops=4 * 10**9, bytes_accessed=8 * 2**20, transcendentals=0),
        name="pressure_solve",
    )(
        *(pltpu.with_memory_space_constraint(operand, pltpu.HBM) for operand in operands)
    )
    return tuple(out.reshape(right_side.shape) for out in outs)


def solution(mesh):
    return jax.shard_map(
        functools.partial(shards, mesh.shape["gx"], mesh.shape["gy"]),
        mesh=mesh,
        in_specs=(P("gx", "gy", None), P("gx", "gy", None), P(), P(), P(("gx", "gy"), None)),
        out_specs=(P("gx", "gy", None), P("gx", "gy", None)),
        check_vma=False,
    )
```

```python
import functools

import jax
import jax.numpy as jnp
import ml_dtypes
import numpy as np
from jax import lax
from jax.experimental import pallas as pl
from jax.experimental.pallas import tpu as pltpu
from jax.sharding import PartitionSpec as P

ITERS = 4
MOST = 12
LANES = 128
ROWS = 8
GATHERS = ITERS + 2
SUM_LANE = 3
PAIRS = 2
COLUMNS = 16
PLANES = 32
APPLIES = 16
UPDATES = 8
F32 = jnp.float32
MESH = pl.DeviceIdType.MESH


def sine_table(count):
    index = np.arange(count, dtype=np.float64)
    angle = np.pi * (index[:, None] + 1.0) * (index[None, :] + 1.0) / (count + 1.0)
    return np.sqrt(2.0 / (count + 1.0)) * np.sin(angle)


def eigen_values(count):
    index = np.arange(count, dtype=np.float64)
    return 2.0 - 2.0 * np.cos(np.pi * (index + 1.0) / (count + 1.0))


def split_table(count):
    table = sine_table(count).astype(np.float32)
    high = table.astype(ml_dtypes.bfloat16)
    low = (table - high.astype(np.float32)).astype(ml_dtypes.bfloat16)
    return np.concatenate([np.concatenate([high, high], axis=1), np.concatenate([low, low], axis=1)], axis=0)


def transform(table, field):
    high = field.astype(jnp.bfloat16)
    low = (field - high.astype(F32)).astype(jnp.bfloat16)
    stacked = jnp.concatenate([high, low], axis=0)
    both = jnp.dot(table, stacked, preferred_element_type=F32)
    return both[:field.shape[0]] + both[field.shape[0]:]


def fold(value):
    return jnp.sum(value.reshape(-1, ROWS, LANES), axis=0)


def kernel(
    n_gx, n_gy, size,
    rhs_hbm, diag_hbm, count_hbm, flag_hbm, coarse_hbm, table_hbm, mu_hbm,
    x_ref, r_ref,
    count_ref, flag_ref, coarse_ref, table_ref, mu_ref,
    diag_ref, p_ref, s_ref, image_ref, back_ref, hat_ref, hat_s_ref, hat_r_ref, line_ref, step_ref, mode_ref,
    twice_ref, guess_ref, root_ref, near_ref, far_ref, mid_ref,
    edge_ref, ghost_x, ghost_y, small_ref, all_ref, known_ref,
    in_sem, halo_send, halo_recv, row_send, row_recv, col_send, col_recv,
):
    gx = lax.axis_index("gx")
    gy = lax.axis_index("gy")
    mine = gx * n_gy + gy
    pitch = size + ROWS
    odd_pitch = size + 1
    plain = size * size
    roomy = (size + 2) * pitch
    row8 = lax.broadcasted_iota(jnp.int32, (ROWS, LANES), 0)
    lane8 = lax.broadcasted_iota(jnp.int32, (ROWS, LANES), 1)
    lane = lax.broadcasted_iota(jnp.int32, (size, LANES), 1)
    slim = lax.broadcasted_iota(jnp.int32, (1, LANES), 1)

    def plane(index):
        return pl.ds(pl.multiple_of(index * size, ROWS), size)

    def rows(base, index):
        return pl.ds(base + index * size, size)

    def image_base(parity, first):
        return pl.multiple_of(parity * plain + first * size, ROWS)

    def back_base(parity, first):
        return pl.multiple_of(parity * roomy + (first + 1) * pitch, ROWS)

    pairs = (
        (rhs_hbm, r_ref), (flag_hbm, flag_ref), (mu_hbm, mu_ref), (coarse_hbm, coarse_ref), (count_hbm, count_ref),
        (table_hbm, table_ref), (diag_hbm, diag_ref),
    )
    loads = [pltpu.make_async_copy(source, target, in_sem.at[n]) for n, (source, target) in enumerate(pairs)]
    for load in loads:
        load.start()
    if n_gx * ROWS < LANES:
        all_ref[...] = jnp.zeros_like(all_ref)

    barrier = pltpu.get_barrier_semaphore()

    def over(first, last, act):
        def body(step, carry):
            act(step)
            return carry

        lax.fori_loop(first, last, body, 0)

    def beside_row(step):
        return gx, lax.rem(gy + step, n_gy)

    def beside_col(step):
        return lax.rem(gx + step, n_gx), gy

    def greet(device):
        pl.semaphore_signal(barrier, inc=1, device_id=device, device_id_type=MESH)

    over(1, n_gy, lambda step: greet(beside_row(step)))
    over(1, n_gx, lambda step: greet(beside_col(step)))

    def row_copy(slot, step):
        return pltpu.make_async_remote_copy(
            src_ref=small_ref.at[slot, gy], dst_ref=small_ref.at[slot, gy],
            send_sem=row_send.at[slot, step], recv_sem=row_recv.at[slot, step],
            device_id=beside_row(step), device_id_type=MESH,
        )

    def col_copy(slot, step):
        return pltpu.make_async_remote_copy(
            src_ref=all_ref.at[slot, gx], dst_ref=all_ref.at[slot, gx],
            send_sem=col_send.at[slot, step], recv_sem=col_recv.at[slot, step],
            device_id=beside_col(step), device_id_type=MESH,
        )

    def gather_start(slot, payload):
        small_ref[slot, gy] = jnp.where(row8 == gy, payload, 0.0)
        over(1, n_gy, lambda step: row_copy(slot, step).start())

    def gather_middle(slot):
        over(1, n_gy, lambda step: row_copy(slot, step).wait_recv())
        total = small_ref[slot, 0]
        for other in range(1, n_gy):
            total = total + small_ref[slot, other]
        all_ref[slot, gx] = total
        over(1, n_gx, lambda step: col_copy(slot, step).start())

    def gather_end(slot):
        over(1, n_gx, lambda step: col_copy(slot, step).wait_recv())
        return all_ref[slot].reshape(LANES, LANES)

    def gather_drain(slot):
        over(1, n_gy, lambda step: row_copy(slot, step).wait_send())
        over(1, n_gx, lambda step: col_copy(slot, step).wait_send())

    def lane_pick(row, which):
        total = jnp.sum(jnp.where(slim == which, row, 0.0), axis=1, keepdims=True)
        return jnp.broadcast_to(total, (ROWS, LANES))

    loads[0].wait()

    def add_up(t, total):
        base = pl.multiple_of(t * (8 * size), ROWS)
        for m in range(8):
            total = total + fold(r_ref[rows(base, m), :])
        return total

    total = lax.fori_loop(0, size // 8, add_up, jnp.zeros((ROWS, LANES), F32))
    total = jnp.sum(jnp.sum(total, axis=0, keepdims=True), axis=1, keepdims=True)
    for load in loads[1:6]:
        load.wait()
    pl.semaphore_wait(barrier, n_gx + n_gy - 2)
    gather_start(ITERS, coarse_ref[...])
    gather_start(ITERS + 1, jnp.where(slim == SUM_LANE, total, 0.0))

    shift = 2.5 * flag_ref[pl.ds(mine, 1), :].astype(F32) + 2.5

    height = jnp.transpose(jnp.broadcast_to(shift, (LANES, LANES)))
    two = 2 * size
    wide_lane = lax.broadcasted_iota(jnp.int32, (LANES, LANES), 1)
    wide_row = lax.broadcasted_iota(jnp.int32, (LANES, LANES), 0)

    def turned(pair, offset=0):
        return pl.ds(pl.multiple_of(pair * LANES, LANES) + offset, LANES)

    def coefficients(pair):
        columns = jnp.where(wide_lane < size, mu_ref[pl.ds(2 * pair, 1), :], mu_ref[pl.ds(2 * pair + 1, 1), :])
        d = columns + mu_ref[pl.ds(size, 1), :] + height
        root = lax.rsqrt(d)
        root = root * (1.5 - 0.5 * d * root * root)
        near = jnp.where(wide_row == 0, 0.0, root * pltpu.roll(root, 1, 0))
        square = near * near
        root_ref[turned(pair), :] = root
        near_ref[turned(pair), :] = near
        far_ref[turned(pair), :] = near * pltpu.roll(near, 1, 0)
        mid_ref[turned(pair), :] = square + pltpu.roll(square, LANES - 1, 0)

    def coefficient_some(t, carry):
        coefficients(2 * t)
        coefficients(2 * t + 1)
        return carry

    lax.fori_loop(0, size // 4, coefficient_some, 0)
    near_ref[pl.ds(plain, ROWS), :] = jnp.zeros((ROWS, LANES), F32)
    far_ref[pl.ds(plain, ROWS), :] = jnp.zeros((ROWS, LANES), F32)
    guess_ref[...] = jnp.zeros_like(guess_ref)

    def wipe(t, carry):
        here = pl.ds(pl.multiple_of(t * (4 * size), ROWS), 4 * size)
        for field in (p_ref, s_ref, x_ref, hat_s_ref, hat_r_ref):
            field[here, :] = jnp.zeros((4 * size, LANES), F32)
        return carry

    lax.fori_loop(0, size // 4, wipe, 0)

    for parity in range(2):
        back_ref[pl.ds(parity * roomy, pitch), :] = jnp.zeros((pitch, LANES), F32)
        back_ref[pl.ds(parity * roomy + (size + 1) * pitch, pitch), :] = jnp.zeros((pitch, LANES), F32)

    def clear(index, carry):
        for parity in range(2):
            start = pl.multiple_of(parity * roomy + (index + 1) * pitch + size, ROWS)
            back_ref[pl.ds(start, ROWS), :] = jnp.zeros((ROWS, LANES), F32)
        return carry

    lax.fori_loop(0, size, clear, 0)
    gather_middle(ITERS)
    gather_middle(ITERS + 1)

    count = jnp.full((ROWS, LANES), count_ref[mine], jnp.int32)
    count = jnp.concatenate([count] * (LANES // ROWS), axis=0)
    odd = count % 2 == 1
    active = [count > 2 * step for step in range(MOST // 2)]

    def transform_all(parts):
        table = table_ref[...]
        done = []
        for n in range(0, len(parts), 2):
            both = transform(table, jnp.concatenate(parts[n:n + 2], axis=1))
            done += [both[:, :LANES], both[:, LANES:]]
        return done

    def odd_base(first):
        return pl.multiple_of(first * odd_pitch, ROWS)

    def forward_y(source, parity):
        def body(t, carry):
            base = image_base(parity, t * PLANES)
            target = odd_base(t * PLANES)
            parts = [source[rows(base, m), :] for m in range(PLANES)]
            for m, part in enumerate(transform_all(parts)):
                step_ref[pl.ds(target + m * odd_pitch, size), :] = part
            return carry

        lax.fori_loop(0, size // PLANES, body, 0)

    def forward_x():
        def body(t, carry):
            first = t * COLUMNS
            base = pl.multiple_of(first * size, ROWS)
            parts = [step_ref[pl.ds(first + m, size, stride=odd_pitch), :] for m in range(COLUMNS)]
            for m, part in enumerate(transform_all(parts)):
                hat_ref[rows(base, m), :] = part
            return carry

        lax.fori_loop(0, size // COLUMNS, body, 0)

    turn_over = jnp.transpose

    def lines_sweep(base, shift, alpha, beta, sums):
        first = base
        sums = list(sums)
        for part in range(0, COLUMNS // 2, PAIRS):
            pairs = range(part, part + PAIRS)
            here = [pl.ds(base + n * two + shift * size, two) for n in pairs]
            after = [[pl.ds(first + n * LANES + far, LANES) for far in range(3)] for n in pairs]
            held = [n * (LANES + 2 * ROWS) + ROWS for n in pairs]
            kept = [pl.ds(n * LANES, LANES) for n in pairs]
            guess = []
            for n in range(PAIRS):
                hat_s = hat_ref[here[n], :] + beta * hat_s_ref[here[n], :]
                hat_r = hat_r_ref[here[n], :] - alpha * hat_s
                hat_s_ref[here[n], :] = hat_s
                hat_r_ref[here[n], :] = hat_r
                start = turn_over(hat_r) * root_ref[after[n][0], :]
                guess_ref[pl.ds(held[n], LANES), :] = start
                low = guess_ref[pl.ds(held[n] - 1, LANES), :]
                high = guess_ref[pl.ds(held[n] + 1, LANES), :]
                twice = start + near_ref[after[n][0], :] * low + near_ref[after[n][1], :] * high
                twice_ref[kept[n], :] = twice
                guess.append(jnp.where(odd, start, twice))
            for step in range(1, MOST // 2):
                for n in range(PAIRS):
                    guess_ref[pl.ds(held[n], LANES), :] = guess[n]
                    low = guess_ref[pl.ds(held[n] - 2, LANES), :]
                    high = guess_ref[pl.ds(held[n] + 2, LANES), :]
                    fresh = (twice_ref[kept[n], :] + mid_ref[after[n][0], :] * guess[n]) + (
                        far_ref[after[n][0], :] * low + far_ref[after[n][2], :] * high
                    )
                    guess[n] = jnp.where(active[step], fresh, guess[n])
            for n in range(PAIRS):
                line = turn_over(guess[n] * root_ref[after[n][0], :])
                line_ref[here[n], :] = line
                sums[0] = sums[0] + fold(line * hat_r_ref[here[n], :])
                sums[1] = sums[1] + fold(line * hat_s_ref[here[n], :])
        return tuple(sums)

    def lines_out(base, shift, target):
        parts = [line_ref[rows(base, m + shift), :] for m in range(COLUMNS)]
        for m, part in enumerate(transform_all(parts)):
            mode_ref[pl.ds(target + m * odd_pitch, size), :] = part

    def solve_lines(alpha, beta):
        alpha = jnp.broadcast_to(alpha[:1], (two, LANES))
        beta = jnp.broadcast_to(beta[:1], (two, LANES))

        def body(t, sums):
            base = pl.multiple_of(t * (COLUMNS * size), ROWS)
            lines_out(base, -COLUMNS, odd_base((t - 1) * COLUMNS))
            return lines_sweep(base, 0, alpha, beta, sums)

        zeros = (jnp.zeros((ROWS, LANES), F32),) * 2
        sums = lines_sweep(0, 0, alpha, beta, zeros)
        sums = lax.fori_loop(1, size // COLUMNS, body, sums)
        lines_out(plain, -COLUMNS, (size - COLUMNS) * odd_pitch)
        return sums

    def backward(parity, first, own):
        parts = [mode_ref[pl.ds(first + m, size, stride=odd_pitch), :] for m in range(PLANES)]
        base = back_base(parity, first)
        for m, part in enumerate(transform_all(parts)):
            part = part + own
            back_ref[pl.ds(base + m * pitch, size), :] = part
            edge_ref[0, pl.ds(first + m, 1), :] = part[:1]
            edge_ref[1, pl.ds(first + m, 1), :] = part[size - 1:]

    def halo_copy(turn, side):
        if side < 2:
            device = beside_col(1 if side == 0 else n_gx - 1)
            source = back_ref.at[pl.ds(back_base(turn % 2, size - 1 if side == 0 else 0), size)]
            target = ghost_x.at[turn, side]
        else:
            device = beside_row(1 if side == 2 else n_gy - 1)
            source = edge_ref.at[1 if side == 2 else 0]
            target = ghost_y.at[turn, side - 2]
        return pltpu.make_async_remote_copy(
            src_ref=source, dst_ref=target,
            send_sem=halo_send.at[turn, side], recv_sem=halo_recv.at[turn, side],
            device_id=device, device_id_type=MESH,
        )

    inside = [gx > 0, gx < n_gx - 1, gy > 0, gy < n_gy - 1]

    def ghosts(turn):
        raw = [ghost_x[turn, 0], ghost_x[turn, 1], ghost_y[turn, 0], ghost_y[turn, 1]]
        return [jnp.where(inside[n], raw[n], 0.0) for n in range(4)]

    def apply(parity, i, sums):
        start = back_base(parity, i)
        here = back_ref[pl.ds(start, size), :]
        beside = back_ref[pl.ds(start - pitch, size), :] + back_ref[pl.ds(start + pitch, size), :]
        beside = beside + back_ref[pl.ds(start - 1, size), :] + back_ref[pl.ds(start + 1, size), :]
        below = jnp.where(lane == 0, 0.0, pltpu.roll(here, 1, 1))
        above = jnp.where(lane == LANES - 1, 0.0, pltpu.roll(here, LANES - 1, 1))
        image = (6.0 + diag_ref[plane(i), :]) * here - (beside + (below + above))
        image_ref[pl.ds(image_base(parity, i), size), :] = image
        return sums[0] + fold(here * image), sums[1] + fold(image)

    def update(parity, alpha, beta):
        alpha = jnp.broadcast_to(alpha[:1], (size, LANES))
        beta = jnp.broadcast_to(beta[:1], (size, LANES))

        def body(t, carry):
            base = pl.multiple_of(t * (UPDATES * size), ROWS)
            image = image_base(parity, t * UPDATES)
            back = back_base(parity, t * UPDATES)
            for m in range(UPDATES):
                here = rows(base, m)
                moved = image_ref[rows(image, m), :] + beta * s_ref[here, :]
                direction = back_ref[pl.ds(back + m * pitch, size), :] + beta * p_ref[here, :]
                s_ref[here, :] = moved
                p_ref[here, :] = direction
                x_ref[here, :] = x_ref[here, :] + alpha * direction
                r_ref[here, :] = r_ref[here, :] - alpha * moved
            return carry

        lax.fori_loop(0, size // UPDATES, body, 0)

    forward_y(r_ref, 0)
    forward_x()
    loads[6].wait()
    gather_end(ITERS)
    sums = gather_end(ITERS + 1)

    def spread(matrix):
        return jnp.broadcast_to(matrix[:, SUM_LANE:SUM_LANE + 1], (LANES, LANES))

    def coarse_solve():
        known_ref[2] = jnp.dot(
            all_ref[ITERS].reshape(LANES, LANES), known_ref[0],
            precision=lax.Precision.HIGHEST, preferred_element_type=F32,
        )

    known_ref[0] = spread(sums)
    known_ref[1] = jnp.zeros((LANES, LANES), F32)
    coarse_solve()
    gather_drain(ITERS)
    gather_drain(ITERS + 1)

    def iterate(turn, scalars):
        gamma, energy, alpha, beta = scalars
        parity = turn % 2
        own = known_ref[2, pl.ds(mine, 1), :]
        extra = jnp.where(row8 == 0, own * known_ref[0, pl.ds(mine, 1), :], 0.0)
        extra = jnp.where(row8 == 2, own * known_ref[1, pl.ds(mine, 1), :], extra)
        mode_sums = solve_lines(alpha, beta)

        def ends(t, carry):
            backward(parity, t * (size - PLANES), own)
            return carry

        def others(t, carry):
            backward(parity, t * PLANES, own)
            return carry

        lax.fori_loop(0, 2, ends, 0)
        halos = [halo_copy(turn, side) for side in range(4)]
        halos[0].start()
        halos[1].start()
        lax.fori_loop(1, size // PLANES - 1, others, 0)
        halos[2].start()
        halos[3].start()

        def apply_some(t, sums):
            for m in range(APPLIES):
                sums = apply(parity, APPLIES * t + m, sums)
            return sums

        zeros = (jnp.zeros((ROWS, LANES), F32),) * 2
        curve, flow = lax.fori_loop(0, size // APPLIES, apply_some, zeros)
        for halo in halos:
            halo.wait_recv()
        ghost = ghosts(turn)
        low = pl.ds(back_base(parity, 0), size)
        high = pl.ds(back_base(parity, size - 1), size)
        faces = [back_ref[low, :], back_ref[high, :], edge_ref[0], edge_ref[1]]
        for n in range(4):
            curve = curve - fold(faces[n] * ghost[n])
            flow = flow - fold(ghost[n])
        stacked = jnp.zeros((ROWS, LANES), F32)
        for n, total in enumerate((mode_sums[0], curve, mode_sums[1], flow)):
            stacked = jnp.where(row8 == n, jnp.sum(total, axis=0, keepdims=True), stacked)
        stacked = jnp.sum(stacked, axis=1, keepdims=True) + extra
        payload = jnp.sum(jnp.where(row8 == lane8, stacked, 0.0), axis=0, keepdims=True)
        gather_start(turn, payload)

        base = image_base(parity, 0)
        spots = [
            pl.ds(base, size), pl.ds(base + (size - 1) * size, size),
            pl.ds(base, size, stride=size), pl.ds(base + size - 1, size, stride=size),
        ]
        for n in range(4):
            image_ref[spots[n], :] = image_ref[spots[n], :] - ghost[n]

        @pl.when(turn < ITERS - 1)
        def _():
            forward_y(image_ref, parity)

        gather_middle(turn)

        @pl.when(turn < ITERS - 1)
        def _():
            forward_x()

        @pl.when(turn > 0)
        def _():
            update(1 - parity, alpha, beta)

        for halo in halos:
            halo.wait_send()
        every = gather_end(turn)
        totals = jnp.sum(every, axis=0, keepdims=True)
        fresh = lane_pick(totals, 0)
        beta = jnp.where(turn == 0, 0.0, fresh / gamma)
        energy = lane_pick(totals, 1) + beta * (2.0 * lane_pick(totals, 2) + beta * energy)
        alpha = fresh / energy
        known_ref[1] = spread(every) + beta[:1] * known_ref[1]
        known_ref[0] = known_ref[0] - alpha[:1] * known_ref[1]
        coarse_solve()
        gather_drain(turn)
        return fresh, energy, alpha, beta

    one = jnp.ones((ROWS, LANES), F32)
    zero = jnp.zeros((ROWS, LANES), F32)
    gamma, energy, alpha, beta = lax.fori_loop(0, ITERS, iterate, (one, zero, -one, zero))
    update((ITERS - 1) % 2, alpha, beta)


def shards(n_gx, n_gy, right_side, diagonal, sweep_counts, refine_flags, coarse_inverse):
    size, _, cells = right_side.shape
    flat = (size * size, cells)
    table = jnp.asarray(split_table(size))
    mu = eigen_values(size).astype(np.float32)
    mu = np.concatenate([np.repeat(mu[:, None], cells, axis=1), np.tile(mu, (ROWS, cells // size))], axis=0)
    mu = jnp.asarray(mu)
    subs = n_gx * n_gy
    if coarse_inverse.shape[1] < LANES:
        coarse_inverse = jnp.pad(coarse_inverse, ((0, 0), (0, LANES - subs)))
    operands = (
        right_side.reshape(flat), diagonal.reshape(flat), sweep_counts, refine_flags, coarse_inverse, table, mu
    )
    vmem = pl.BlockSpec(memory_space=pltpu.VMEM)
    hbm = pl.BlockSpec(memory_space=pltpu.HBM)
    field = pltpu.VMEM(flat, F32)
    face = (size, LANES)
    outs = pl.pallas_call(
        functools.partial(kernel, n_gx, n_gy, size),
        out_shape=[jax.ShapeDtypeStruct(flat, F32)] * 2,
        in_specs=[hbm] * 7,
        out_specs=[vmem, vmem],
        scratch_shapes=[
            pltpu.SMEM(sweep_counts.shape, jnp.int32),
            pltpu.VMEM(refine_flags.shape, jnp.int32),
            pltpu.VMEM(coarse_inverse.shape, F32),
            pltpu.VMEM(table.shape, table.dtype),
            pltpu.VMEM(mu.shape, F32),
            field, field, field,
            pltpu.VMEM((2 * size * size, LANES), F32),
            pltpu.VMEM((2 * (size + 2) * (size + ROWS), LANES), F32),
            field, field, field, field,
            pltpu.VMEM((size * (size + 1), LANES), F32),
            pltpu.VMEM((size * (size + 1), LANES), F32),
            pltpu.VMEM((COLUMNS * size, LANES), F32),
            pltpu.VMEM((COLUMNS // 2 * (LANES + 2 * ROWS), LANES), F32),
            field,
            pltpu.VMEM((size * size + ROWS, LANES), F32),
            pltpu.VMEM((size * size + ROWS, LANES), F32),
            field,
            pltpu.VMEM((2,) + face, F32),
            pltpu.VMEM((ITERS, 2) + face, F32),
            pltpu.VMEM((ITERS, 2) + face, F32),
            pltpu.VMEM((GATHERS, n_gy, ROWS, LANES), F32),
            pltpu.VMEM((GATHERS, LANES // ROWS, ROWS, LANES), F32),
            pltpu.VMEM((3, LANES, LANES), F32),
            pltpu.SemaphoreType.DMA((7,)),
            pltpu.SemaphoreType.DMA((ITERS, 4)),
            pltpu.SemaphoreType.DMA((ITERS, 4)),
            pltpu.SemaphoreType.DMA((GATHERS, n_gy)),
            pltpu.SemaphoreType.DMA((GATHERS, n_gy)),
            pltpu.SemaphoreType.DMA((GATHERS, n_gx)),
            pltpu.SemaphoreType.DMA((GATHERS, n_gx)),
        ],
        compiler_params=pltpu.CompilerParams(
            collective_id=0, has_side_effects=True, vmem_limit_bytes=48 * 1024 * 1024
        ),
        cost_estimate=pl.CostEstimate(flops=4 * 10**9, bytes_accessed=8 * 2**20, transcendentals=0),
        name="pressure_solve",
    )(
        *(pltpu.with_memory_space_constraint(operand, pltpu.HBM) for operand in operands)
    )
    return tuple(out.reshape(right_side.shape) for out in outs)


def solution(mesh):
    return jax.shard_map(
        functools.partial(shards, mesh.shape["gx"], mesh.shape["gy"]),
        mesh=mesh,
        in_specs=(P("gx", "gy", None), P("gx", "gy", None), P(), P(), P(("gx", "gy"), None)),
        out_specs=(P("gx", "gy", None), P("gx", "gy", None)),
        check_vma=False,
    )
```
